32 devices in a mesh: group: 4 (over y, x), dp: 8 (over z, core).
Axes of the slice: x: 2, y: 2, z: 4, core: 2. Of those that a mesh axis runs over, the one named last changes fastest.
Arguments:
- hidden: bfloat16 [8192, 2048], P(('group', 'dp')), may hold values from 0 to 40, as said below
- weight: bfloat16 [2048, 1024], replicated, may hold values from -0.125 to 0.125
- partners: int32 [32, 256], P(('group', 'dp')), may hold values from 0 to 255, each once within a row
Outputs:
- whitened: bfloat16 [8192, 1024], P(('group', 'dp'))
- grad_weight: float32 [2048, 1024], P(('group', 'dp'))
- grad_hidden: bfloat16 [8192, 2048], P(('group', 'dp'))
The draws below stay inside these ranges and needn't reach their ends.
Inputs may be any that keep to these rules, and one draw needn't show every extreme that they name: `hidden`: nonnegative activations. `partners`: each row is a permutation of 0 to 255.
All inputs are finite; a program needn't handle non-finite values.
Results may differ from the reference program's by a relative error of at most 0.0089.
Values sent between devices are 32-bit elements; how exact they have to be, the bound alone decides.
No kernel may reach another device: no remote copies, remote signals or barrier semaphores. Data moves between devices by JAX's collectives and lax.ppermute only.
A program may use at most 128 MiB of HBM per device.

```python
import math
import jax
import jax.numpy as jnp
from jax import lax

HID = 2048
EMB = 1024
ROWS_DEV = 256
ROWS = 8192
N_GROUP = 4
N_DP = 8


def mixed_columns(key, base_vals):
    shift_key, coef_key = jax.random.split(key)
    shifts = jax.random.randint(shift_key, (5,), 1, HID)
    coefs = jax.random.uniform(coef_key, (5,), jnp.float32, 0.1, 0.25)
    total = 1.5 * base_vals
    for term in range(5):
        total = total + coefs[term] * jnp.roll(base_vals, shifts[term], axis=1)
    return total / jnp.sqrt(2.25 + jnp.sum(coefs * coefs))


def draw_hidden(key, part):
    first_key = jax.random.fold_in(key, 0)
    second_key = jax.random.fold_in(key, 1)
    fourth_key = jax.random.fold_in(key, 3)
    col_scale = jnp.exp(jax.random.uniform(second_key, (1, HID), jnp.float32, math.log(0.3), math.log(3.0)))
    base_vals = jnp.clip(jax.random.normal(first_key, (ROWS, HID), jnp.float32), -6.0, 6.0)
    mixed = mixed_columns(fourth_key, base_vals) + 0.5
    return jnp.minimum(jnp.maximum(mixed, 0.0) * col_scale, 40.0).astype(jnp.bfloat16)


def normal_values(own_key, extent, deviation, most, kind=jnp.bfloat16):
    return jnp.clip(deviation * jax.random.normal(own_key, extent, jnp.float32), -most, most).astype(kind)


def setup_inputs(seed: int = 0) -> dict:
    seeds = jax.random.split(jax.random.key(seed), 4)
    hidden = draw_hidden(jax.random.fold_in(seeds[3], 71), 0)
    weight = normal_values(seeds[1], (HID, EMB), HID ** -0.5, 0.125)
    partners = jax.vmap(lambda own: jax.random.permutation(own, ROWS_DEV))(jax.random.split(seeds[2], (N_GROUP * N_DP))).reshape((N_GROUP * N_DP, ROWS_DEV)).astype(jnp.int32)
    return {"hidden": hidden, "weight": weight, "partners": partners}


epsilon = 1e-06
highest = lax.Precision.HIGHEST

def reference(hidden, weight, partners):
    total_rows = hidden.shape[0]
    embedded = jnp.dot(hidden.astype(jnp.float32), weight.astype(jnp.float32), preferred_element_type=jnp.float32)
    mean_row = lax.optimization_barrier(jnp.sum(embedded, axis=0)) / total_rows
    centered = embedded - mean_row
    scatter = jnp.dot(centered.T, centered, precision=highest)
    cov = scatter / (total_rows - 1)
    factor = jnp.linalg.cholesky(cov)
    white = lax.linalg.triangular_solve(factor, centered, left_side=False, lower=True, transpose_a=True)
    whitened = white.astype(jnp.bfloat16)
    row_norm = jnp.sqrt(lax.optimization_barrier(jnp.sum(white * white, axis=1, keepdims=True)) + epsilon)
    unit = white / row_norm
    offsets = jnp.arange(total_rows, dtype=jnp.int32) // ROWS_DEV * ROWS_DEV
    partner = partners.reshape(-1).astype(jnp.int32) + offsets
    inverse = jnp.zeros((total_rows,), jnp.int32).at[partner].set(jnp.arange(total_rows, dtype=jnp.int32))
    grad_unit = 2.0 * (2.0 * unit - unit[partner] - unit[inverse])
    inner_prod = lax.optimization_barrier(jnp.sum(white * grad_unit, axis=1, keepdims=True))
    grad_white = grad_unit / row_norm - white * (inner_prod / row_norm ** 3)
    pair_moment = jnp.dot(grad_white.T, white, precision=highest)
    lower_half = -(jnp.tril(pair_moment) - 0.5 * jnp.diag(jnp.diag(pair_moment)))
    left_solved = lax.linalg.triangular_solve(factor, lower_half, left_side=True, lower=True, transpose_a=True)
    solved = lax.linalg.triangular_solve(factor, left_solved, left_side=False, lower=True, transpose_a=False)
    grad_cov = 0.5 * (solved + solved.T)
    direct = lax.linalg.triangular_solve(factor, grad_white, left_side=False, lower=True, transpose_a=False)
    grad_cent = direct + 2.0 / (total_rows - 1) * jnp.dot(centered, grad_cov, precision=highest)
    grad_z = (grad_cent - lax.optimization_barrier(jnp.sum(grad_cent, axis=0)) / total_rows).astype(jnp.bfloat16)
    grad_weight = lax.dot_general(hidden.astype(jnp.float32), grad_z.astype(jnp.float32), (((0,), (0,)), ((), ())), preferred_element_type=jnp.float32)
    grad_hidden = jnp.dot(grad_z.astype(jnp.float32), weight.T.astype(jnp.float32), preferred_element_type=jnp.float32).astype(jnp.bfloat16)
    return (whitened, grad_weight, grad_hidden)
```

```python
import functools

import jax
import jax.numpy as jnp
from jax import lax
from jax.experimental import pallas as pl
from jax.experimental.pallas import tpu as pltpu
from jax.sharding import PartitionSpec as P

AXES = ("group", "dp")
epsilon = 1e-06
f32 = jnp.float32
bf16 = jnp.bfloat16
NN = (((1,), (0,)), ((), ()))
NT = (((1,), (1,)), ((), ()))
TN = (((0,), (0,)), ((), ()))
BLK = 128
PANEL = 32
VMEM = pl.BlockSpec(memory_space=pltpu.VMEM)
SMEM = pl.BlockSpec(memory_space=pltpu.SMEM)
PARAMS = pltpu.CompilerParams(vmem_limit_bytes=50 * 2**20)


def split2(x):
    high = x.astype(bf16)
    return high, (x - high.astype(f32)).astype(bf16)


def split3(x):
    high = x.astype(bf16)
    rest = x - high.astype(f32)
    mid = rest.astype(bf16)
    return high, mid, (rest - mid.astype(f32)).astype(bf16)


def left6(parts, axis):
    high, mid, low = parts
    return jnp.concatenate([high, high, mid, high, low, mid], axis=axis)


def right6(parts, axis):
    high, mid, low = parts
    return jnp.concatenate([high, mid, high, low, high, mid], axis=axis)


def left3(parts, axis):
    return jnp.concatenate([parts[0], parts[0], parts[1]], axis=axis)


def right3(parts, axis):
    return jnp.concatenate([parts[0], parts[1], parts[0]], axis=axis)


def mm(a, b, dims):
    return lax.dot_general(a, b, dims, preferred_element_type=f32)


def dot6(a, b, dims):
    (ca,), (cb,) = dims[0]
    return mm(left6(split3(a), ca), right6(split3(b), cb), dims)


def dot3(a, b, dims):
    (ca,), (cb,) = dims[0]
    return mm(left3(split2(a), ca), right3(split2(b), cb), dims)


def starts(blocks):
    out, at = [], 0
    for j in range(blocks):
        out.append(at)
        at += (blocks - j) * BLK
    return out, at


def radices(count):
    out = []
    while count > 1:
        out.append(4 if count % 4 == 0 else 2)
        count //= out[-1]
    return out


def rounds():
    groups, per = lax.axis_size("group"), lax.axis_size("dp")
    out, at = [(1, 2)], per
    for radix in radices(groups):
        out.append((at, radix))
        at *= radix
    at = 2
    for radix in radices(per // 2):
        out.append((at, radix))
        at *= radix
    return out


def place():
    index = lax.axis_index("group") * lax.axis_size("dp") + lax.axis_index("dp")
    out = 0
    for stride, radix in rounds():
        out = out * radix + (index // stride) % radix
    return out.astype(jnp.int32).reshape(1, 1)


def owner(position):
    index = 0
    for stride, radix in reversed(rounds()):
        index = index + (position % radix) * stride
        position = position // radix
    return index


def swap(x, stride, by):
    count = lax.axis_size("group") * lax.axis_size("dp")
    return lax.ppermute(x, AXES, [(i, i ^ (by * stride)) for i in range(count)])


def combine_kernel(size, extra, listed, parts, radix, *refs):
    ins, outs = refs[:parts], refs[parts:]
    total = ins[0][0:size, :]
    for r in ins[1:]:
        total = total + r[0:size, :]
    if listed:
        more = jnp.concatenate([r[size : size + extra, :] for r in ins], 0)
    else:
        more = ins[0][size : size + extra, :]
        for r in ins[1:]:
            more = more + r[size : size + extra, :]
    if radix == 1:
        outs[0][...] = total
        outs[1][...] = more
        return
    cut = size // radix
    for i, out in enumerate(outs):
        out[0:cut, :] = total[i * cut : (i + 1) * cut, :]
        out[cut:, :] = more


def reduce_scatter(keep, send, size, extra, listed):
    steps = rounds()
    pieces = [keep, send]
    for at, (stride, radix) in enumerate(steps):
        ins = [pieces[0]] + [swap(p, stride, by) for by, p in enumerate(pieces) if by]
        after = steps[at + 1][1] if at + 1 < len(steps) else 1
        more = extra * radix if listed else extra
        shapes = [(size // after + more, BLK)] * after if after > 1 else [(size, BLK), (more, BLK)]
        pieces = call(
            functools.partial(combine_kernel, size, extra, listed, len(ins), after),
            [(s, f32) for s in shapes],
            *ins,
        )
        extra, size = more, size // after
    return pieces


def all_gather(x):
    steps = rounds()
    parts = [x]
    for at in range(len(steps) - 1, 0, -1):
        stride, radix = steps[at]
        whole = parts[0] if len(parts) == 1 else jnp.concatenate(parts, 0)
        parts = [whole] + [swap(whole, stride, by) for by in range(1, radix)]
    return parts + [swap(p, 1, 1) for p in parts]


def padded(rows):
    unit = 8 * lax.axis_size("group") * lax.axis_size("dp")
    return -(-rows // unit) * unit


def gather_into(pos, parts, out_ref, devices):
    chunk = out_ref.shape[0] // devices
    each = devices // len(parts)
    for i, part in enumerate(parts):
        for j in range(each):
            to = pl.multiple_of(((i * each + j) ^ pos) * chunk, 8)
            out_ref[pl.ds(to, chunk), :] = part[j * chunk : (j + 1) * chunk, :]


def scatter_from(pos, src_ref, keep_ref, send_ref, devices):
    chunk = src_ref.shape[0] // devices
    half = devices // 2
    for i in range(devices):
        at = pl.multiple_of((i ^ pos) * chunk, 8)
        out = keep_ref if i < half else send_ref
        out[(i % half) * chunk : (i % half + 1) * chunk, :] = src_ref[pl.ds(at, chunk), :]


def put_row(out_ref, at, row):
    for i in range(row.shape[1] // BLK):
        out_ref[at + i : at + i + 1, :] = row[:, i * BLK : (i + 1) * BLK]


def get_row(ref, at, blocks):
    return jnp.concatenate([ref[at + i : at + i + 1, :] for i in range(blocks)], 1)


def lower_products(a, b, out_ref, blocks):
    at, total = starts(blocks)
    left, right = left6(split3(a), 0), right6(split3(b), 0)
    for j in range(blocks):
        rows = (blocks - j) * BLK
        out_ref[at[j] : at[j] + rows, :] = mm(left[:, j * BLK :], right[:, j * BLK : (j + 1) * BLK], TN)
    if out_ref.shape[0] > total:
        out_ref[total:, :] = jnp.zeros((out_ref.shape[0] - total, BLK), f32)


def front_kernel(blocks, devices, pos_ref, hid_ref, w_ref, emb_ref, keep_ref, send_ref, pay_ref):
    emb = mm(hid_ref[...], w_ref[...], NN)
    emb_ref[...] = emb
    total = jnp.sum(emb, axis=0, keepdims=True)
    cent = emb - total / emb.shape[0]
    lower_products(cent, cent, pay_ref, blocks)
    scatter_from(pos_ref[0, 0], pay_ref, keep_ref, send_ref, devices)
    half = pay_ref.shape[0] // 2
    put_row(keep_ref, half, total)
    put_row(send_ref, half, total)


def turn_kernel(places, pos_ref, hid_ref, keep_a, keep_b, send_a, send_b, turned_ref, part_ref):
    turned_ref[...] = hid_ref[...].astype(f32).T
    pos = pos_ref[0, 0]
    groups, rest = lax.axis_size("group"), lax.axis_size("dp") // 2
    own = turned_ref.shape[0] // (2 * groups * rest)
    for core, outs in enumerate(((keep_a, keep_b), (send_a, send_b))):
        for order, out in zip(places, outs):
            for i, g in enumerate(order):
                for z in range(rest):
                    device = owner(((core * groups + g) * rest + z) ^ pos)
                    rows = turned_ref[pl.ds(pl.multiple_of(device * own, 8), own), :]
                    part_ref[(i * rest + z) * own : (i * rest + z + 1) * own, :] = rows
            out[...] = part_ref[...].astype(bf16)


def lane(x, c):
    return jnp.broadcast_to(x[:, c : c + 1], (x.shape[0], BLK))


def sub(x, i):
    return jnp.broadcast_to(x[i : i + 1, :], (8, x.shape[1]))


def eye():
    shape = (BLK, BLK)
    return (lax.broadcasted_iota(jnp.int32, shape, 0) == lax.broadcasted_iota(jnp.int32, shape, 1)).astype(f32)


def inverse_factor(s):
    row = lax.broadcasted_iota(jnp.int32, (8, BLK), 0)
    t = eye()
    count = PANEL // 8
    outs = []
    for at in range(0, BLK, PANEL):
        r = [s[8 * q : 8 * q + 8] for q in range(count)]
        v = [t[8 * q : 8 * q + 8] for q in range(count)]
        done_r, done_v = [], []
        for p in range(count):
            col = at + 8 * p
            a = {q: [lane(r[q], col + l) for l in range(8)] for q in range(p, count)}
            pivots = jnp.ones((8, BLK), f32)
            for i in range(8):
                piv = [sub(a[p][l], i) for l in range(i, 8)]
                inv = 1.0 / piv[0]
                pivots = jnp.where(row == i, piv[0], pivots)
                rs, vs = sub(r[p], i), sub(v[p], i)
                for q in range(p, count):
                    if q == p and i == 7:
                        continue
                    m = a[q][i] * inv
                    if q == p:
                        m = jnp.where(row > i, m, 0.0)
                    for l in range(i + 1, 8):
                        a[q][l] = a[q][l] - m * piv[l - i]
                    r[q] = r[q] - m * rs
                    v[q] = v[q] - m * vs
            scale = lax.rsqrt(pivots)
            done_r.append(r[p] * scale)
            done_v.append(v[p] * scale)
        u, w = jnp.concatenate(done_r, 0), jnp.concatenate(done_v, 0)
        outs.append(w)
        if at + PANEL < BLK:
            us, ws = split3(u), split3(w)
            right = jnp.concatenate([right6(us, 0), right6(ws, 0)], axis=1)
            update = mm(left6(us, 0), right, TN)
            s = s[PANEL:] - update[at + PANEL :, :BLK]
            t = t[PANEL:] - update[at + PANEL :, BLK:]
    return jnp.concatenate(outs, 0)


def factor_kernel(blocks, total_rows, devices, parts, *refs):
    pos_ref, sums_ref, emb_ref, partner_ref = refs[:4]
    part_refs = refs[4 : 4 + parts]
    xt_ref, white_ref, out_ref, grad_ref, keep_ref, send_ref, a_ref, pay_ref = refs[4 + parts :]
    pos = pos_ref[0, 0]
    gather_into(pos, part_refs, pay_ref, devices)
    n = blocks * BLK
    local = emb_ref.shape[0]
    at, _ = starts(blocks)
    sums = jnp.concatenate([sums_ref[pl.ds(j, devices, blocks), :] for j in range(blocks)], 1)
    mean = jnp.sum(sums, axis=0, keepdims=True) / total_rows
    apart = sums / local - mean
    left, right = left6(split3(apart), 0), right6(split3(apart), 0)
    for j in range(blocks):
        lo, hi = j * BLK, (j + 1) * BLK
        between = mm(left[:, lo:], right[:, lo:hi], TN)
        a_ref[j, lo:n, :] = (pay_ref[at[j] : at[j] + n - lo, :] + local * between) / (total_rows - 1)
        a_ref[j, n:, :] = emb_ref[:, lo:hi] - mean[:, lo:hi]
        if j:
            a_ref[j, 0:lo, :] = jnp.zeros((lo, BLK), f32)
    one = eye()

    def step(k, _):
        lo = pl.ds(pl.multiple_of(k * BLK, BLK), BLK)
        x = inverse_factor(a_ref[k, lo, :])
        a_ref[k, lo, :] = one
        panel = dot6(a_ref[k], x, NT)
        a_ref[k] = panel
        left = left6(split3(panel), 1)

        def update(j, _):
            here = pl.ds(pl.multiple_of(j * BLK, BLK), BLK)
            right = right6(split3(a_ref[k, here, :]), 1)
            a_ref[j, lo, :] = jnp.zeros((BLK, BLK), f32)
            a_ref[j] = a_ref[j] - mm(left, right, NT)
            return 0

        lax.fori_loop(k + 1, blocks, update, 0)
        return 0

    lax.fori_loop(0, blocks, step, 0)
    for j in range(blocks):
        lo, hi = j * BLK, (j + 1) * BLK
        xt_ref[0:hi, lo:hi] = a_ref[j, 0:hi, :]
        if hi < n:
            xt_ref[hi:, lo:hi] = jnp.zeros((n - hi, BLK), f32)
        white_ref[:, lo:hi] = a_ref[j, n:, :]


    white = white_ref[...]
    rows = white.shape[0]
    out_ref[...] = white.astype(bf16)
    norm = jnp.sqrt(jnp.sum(white * white, axis=1, keepdims=True) + epsilon)
    unit = white / norm
    hit = (lax.broadcasted_iota(jnp.int32, (rows, rows), 0) == partner_ref[...]).astype(f32)
    pairs = (hit + hit.T).astype(bf16)
    parts = split3(unit)
    near = mm(jnp.concatenate([pairs] * 3, 1), jnp.concatenate(parts, 0), NN)
    grad_unit = 2.0 * (2.0 * unit - near)
    inner = jnp.sum(white * grad_unit, axis=1, keepdims=True)
    grad = grad_unit / norm - white * (inner / (norm * norm * norm))
    grad_ref[...] = grad
    lower_products(grad, white, pay_ref, blocks)
    scatter_from(pos, pay_ref, keep_ref, send_ref, devices)
    half = pay_ref.shape[0] // 2
    for i, rows in enumerate((grad, white)):
        total = jnp.sum(rows, axis=0, keepdims=True)
        put_row(keep_ref, half + i * blocks, total)
        put_row(send_ref, half + i * blocks, total)


def moment_product(rows, pay_ref, blocks):
    n = blocks * BLK
    at, _ = starts(blocks)
    below = lax.broadcasted_iota(jnp.int32, (BLK, BLK), 0) > lax.broadcasted_iota(jnp.int32, (BLK, BLK), 1)
    parts = split2(rows)
    outs = [None] * blocks
    for j in range(blocks):
        lo = j * BLK
        block = pay_ref[at[j] : at[j] + BLK, :]
        strict = jnp.where(below, block, 0.0)
        column = jnp.where(eye() > 0, block, 0.0) + strict + strict.T
        if j + 1 < blocks:
            column = jnp.concatenate([column, pay_ref[at[j] + BLK : at[j] + n - lo, :]], 0)
        part = mm(left3([p[:, lo:] for p in parts], 1), right3(split2(column), 0), NN)
        outs[j] = part if outs[j] is None else outs[j] + part
        if j + 1 < blocks:
            part = mm(left3([p[:, lo : lo + BLK] for p in parts], 1), right3(split2(column[BLK:]), 1), NT)
            for i in range(j + 1, blocks):
                add = part[:, (i - j - 1) * BLK : (i - j) * BLK]
                outs[i] = add if outs[i] is None else outs[i] + add
    return jnp.concatenate(outs, 1)


def back_kernel(blocks, total_rows, devices, parts, *refs):
    pos_ref, sums_ref, grad_ref, white_ref, xt_ref = refs[:5]
    part_refs = refs[5 : 5 + parts]
    out_ref, pay_ref = refs[5 + parts :]
    gather_into(pos_ref[0, 0], part_refs, pay_ref, devices)
    n = blocks * BLK
    rows = jnp.concatenate([white_ref[...], jnp.broadcast_to(get_row(sums_ref, blocks, blocks), (8, n))], 0)
    firsts = jnp.concatenate([grad_ref[...], jnp.broadcast_to(get_row(sums_ref, 0, blocks), (8, n))], 0)
    left = firsts - moment_product(rows, pay_ref, blocks) / (total_rows - 1)
    cent = dot3(left, xt_ref[...], NT)
    local = grad_ref.shape[0]
    out_ref[...] = (cent[:local] - cent[local : local + 1, :] / total_rows).astype(bf16)


def call(kernel, outs, *args, scratch=()):
    return pl.pallas_call(
        kernel,
        out_shape=tuple(jax.ShapeDtypeStruct(s, t) for s, t in outs),
        in_specs=[SMEM if a.dtype == jnp.int32 and a.size == 1 else VMEM for a in args],
        out_specs=(VMEM,) * len(outs),
        scratch_shapes=list(scratch),
        compiler_params=PARAMS,
    )(*args)


def weight_sums(keep_a, keep_b, send_a, send_b, grad_z):
    groups, per = lax.axis_size("group"), lax.axis_size("dp")
    half = grad_z.shape[1] // 2
    own = keep_a.shape[0] // (groups * (per // 2))
    cols = (grad_z[:, :half], grad_z[:, half:])
    sent = [swap(mm(h, c, NN), 1, 1) for h, c in zip((send_a, send_b), cols)]
    kept = [mm(h, c, NN) for h, c in zip((keep_a, keep_b), cols)]
    steps = [1 << i for i in range(groups.bit_length() - 1)]
    for at in range(len(steps)):
        order = (steps[at:] + steps[:at], steps[::-1][at:] + steps[::-1][:at])
        size = kept[0].shape[0] // 2
        out = []
        for k, r, o in zip(kept, sent, order):
            out.append((k[:size] + r[:size], swap(k[size:] + r[size:], per, o[0])))
        kept, sent = [k for k, _ in out], [r for _, r in out]
    x = jnp.concatenate([k + r for k, r in zip(kept, sent)], 1)
    for stride, radix in rounds():
        if stride == 1 or stride >= per:
            continue
        size = x.shape[0] // radix
        got = [swap(x[by * size : (by + 1) * size], stride, by) for by in range(1, radix)]
        x = x[:size]
        for g in got:
            x = x + g
    return x


def group_orders(groups):
    def order(bits):
        out = [0]
        for bit in reversed(bits):
            out = out + [o | bit for o in out]
        return out

    bits = [1 << i for i in range(groups.bit_length() - 1)]
    return order(bits), order(bits[::-1])


def body(hidden, weight, partners):
    local, hid = hidden.shape
    emb = weight.shape[1]
    blocks = emb // BLK
    devices = lax.axis_size("group") * lax.axis_size("dp")
    total_rows = local * devices
    _, packed = starts(blocks)
    rows = padded(packed)
    half = rows // 2
    pos = place()
    pay_scratch = pltpu.VMEM((rows, BLK), f32)

    embedded, keep, send = call(
        functools.partial(front_kernel, blocks, devices),
        [((local, emb), f32), ((half + blocks, BLK), f32), ((half + blocks, BLK), f32)],
        pos,
        hidden,
        weight,
        scratch=[pay_scratch],
    )
    turned = call(
        functools.partial(turn_kernel, group_orders(lax.axis_size("group"))),
        [((hid // 2, local), bf16)] * 4,
        pos,
        hidden,
        scratch=[pltpu.VMEM((hid, local), f32), pltpu.VMEM((hid // 2, local), f32)],
    )
    part, sums = reduce_scatter(keep, send, half, blocks, True)
    parts = all_gather(part)
    xt, white, whitened, grad, keep, send = call(
        functools.partial(factor_kernel, blocks, total_rows, devices, len(parts)),
        [((emb, emb), f32), ((local, emb), f32), ((local, emb), bf16), ((local, emb), f32)]
        + [((half + 2 * blocks, BLK), f32)] * 2,
        pos,
        sums,
        embedded,
        partners,
        *parts,
        scratch=[pltpu.VMEM((blocks, emb + local, BLK), f32), pay_scratch],
    )
    part, sums = reduce_scatter(keep, send, half, 2 * blocks, False)
    parts = all_gather(part)
    (grad_z,) = call(
        functools.partial(back_kernel, blocks, total_rows, devices, len(parts)),
        [((local, emb), bf16)],
        pos,
        sums,
        grad,
        white,
        xt,
        *parts,
        scratch=[pay_scratch],
    )
    grad_weight = weight_sums(*turned, grad_z)
    grad_hidden = mm(grad_z, weight, NT).astype(bf16)
    return (whitened, grad_weight, grad_hidden)


def solution(mesh):
    return jax.shard_map(
        body,
        mesh=mesh,
        in_specs=(P(AXES, None), P(), P(AXES, None)),
        out_specs=(P(AXES, None), P(AXES, None), P(AXES, None)),
        check_vma=False,
    )
```

```python
import functools

import jax
import jax.numpy as jnp
from jax import lax
from jax.experimental import pallas as pl
from jax.experimental.pallas import tpu as pltpu
from jax.sharding import PartitionSpec as P

AXES = ("group", "dp")
epsilon = 1e-06
f32 = jnp.float32
bf16 = jnp.bfloat16
NN = (((1,), (0,)), ((), ()))
NT = (((1,), (1,)), ((), ()))
TN = (((0,), (0,)), ((), ()))
BLK = 128
PAIR = 256
PANEL = 32
AHEAD = 16
VMEM = pl.BlockSpec(memory_space=pltpu.VMEM)
SMEM = pl.BlockSpec(memory_space=pltpu.SMEM)
PARAMS = pltpu.CompilerParams(vmem_limit_bytes=50 * 2**20)


def split2(x):
    high = x.astype(bf16)
    return high, (x - high.astype(f32)).astype(bf16)


def split3(x):
    high = x.astype(bf16)
    rest = x - high.astype(f32)
    mid = rest.astype(bf16)
    return high, mid, (rest - mid.astype(f32)).astype(bf16)


def left6(parts, axis):
    high, mid, low = parts
    return jnp.concatenate([high, high, mid, high, low, mid], axis=axis)


def right6(parts, axis):
    high, mid, low = parts
    return jnp.concatenate([high, mid, high, low, high, mid], axis=axis)


def left3(parts, axis):
    return jnp.concatenate([parts[0], parts[0], parts[1]], axis=axis)


def right3(parts, axis):
    return jnp.concatenate([parts[0], parts[1], parts[0]], axis=axis)


def mm(a, b, dims):
    return lax.dot_general(a, b, dims, preferred_element_type=f32)


def dot6(a, b, dims):
    (ca,), (cb,) = dims[0]
    return mm(left6(split3(a), ca), right6(split3(b), cb), dims)


def dot3(a, b, dims):
    (ca,), (cb,) = dims[0]
    return mm(left3(split2(a), ca), right3(split2(b), cb), dims)


def starts(blocks):
    out, at = [], 0
    for j in range(blocks):
        out.append(at)
        at += (blocks - j) * BLK
    return out, at


def radices(count):
    out = []
    while count > 1:
        out.append(4 if count % 4 == 0 else 2)
        count //= out[-1]
    return out


def rounds():
    groups, per = lax.axis_size("group"), lax.axis_size("dp")
    out, at = [(1, 2)], per
    for radix in radices(groups):
        out.append((at, radix))
        at *= radix
    at = 2
    for radix in radices(per // 2):
        out.append((at, radix))
        at *= radix
    return out


def place():
    index = lax.axis_index("group") * lax.axis_size("dp") + lax.axis_index("dp")
    out = 0
    for stride, radix in rounds():
        out = out * radix + (index // stride) % radix
    return out.astype(jnp.int32).reshape(1, 1)


def swap(x, stride, by):
    count = lax.axis_size("group") * lax.axis_size("dp")
    return lax.ppermute(x, AXES, [(i, i ^ (by * stride)) for i in range(count)])


def combine_kernel(size, extra, listed, parts, radix, *refs):
    ins, outs = refs[:parts], refs[parts:]
    total = ins[0][0:size, :]
    for r in ins[1:]:
        total = total + r[0:size, :]
    if listed:
        more = jnp.concatenate([r[size : size + extra, :] for r in ins], 0)
    else:
        more = ins[0][size : size + extra, :]
        for r in ins[1:]:
            more = more + r[size : size + extra, :]
    if radix == 1:
        outs[0][...] = total
        outs[1][...] = more
        return
    cut = size // radix
    for i, out in enumerate(outs):
        out[0:cut, :] = total[i * cut : (i + 1) * cut, :]
        out[cut:, :] = more


def reduce_scatter(keep, send, size, extra, listed):
    steps = rounds()
    pieces = [keep, send]
    for at, (stride, radix) in enumerate(steps):
        ins = [pieces[0]] + [swap(p, stride, by) for by, p in enumerate(pieces) if by]
        after = steps[at + 1][1] if at + 1 < len(steps) else 1
        more = extra * radix if listed else extra
        shapes = [(size // after + more, BLK)] * after if after > 1 else [(size, BLK), (more, BLK)]
        pieces = call(
            functools.partial(combine_kernel, size, extra, listed, len(ins), after),
            [(s, f32) for s in shapes],
            *ins,
        )
        extra, size = more, size // after
    return pieces


def all_gather(x):
    steps = rounds()
    parts = [x]
    for at in range(len(steps) - 1, 0, -1):
        stride, radix = steps[at]
        whole = parts[0] if len(parts) == 1 else jnp.concatenate(parts, 0)
        parts = [whole] + [swap(whole, stride, by) for by in range(1, radix)]
    return parts + [swap(p, 1, 1) for p in parts]


def padded(rows):
    unit = 8 * lax.axis_size("group") * lax.axis_size("dp")
    return -(-rows // unit) * unit


def gather_into(pos, parts, out_ref, devices):
    chunk = out_ref.shape[0] // devices
    each = devices // len(parts)
    for i, part in enumerate(parts):
        for j in range(each):
            to = pl.multiple_of(((i * each + j) ^ pos) * chunk, 8)
            out_ref[pl.ds(to, chunk), :] = part[j * chunk : (j + 1) * chunk, :]


def scatter_from(pos, src_ref, keep_ref, send_ref, devices):
    chunk = src_ref.shape[0] // devices
    half = devices // 2
    for i in range(devices):
        at = pl.multiple_of((i ^ pos) * chunk, 8)
        out = keep_ref if i < half else send_ref
        out[(i % half) * chunk : (i % half + 1) * chunk, :] = src_ref[pl.ds(at, chunk), :]


def put_row(out_ref, at, row):
    for i in range(row.shape[1] // BLK):
        out_ref[at + i : at + i + 1, :] = row[:, i * BLK : (i + 1) * BLK]


def get_row(ref, at, blocks):
    return jnp.concatenate([ref[at + i : at + i + 1, :] for i in range(blocks)], 1)


def lower_products(left, right, out_ref, blocks):
    at, total = starts(blocks)
    n = blocks * BLK
    for j in range(0, blocks, 2):
        lo = j * BLK
        part = mm(left[:, lo:], right[:, lo : lo + PAIR], TN)
        out_ref[at[j] : at[j] + n - lo, :] = part[:, :BLK]
        out_ref[at[j + 1] : at[j + 1] + n - lo - BLK, :] = part[BLK:, BLK:]
    if out_ref.shape[0] > total:
        out_ref[total:, :] = jnp.zeros((out_ref.shape[0] - total, BLK), f32)


def front_kernel(blocks, devices, pos_ref, hid_ref, w_ref, emb_ref, keep_ref, send_ref, pay_ref):
    emb = mm(hid_ref[...], w_ref[...], NN)
    emb_ref[...] = emb
    total = jnp.sum(emb, axis=0, keepdims=True)
    cent = emb - total / emb.shape[0]
    parts = split3(cent)
    lower_products(left6(parts, 0), right6(parts, 0), pay_ref, blocks)
    scatter_from(pos_ref[0, 0], pay_ref, keep_ref, send_ref, devices)
    half = pay_ref.shape[0] // 2
    put_row(keep_ref, half, total)
    put_row(send_ref, half, total)


def turn_kernel(orders, me_ref, hid_ref, *refs):
    outs, turned_ref, part_ref = refs[:-2], refs[-2], refs[-1]
    turned_ref[...] = hid_ref[...].astype(f32).T
    me = me_ref[0, 0]
    own = part_ref.shape[0] >> len(orders[0])
    for core in range(2):
        for bits, out in zip(orders, outs[core * len(orders) :]):
            for i in range(1 << len(bits)):
                far = core
                for t, bit in enumerate(reversed(bits)):
                    far |= bit * ((i >> t) & 1)
                rows = turned_ref[pl.ds(pl.multiple_of((me ^ far) * own, 8), own), :]
                part_ref[i * own : (i + 1) * own, :] = rows
            out[...] = part_ref[...].astype(bf16)


def lane(x, c):
    return jnp.broadcast_to(x[:, c : c + 1], (x.shape[0], BLK))


def sub(x, i):
    return jnp.broadcast_to(x[i : i + 1, :], (8, x.shape[1]))


def eye():
    shape = (BLK, BLK)
    return (lax.broadcasted_iota(jnp.int32, shape, 0) == lax.broadcasted_iota(jnp.int32, shape, 1)).astype(f32)


def inverse_factor(s, out):
    row = lax.broadcasted_iota(jnp.int32, (8, BLK), 0)
    t = eye()
    count = PANEL // 8
    outs = []
    for at in range(0, BLK, PANEL):
        r = [s[8 * q : 8 * q + 8] for q in range(count)]
        v = [t[8 * q : 8 * q + 8] for q in range(count)]
        pivots = [jnp.ones((8, BLK), f32)] * count
        for first in range(0, PANEL, AHEAD):
            last = first + AHEAD
            a = {(l, q): lane(r[q], at + l) for l in range(first, last) for q in range(l // 8, count)}
            for c in range(first, last):
                p, i = c // 8, c % 8
                piv = {l: sub(a[c, l // 8], l % 8) for l in range(c, last)}
                inv = 1.0 / piv[c]
                pivots[p] = jnp.where(row == i, piv[c], pivots[p])
                rs, vs = sub(r[p], i), sub(v[p], i)
                for q in range(p, count):
                    if q == p and i == 7:
                        continue
                    m = a[c, q] * inv
                    if q == p:
                        m = jnp.where(row > i, m, 0.0)
                    for l in range(c + 1, last):
                        if q >= l // 8:
                            a[l, q] = a[l, q] - m * piv[l]
                    r[q] = r[q] - m * rs
                    v[q] = v[q] - m * vs
            yield
        scale = [lax.rsqrt(p) for p in pivots]
        u = jnp.concatenate([x * g for x, g in zip(r, scale)], 0)
        w = jnp.concatenate([x * g for x, g in zip(v, scale)], 0)
        outs.append(w)
        if at + PANEL < BLK:
            us, ws = split3(u), split3(w)
            right = jnp.concatenate([right6(us, 0), right6(ws, 0)], axis=1)
            update = mm(left6(us, 0), right, TN)
            s = s[PANEL:] - update[at + PANEL :, :BLK]
            t = t[PANEL:] - update[at + PANEL :, BLK:]
    out.append(jnp.concatenate(outs, 0))


def inverse_pair(s11, s21, s22, out):
    got = []
    yield from inverse_factor(s11, got)
    l21 = dot6(s21, got[0], NT)
    rest = s22 - dot6(l21, l21, NT)
    yield
    yield from inverse_factor(rest, got)
    x21 = -dot6(got[1], dot6(l21, got[0], NN), NN)
    top = jnp.concatenate([got[0], jnp.zeros((BLK, BLK), f32)], 1)
    out.append(jnp.concatenate([top, jnp.concatenate([x21, got[1]], 1)], 0))


def factor_kernel(blocks, total_rows, devices, parts, *refs):
    pos_ref, sums_ref, emb_ref, partner_ref = refs[:4]
    part_refs = refs[4 : 4 + parts]
    xt_ref, white_ref, out_ref, grad_ref, keep_ref, send_ref, a_ref, pay_ref = refs[4 + parts :]
    pos = pos_ref[0, 0]
    gather_into(pos, part_refs, pay_ref, devices)
    n = blocks * BLK
    local = emb_ref.shape[0]
    at, _ = starts(blocks)
    sums = jnp.concatenate([sums_ref[pl.ds(j, devices, blocks), :] for j in range(blocks)], 1)
    mean = jnp.sum(sums, axis=0, keepdims=True) / total_rows
    apart = sums / local - mean
    left, right = left6(split3(apart), 0), right6(split3(apart), 0)
    pairs = blocks // 2
    for p in range(pairs):
        lo, hi = p * PAIR, (p + 1) * PAIR
        between = mm(left[:, lo:], right[:, lo:hi], TN)
        for h in range(2):
            top = lo + h * BLK
            have = pay_ref[at[2 * p + h] : at[2 * p + h] + n - top, :]
            a_ref[p, top:n, h * BLK : (h + 1) * BLK] = (have + local * between[h * BLK :, h * BLK : (h + 1) * BLK]) / (
                total_rows - 1
            )
        a_ref[p, n:, :] = emb_ref[:, lo:hi] - mean[:, lo:hi]
    end = n + local

    def tiles(first, last):
        return [(i, min(i + PAIR, last)) for i in range(first, last, PAIR)]

    def solve(p, i, e, x, dot):
        a_ref[p, i:e, :] = dot(a_ref[p, i:e, :], x, NT)

    def update(p, j, i, e, dot):
        part = dot(a_ref[p, i:e, :], a_ref[p, j * PAIR : (j + 1) * PAIR, :], NT)
        fresh = p * PAIR <= i < (p + 1) * PAIR
        a_ref[j, i:e, :] = -part if fresh else a_ref[j, i:e, :] - part

    tasks = []
    for p in range(pairs):
        lo, hi = p * PAIR, (p + 1) * PAIR
        got = []
        chain = inverse_pair(
            a_ref[p, lo : lo + BLK, :BLK], a_ref[p, lo + BLK : hi, :BLK], a_ref[p, lo + BLK : hi, BLK:], got
        )
        steps = 2 * BLK // AHEAD + 1
        for step, _ in enumerate(chain):
            for _ in range(-(-len(tasks) // max(steps - step, 1))):
                tasks.pop(0)()
        for task in tasks:
            task()
        tasks = []
        x = got[0]
        a_ref[p, lo:hi, :] = x.T
        for i, e in tiles(hi, n):
            solve(p, i, e, x, dot6)
        if p + 1 < pairs:
            for i, e in tiles(hi, n):
                update(p, p + 1, i, e, dot6)
        others = tiles(0, lo) + tiles(n, end)
        tasks += [functools.partial(solve, p, i, e, x, dot3) for i, e in others]
        for j in range(p + 1, pairs):
            if j > p + 1:
                tasks += [functools.partial(update, p, j, i, e, dot6) for i, e in tiles(j * PAIR, n)]
            tasks += [functools.partial(update, p, j, i, e, dot3) for i, e in tiles(0, hi) + tiles(n, end)]
    for task in tasks:
        task()
    for p in range(pairs):
        lo, hi = p * PAIR, (p + 1) * PAIR
        xt_ref[0:hi, lo:hi] = a_ref[p, 0:hi, :]
        if hi < n:
            xt_ref[hi:, lo:hi] = jnp.zeros((n - hi, PAIR), f32)
        white_ref[:, lo:hi] = a_ref[p, n:, :]
    white = white_ref[...]
    rows = white.shape[0]
    out_ref[...] = white.astype(bf16)
    norm = jnp.sqrt(jnp.sum(white * white, axis=1, keepdims=True) + epsilon)
    unit = white / norm
    hit = (lax.broadcasted_iota(jnp.int32, (rows, rows), 0) == partner_ref[...]).astype(f32)
    both = (hit + hit.T).astype(bf16)
    parts = split3(unit)
    near = mm(jnp.concatenate([both] * 3, 1), jnp.concatenate(parts, 0), NN)
    grad_unit = 2.0 * (2.0 * unit - near)
    inner = jnp.sum(white * grad_unit, axis=1, keepdims=True)
    grad = grad_unit / norm - white * (inner / (norm * norm * norm))
    grad_ref[...] = grad
    lower_products(left3(split2(grad), 0), right3(split2(white), 0), pay_ref, blocks)
    scatter_from(pos, pay_ref, keep_ref, send_ref, devices)
    half = pay_ref.shape[0] // 2
    for i, rows in enumerate((grad, white)):
        total = jnp.sum(rows, axis=0, keepdims=True)
        put_row(keep_ref, half + i * blocks, total)
        put_row(send_ref, half + i * blocks, total)


def moment_product(rows, pay_ref, blocks):
    n = blocks * BLK
    at, _ = starts(blocks)
    below = lax.broadcasted_iota(jnp.int32, (BLK, BLK), 0) > lax.broadcasted_iota(jnp.int32, (BLK, BLK), 1)

    def symmetric(block):
        strict = jnp.where(below, block, 0.0)
        return jnp.where(eye() > 0, block, 0.0) + strict + strict.T

    parts = split2(rows)
    outs = [0.0] * (blocks // 2)
    for j in range(0, blocks, 2):
        lo, hi = j * BLK, (j + 2) * BLK
        cross = pay_ref[at[j] + BLK : at[j] + PAIR, :]
        one = jnp.concatenate([symmetric(pay_ref[at[j] : at[j] + BLK, :]), cross], 0)
        two = jnp.concatenate([cross.T, symmetric(pay_ref[at[j + 1] : at[j + 1] + BLK, :])], 0)
        column = split2(jnp.concatenate([one, two], 1))
        outs[j // 2] += mm(left3([p[:, lo:hi] for p in parts], 1), right3(column, 0), NN)
        if hi < n:
            rest = jnp.concatenate(
                [pay_ref[at[j] + PAIR : at[j] + n - lo, :], pay_ref[at[j + 1] + BLK : at[j + 1] + n - lo - BLK, :]], 1
            )
            rest = split2(rest)
            outs[j // 2] += mm(left3([p[:, hi:] for p in parts], 1), right3(rest, 0), NN)
            turned = mm(left3([p[:, lo:hi] for p in parts], 1), right3(rest, 1), NT)
            for i in range(hi, n, PAIR):
                outs[i // PAIR] += turned[:, i - hi : i - hi + PAIR]
    return jnp.concatenate(outs, 1)


def back_kernel(blocks, total_rows, devices, parts, *refs):
    pos_ref, sums_ref, grad_ref, white_ref, xt_ref = refs[:5]
    part_refs = refs[5 : 5 + parts]
    out_ref, pay_ref = refs[5 + parts :]
    gather_into(pos_ref[0, 0], part_refs, pay_ref, devices)
    n = blocks * BLK
    rows = jnp.concatenate([white_ref[...], jnp.broadcast_to(get_row(sums_ref, blocks, blocks), (8, n))], 0)
    firsts = jnp.concatenate([grad_ref[...], jnp.broadcast_to(get_row(sums_ref, 0, blocks), (8, n))], 0)
    left = firsts - moment_product(rows, pay_ref, blocks) / (total_rows - 1)
    cent = dot3(left, xt_ref[...], NT)
    local = grad_ref.shape[0]
    out_ref[...] = (cent[:local] - cent[local : local + 1, :] / total_rows).astype(bf16)


def call(kernel, outs, *args, scratch=()):
    return pl.pallas_call(
        kernel,
        out_shape=tuple(jax.ShapeDtypeStruct(s, t) for s, t in outs),
        in_specs=[SMEM if a.dtype == jnp.int32 and a.size == 1 else VMEM for a in args],
        out_specs=(VMEM,) * len(outs),
        scratch_shapes=list(scratch),
        compiler_params=PARAMS,
    )(*args)


def halving():
    per, groups = lax.axis_size("dp"), lax.axis_size("group")
    group = [per << i for i in range(groups.bit_length() - 1)]
    rest = [2 << i for i in range(per.bit_length() - 2)]
    return (group + rest, group[::-1] + rest, rest + group), (3, 3, 2)


def weight_sums(turned, grad_z):
    orders, shares = halving()
    unit = grad_z.shape[1] // sum(shares)
    cols, at = [], 0
    for share in shares:
        cols.append(grad_z[:, at * unit : (at + share) * unit])
        at += share
    sent = [swap(mm(h, c, NN), 1, 1) for h, c in zip(turned[len(orders) :], cols)]
    kept = [mm(h, c, NN) for h, c in zip(turned, cols)]
    for step in range(len(orders[0])):
        size = kept[0].shape[0] // 2
        sent_next = [swap(k[size:] + r[size:], o[step], 1) for k, r, o in zip(kept, sent, orders)]
        kept = [k[:size] + r[:size] for k, r in zip(kept, sent)]
        sent = sent_next
    return jnp.concatenate([k + r for k, r in zip(kept, sent)], 1)


def body(hidden, weight, partners):
    local, hid = hidden.shape
    emb = weight.shape[1]
    blocks = emb // BLK
    devices = lax.axis_size("group") * lax.axis_size("dp")
    total_rows = local * devices
    _, packed = starts(blocks)
    rows = padded(packed)
    half = rows // 2
    pos = place()
    pay_scratch = pltpu.VMEM((rows, BLK), f32)

    embedded, keep, send = call(
        functools.partial(front_kernel, blocks, devices),
        [((local, emb), f32), ((half + blocks, BLK), f32), ((half + blocks, BLK), f32)],
        pos,
        hidden,
        weight,
        scratch=[pay_scratch],
    )
    me = (lax.axis_index("group") * lax.axis_size("dp") + lax.axis_index("dp")).astype(jnp.int32).reshape(1, 1)
    orders, _ = halving()
    turned = call(
        functools.partial(turn_kernel, orders),
        [((hid // 2, local), bf16)] * (2 * len(orders)),
        me,
        hidden,
        scratch=[pltpu.VMEM((hid, local), f32), pltpu.VMEM((hid // 2, local), f32)],
    )
    part, sums = reduce_scatter(keep, send, half, blocks, True)
    parts = all_gather(part)
    xt, white, whitened, grad, keep, send = call(
        functools.partial(factor_kernel, blocks, total_rows, devices, len(parts)),
        [((emb, emb), f32), ((local, emb), f32), ((local, emb), bf16), ((local, emb), f32)]
        + [((half + 2 * blocks, BLK), f32)] * 2,
        pos,
        sums,
        embedded,
        partners,
        *parts,
        scratch=[pltpu.VMEM((emb // PAIR, emb + local, PAIR), f32), pay_scratch],
    )
    part, sums = reduce_scatter(keep, send, half, 2 * blocks, False)
    parts = all_gather(part)
    (grad_z,) = call(
        functools.partial(back_kernel, blocks, total_rows, devices, len(parts)),
        [((local, emb), bf16)],
        pos,
        sums,
        grad,
        white,
        xt,
        *parts,
        scratch=[pay_scratch],
    )
    grad_weight = weight_sums(turned, grad_z)
    grad_hidden = mm(grad_z, weight, NT).astype(bf16)
    return (whitened, grad_weight, grad_hidden)


def solution(mesh):
    return jax.shard_map(
        body,
        mesh=mesh,
        in_specs=(P(AXES, None), P(), P(AXES, None)),
        out_specs=(P(AXES, None), P(AXES, None), P(AXES, None)),
        check_vma=False,
    )
```

```python
import functools

import jax
import jax.numpy as jnp
from jax import lax
from jax.experimental import pallas as pl
from jax.experimental.pallas import tpu as pltpu
from jax.sharding import PartitionSpec as P

AXES = ("group", "dp")
epsilon = 1e-06
f32 = jnp.float32
bf16 = jnp.bfloat16
NN = (((1,), (0,)), ((), ()))
NT = (((1,), (1,)), ((), ()))
TN = (((0,), (0,)), ((), ()))
BLK = 128
PAIR = 256
PANEL = 32
AHEAD = 16
VMEM = pl.BlockSpec(memory_space=pltpu.VMEM)
SMEM = pl.BlockSpec(memory_space=pltpu.SMEM)
HBM = pl.BlockSpec(memory_space=pltpu.HBM)


def split2(x):
    high = x.astype(bf16)
    return high, (x - high.astype(f32)).astype(bf16)


def split3(x):
    high = x.astype(bf16)
    rest = x - high.astype(f32)
    mid = rest.astype(bf16)
    return high, mid, (rest - mid.astype(f32)).astype(bf16)


def left6(parts, axis):
    high, mid, low = parts
    return jnp.concatenate([high, high, mid, high, low, mid], axis=axis)


def right6(parts, axis):
    high, mid, low = parts
    return jnp.concatenate([high, mid, high, low, high, mid], axis=axis)


def left3(parts, axis):
    return jnp.concatenate([parts[0], parts[0], parts[1]], axis=axis)


def right3(parts, axis):
    return jnp.concatenate([parts[0], parts[1], parts[0]], axis=axis)


def mm(a, b, dims):
    return lax.dot_general(a, b, dims, preferred_element_type=f32)


def dot6(a, b, dims):
    (ca,), (cb,) = dims[0]
    return mm(left6(split3(a), ca), right6(split3(b), cb), dims)


def dot3(a, b, dims):
    (ca,), (cb,) = dims[0]
    return mm(left3(split2(a), ca), right3(split2(b), cb), dims)


def starts(blocks):
    out, at = [], 0
    for j in range(blocks):
        out.append(at)
        at += (blocks - j - j % 2) * BLK
    return out, at


def radices(count):
    out = []
    while count > 1:
        out.append(4 if count % 4 == 0 else 2)
        count //= out[-1]
    return out


def rounds():
    groups, per = lax.axis_size("group"), lax.axis_size("dp")
    out, at = [(1, 2)], per
    for radix in radices(groups):
        out.append((at, radix))
        at *= radix
    at = 2
    for radix in radices(per // 2):
        out.append((at, radix))
        at *= radix
    return out


def place():
    index = lax.axis_index("group") * lax.axis_size("dp") + lax.axis_index("dp")
    out = 0
    for stride, radix in rounds():
        out = out * radix + (index // stride) % radix
    return out.astype(jnp.int32).reshape(1, 1)


def swap(x, stride, by):
    count = lax.axis_size("group") * lax.axis_size("dp")
    return lax.ppermute(x, AXES, [(i, i ^ (by * stride)) for i in range(count)])


def combine_kernel(size, listed, parts, radix, *refs):
    ins, outs = refs[:parts], refs[parts:]
    total, more = ins[0][0:size, :], ins[0][size + listed :, :]
    for r in ins[1:]:
        total = total + r[0:size, :]
        more = more + r[size + listed :, :]
    if listed:
        more = jnp.concatenate([r[size : size + listed, :] for r in ins] + [more], 0)
    if radix == 1:
        outs[0][...] = total
        outs[1][...] = more
        return
    cut = size // radix
    for i, out in enumerate(outs):
        out[0:cut, :] = total[i * cut : (i + 1) * cut, :]
        out[cut:, :] = more


def reduce_scatter(keep, send, size, listed):
    steps = rounds()
    summed = keep.shape[0] - size - listed
    pieces = [keep, send]
    for at, (stride, radix) in enumerate(steps):
        ins = [pieces[0]] + [swap(p, stride, by) for by, p in enumerate(pieces) if by]
        after = steps[at + 1][1] if at + 1 < len(steps) else 1
        more = listed * radix + summed
        shapes = [(size // after + more, BLK)] * after if after > 1 else [(size, BLK), (more, BLK)]
        pieces = call(
            functools.partial(combine_kernel, size, listed, len(ins), after),
            [(s, f32) for s in shapes],
            *ins,
        )
        listed, size = listed * radix, size // after
    return pieces


def all_gather(x):
    steps = rounds()
    parts = [x]
    for at in range(len(steps) - 1, 0, -1):
        stride, radix = steps[at]
        whole = parts[0] if len(parts) == 1 else jnp.concatenate(parts, 0)
        parts = [whole] + [swap(whole, stride, by) for by in range(1, radix)]
    return parts + [swap(p, 1, 1) for p in parts]


def padded(rows):
    unit = 8 * lax.axis_size("group") * lax.axis_size("dp")
    return -(-rows // unit) * unit


def gather_into(pos, parts, out_ref, devices):
    chunk = out_ref.shape[0] // devices
    each = devices // len(parts)
    for i, part in enumerate(parts):
        for j in range(each):
            to = pl.multiple_of(((i * each + j) ^ pos) * chunk, 8)
            out_ref[pl.ds(to, chunk), :] = part[j * chunk : (j + 1) * chunk, :]


def scatter_from(pos, src_ref, keep_ref, send_ref, devices):
    chunk = src_ref.shape[0] // devices
    half = devices // 2
    for i in range(devices):
        at = pl.multiple_of((i ^ pos) * chunk, 8)
        out = keep_ref if i < half else send_ref
        out[(i % half) * chunk : (i % half + 1) * chunk, :] = src_ref[pl.ds(at, chunk), :]


def put_row(out_ref, at, row):
    for i in range(row.shape[1] // BLK):
        out_ref[at + i : at + i + 1, :] = row[:, i * BLK : (i + 1) * BLK]


def put_extra(refs, at, rows):
    count = sum(row.shape[1] // BLK for row in rows)
    for ref in refs:
        end = at
        for row in rows:
            put_row(ref, end, row)
            end += row.shape[1] // BLK
        if count % 8:
            ref[end : at + count + 8 - count % 8, :] = jnp.zeros((8 - count % 8, BLK), f32)


def get_row(ref, at, blocks):
    return jnp.concatenate([ref[at + i : at + i + 1, :] for i in range(blocks)], 1)


def triangle():
    shape = (BLK, BLK)
    rows, cols = lax.broadcasted_iota(jnp.int32, shape, 0), lax.broadcasted_iota(jnp.int32, shape, 1)
    return rows > cols, rows == cols


def lower_products(left, right, out_ref, blocks):
    at, total = starts(blocks)
    n = blocks * BLK
    below, middle = triangle()
    diagonals = []
    for j in range(0, blocks, 2):
        lo = j * BLK
        part = mm(left[:, lo:], right[:, lo : lo + PAIR], TN)
        other = part[BLK:PAIR, BLK:]
        diagonals.append(jnp.sum(jnp.where(middle, other, 0.0), axis=0, keepdims=True))
        out_ref[at[j] : at[j] + BLK, :] = jnp.where(below, part[:BLK, :BLK], jnp.where(middle, part[:BLK, :BLK], other.T))
        out_ref[at[j] + BLK : at[j] + n - lo, :] = part[BLK:, :BLK]
        if lo + PAIR < n:
            out_ref[at[j + 1] : at[j + 1] + n - lo - PAIR, :] = part[PAIR:, BLK:]
    if out_ref.shape[0] > total:
        out_ref[total:, :] = jnp.zeros((out_ref.shape[0] - total, BLK), f32)
    return diagonals


def unpack(pay_ref, at, diagonal):
    below, middle = triangle()
    packed = pay_ref[at : at + BLK, :]
    one = jnp.where(below, packed, 0.0)
    one = jnp.where(middle, packed, one + one.T)
    two = jnp.where(below | middle, 0.0, packed)
    two = jnp.where(middle, diagonal, two + two.T)
    return one, two


def front_kernel(blocks, devices, pos_ref, hid_hbm, w_hbm, emb_hbm, keep_ref, send_ref, pay_ref, hid_ref, w_ref, emb_ref, sems):
    slabs = sems.shape[0] - 2
    deep = w_hbm.shape[0] // slabs
    copies = [pltpu.make_async_copy(hid_hbm, hid_ref, sems.at[slabs])]
    for i in range(slabs):
        rows = pl.ds(i * deep, deep)
        copies.append(pltpu.make_async_copy(w_hbm.at[rows, :], w_ref.at[rows, :], sems.at[i]))
    for copy in copies:
        copy.start()
    copies[0].wait()
    emb = 0.0
    for i in range(slabs):
        copies[1 + i].wait()
        emb = emb + mm(hid_ref[:, i * deep : (i + 1) * deep], w_ref[i * deep : (i + 1) * deep, :], NN)
    emb_ref[...] = emb
    out = pltpu.make_async_copy(emb_ref, emb_hbm, sems.at[slabs + 1])
    out.start()
    total = jnp.sum(emb, axis=0, keepdims=True)
    parts = split3(emb - total / emb.shape[0])
    diagonals = lower_products(left6(parts, 0), right6(parts, 0), pay_ref, blocks)
    scatter_from(pos_ref[0, 0], pay_ref, keep_ref, send_ref, devices)
    put_extra((keep_ref, send_ref), pay_ref.shape[0] // 2, [total] + diagonals)
    out.wait()


def turn_kernel(me_ref, hid_ref, keep_ref, send_ref, turned_ref):
    turned_ref[...] = hid_ref[...].astype(f32).T
    count = lax.axis_size("group") * lax.axis_size("dp")
    own = turned_ref.shape[0] // count
    core = me_ref[0, 0] % 2
    for out, c in ((keep_ref, core), (send_ref, 1 - core)):
        for i in range(count // 2):
            rows = turned_ref[pl.ds(pl.multiple_of((2 * i + c) * own, 8), own), :]
            out[i * own : (i + 1) * own, :] = rows


def order_kernel(orders, me_ref, keep_ref, got_ref, *refs):
    outs, part_ref = refs[:-1], refs[-1]
    chip = me_ref[0, 0] // 2
    own = part_ref.shape[0] >> len(orders[0])
    local = keep_ref.shape[1]
    for bits, out in zip(orders, outs):
        for i in range(1 << len(bits)):
            far = 0
            for t, bit in enumerate(reversed(bits)):
                far |= bit * ((i >> t) & 1)
            rows = pl.ds(pl.multiple_of((chip ^ (far // 2)) * own, 8), own)
            part_ref[i * own : (i + 1) * own, :local] = keep_ref[rows, :]
            part_ref[i * own : (i + 1) * own, local:] = got_ref[rows, :]
        out[...] = part_ref[...].astype(bf16)


def part_kernel(at, width, turned_ref, mine_ref, other_ref, keep_ref, send_ref):
    cols = slice(at, at + width)
    rows = jnp.concatenate([mine_ref[:, cols], other_ref[:, cols]], 0).astype(bf16)
    part = mm(turned_ref[...], rows, NN)
    half = keep_ref.shape[0]
    keep_ref[...] = part[:half]
    send_ref[...] = part[half:]


def lane(x, c):
    return jnp.broadcast_to(x[:, c : c + 1], (x.shape[0], BLK))


def sub(x, i):
    return jnp.broadcast_to(x[i : i + 1, :], (8, x.shape[1]))


def eye():
    shape = (BLK, BLK)
    return (lax.broadcasted_iota(jnp.int32, shape, 0) == lax.broadcasted_iota(jnp.int32, shape, 1)).astype(f32)


def inverse_factor(s, out):
    row = lax.broadcasted_iota(jnp.int32, (8, BLK), 0)
    t = eye()
    count = PANEL // 8
    outs = []
    for at in range(0, BLK, PANEL):
        r = [s[8 * q : 8 * q + 8] for q in range(count)]
        v = [t[8 * q : 8 * q + 8] for q in range(count)]
        pivots = [jnp.ones((8, BLK), f32)] * count
        for first in range(0, PANEL, AHEAD):
            last = first + AHEAD
            a = {(l, q): lane(r[q], at + l) for l in range(first, last) for q in range(l // 8, count)}
            for c in range(first, last):
                p, i = c // 8, c % 8
                piv = {l: sub(a[c, l // 8], l % 8) for l in range(c, last)}
                inv = 1.0 / piv[c]
                pivots[p] = jnp.where(row == i, piv[c], pivots[p])
                rs, vs = sub(r[p], i), sub(v[p], i)
                for q in range(p, count):
                    if q == p and i == 7:
                        continue
                    m = a[c, q] * inv
                    if q == p:
                        m = jnp.where(row > i, m, 0.0)
                    for l in range(c + 1, last):
                        if q >= l // 8:
                            a[l, q] = a[l, q] - m * piv[l]
                    r[q] = r[q] - m * rs
                    v[q] = v[q] - m * vs
            yield
        scale = [lax.rsqrt(p) for p in pivots]
        u = jnp.concatenate([x * g for x, g in zip(r, scale)], 0)
        w = jnp.concatenate([x * g for x, g in zip(v, scale)], 0)
        outs.append(w)
        if at + PANEL < BLK:
            us, ws = split3(u), split3(w)
            right = jnp.concatenate([right6(us, 0), right6(ws, 0)], axis=1)
            update = mm(left6(us, 0), right, TN)
            s = s[PANEL:] - update[at + PANEL :, :BLK]
            t = t[PANEL:] - update[at + PANEL :, BLK:]
    out.append(jnp.concatenate(outs, 0))


def inverse_pair(s11, s21, s22, out):
    got = []
    yield from inverse_factor(s11, got)
    l21 = dot6(s21, got[0], NT)
    rest = s22 - dot6(l21, l21, NT)
    yield
    yield from inverse_factor(rest, got)
    x21 = -dot6(got[1], dot6(l21, got[0], NN), NN)
    top = jnp.concatenate([got[0], jnp.zeros((BLK, BLK), f32)], 1)
    out.append(jnp.concatenate([top, jnp.concatenate([x21, got[1]], 1)], 0))


def factor_kernel(blocks, total_rows, devices, parts, *refs):
    pos_ref, sums_ref, emb_ref, partner_ref = refs[:4]
    part_refs = refs[4 : 4 + parts]
    xt_refs, white_refs = refs[4 + parts : 6 + parts], refs[6 + parts : 8 + parts]
    grad_ref, keep_ref, send_ref, a_ref, pay_ref, high_ref, mid_ref, low_ref = refs[8 + parts : 16 + parts]
    x_refs = refs[16 + parts :]
    pos = pos_ref[0, 0]
    gather_into(pos, part_refs, pay_ref, devices)
    n = blocks * BLK
    local = emb_ref.shape[0]
    at, _ = starts(blocks)
    sums = jnp.concatenate([sums_ref[pl.ds(j, devices, blocks), :] for j in range(blocks)], 1)
    mean = jnp.sum(sums, axis=0, keepdims=True) / total_rows
    apart = sums / local - mean
    left, right = left6(split3(apart), 0), right6(split3(apart), 0)
    pairs = blocks // 2
    for p in range(pairs):
        lo, hi = p * PAIR, (p + 1) * PAIR
        between = local * mm(left[:, lo:], right[:, lo:hi], TN)
        begin, after = at[2 * p], at[2 * p + 1]
        d = devices * blocks + p
        one, two = unpack(pay_ref, begin, sums_ref[d : d + 1, :])
        scale = 1.0 / (total_rows - 1)
        a_ref[p, lo : lo + BLK, :BLK] = (one + between[:BLK, :BLK]) * scale
        a_ref[p, lo + BLK : n, :BLK] = (pay_ref[begin + BLK : begin + n - lo, :] + between[BLK:, :BLK]) * scale
        a_ref[p, lo + BLK : hi, BLK:] = (two + between[BLK:PAIR, BLK:]) * scale
        if hi < n:
            a_ref[p, hi:n, BLK:] = (pay_ref[after : after + n - hi, :] + between[PAIR:, BLK:]) * scale
        a_ref[p, n:, :] = emb_ref[:, lo:hi] - mean[:, lo:hi]
    last = pairs * PAIR

    def rows_of(tile):
        return pl.ds(pl.multiple_of(tile * PAIR, PAIR), PAIR) if tile is not None else slice(last, last + local)

    def keep_parts(tile, x):
        for ref, part in zip((high_ref, mid_ref, low_ref), split3(x)):
            ref[rows_of(tile), :] = part

    def parts_at(tile):
        return [ref[rows_of(tile), :] for ref in (high_ref, mid_ref, low_ref)]

    def solve(q, tile, x):
        if tile is None:
            part = mm(left3(split2(a_ref[q, rows_of(tile), :]), 1), right3(x, 1), NT)
        else:
            part = mm(left6(split3(a_ref[q, rows_of(tile), :]), 1), right6(x, 1), NT)
        a_ref[q, rows_of(tile), :] = part
        keep_parts(tile, part)

    def update(j, tile, right, valid, fresh=False):
        if tile is None:
            part = mm(left3(parts_at(tile), 1), right3(parts_at(right), 1), NT)
        else:
            part = mm(left6(parts_at(tile), 1), right6(parts_at(right), 1), NT)
        have = a_ref[j, rows_of(tile), :]
        if fresh:
            have = have * (1.0 - valid)
        a_ref[j, rows_of(tile), :] = have - part * valid

    def chain(p):
        lo = pl.multiple_of(p * PAIR, PAIR)
        top, low = pl.ds(lo, BLK), pl.ds(pl.multiple_of(lo + BLK, BLK), BLK)
        got = []
        return got, inverse_pair(a_ref[p, top, :BLK], a_ref[p, low, :BLK], a_ref[p, low, BLK:], got)

    def settle(p, x):
        a_ref[p, rows_of(p), :] = x.T
        for ref, part in zip(x_refs, split3(x)):
            ref[...] = part
        solve(p, p + 1, [ref[...] for ref in x_refs])
        next_parts = parts_at(p + 1)
        a_ref[p + 1, rows_of(p + 1), :] -= mm(left6(next_parts, 1), right6(next_parts, 1), NT)

    got, steps = chain(0)
    for _ in steps:
        pass
    settle(0, got[0])

    def step(p, _):
        q = p - 1
        x = [ref[...] for ref in x_refs]
        tasks = [lambda: keep_parts(q, a_ref[q, rows_of(q), :])]
        others = [(q + r) % pairs for r in range(2, pairs)]
        tasks += [functools.partial(solve, q, tile, x) for tile in others + [None]]
        for u in range(pairs - 1):
            j = q + 1 + u
            valid = jnp.where(j < pairs, 1.0, 0.0).astype(f32)
            j = j % pairs
            tasks.append(functools.partial(update, j, q, j, valid, True))
            tasks += [functools.partial(update, j, t, j, valid) for t in others[max(u - 1, 0) :] + [None]]
        got, steps = chain(p)
        count = 2 * BLK // AHEAD + 1
        for i, _ in enumerate(steps):
            for _ in range(-(-len(tasks) // max(count - i, 1))):
                tasks.pop(0)()
        for task in tasks:
            task()

        @pl.when(p + 1 < pairs)
        def _():
            settle(p, got[0])

        @pl.when(p + 1 == pairs)
        def _():
            a_ref[p, rows_of(p), :] = got[0].T
            for ref, part in zip(x_refs, split3(got[0])):
                ref[...] = part

        return 0

    lax.fori_loop(1, pairs, step, 0)
    x = [ref[...] for ref in x_refs]
    for tile in list(range(pairs - 1)) + [None]:
        solve(pairs - 1, tile, x)
    for p in range(pairs):
        lo, hi = p * PAIR, (p + 1) * PAIR
        for ref, part in zip(xt_refs, split2(a_ref[p, 0:hi, :])):
            ref[0:hi, lo:hi] = part
    white = jnp.concatenate([a_ref[p, n:, :] for p in range(pairs)], 1)
    white_parts = split2(white)
    for ref, part in zip(white_refs, white_parts):
        ref[...] = part
    rows = white.shape[0]
    norm = jnp.sqrt(jnp.sum(white * white, axis=1, keepdims=True) + epsilon)
    unit = white / norm
    hit = (lax.broadcasted_iota(jnp.int32, (rows, rows), 0) == partner_ref[...]).astype(f32)
    both = (hit + hit.T).astype(bf16)
    parts = split3(unit)
    near = mm(jnp.concatenate([both] * 3, 1), jnp.concatenate(parts, 0), NN)
    grad_unit = 2.0 * (2.0 * unit - near)
    inner = jnp.sum(white * grad_unit, axis=1, keepdims=True)
    grad = grad_unit / norm - white * (inner / (norm * norm * norm))
    grad_ref[...] = grad
    diagonals = lower_products(left3(split2(grad), 0), right3(white_parts, 0), pay_ref, blocks)
    scatter_from(pos, pay_ref, keep_ref, send_ref, devices)
    totals = [jnp.sum(rows, axis=0, keepdims=True) for rows in (grad, white)]
    put_extra((keep_ref, send_ref), pay_ref.shape[0] // 2, totals + diagonals)


def moment_product(parts, pay_ref, diagonals, blocks):
    n = blocks * BLK
    at, _ = starts(blocks)
    outs = [0.0] * (blocks // 2)
    for j in range(0, blocks, 2):
        lo, hi = j * BLK, (j + 2) * BLK
        cross = pay_ref[at[j] + BLK : at[j] + PAIR, :]
        one, two = unpack(pay_ref, at[j], diagonals[j // 2])
        column = jnp.concatenate([jnp.concatenate([one, cross], 0), jnp.concatenate([cross.T, two], 0)], 1)
        outs[j // 2] += mm(left3([p[:, lo:hi] for p in parts], 1), right3(split2(column), 0), NN)
        if hi < n:
            rest = [pay_ref[at[j] + PAIR : at[j] + n - lo, :], pay_ref[at[j + 1] : at[j + 1] + n - hi, :]]
            rest = split2(jnp.concatenate(rest, 1))
            outs[j // 2] += mm(left3([p[:, hi:] for p in parts], 1), right3(rest, 0), NN)
            turned = mm(left3([p[:, lo:hi] for p in parts], 1), right3(rest, 1), NT)
            for i in range(hi, n, PAIR):
                outs[i // PAIR] += turned[:, i - hi : i - hi + PAIR]
    return jnp.concatenate(outs, 1)


def back_kernel(blocks, total_rows, devices, parts, *refs):
    pos_ref, sums_ref, grad_ref = refs[:3]
    xt_refs, white_refs = refs[3:5], refs[5:7]
    part_refs = refs[7 : 7 + parts]
    out_ref, wide_ref, pay_ref = refs[7 + parts :]
    gather_into(pos_ref[0, 0], part_refs, pay_ref, devices)
    n = blocks * BLK
    sums = split2(jnp.broadcast_to(get_row(sums_ref, blocks, blocks), (16, n)))
    rows = [jnp.concatenate([w[...], s], 0) for w, s in zip(white_refs, sums)]
    firsts = jnp.concatenate([grad_ref[...], jnp.broadcast_to(get_row(sums_ref, 0, blocks), (16, n))], 0)
    diagonals = [sums_ref[2 * blocks + p : 2 * blocks + p + 1, :] for p in range(blocks // 2)]
    left = split2(firsts - moment_product(rows, pay_ref, diagonals, blocks) / (total_rows - 1))
    local = grad_ref.shape[0]
    for lo in range(0, n, PAIR):
        here = slice(lo, lo + PAIR)
        cent = mm(left3([p[:, lo:] for p in left], 1), right3([x[here, lo:] for x in xt_refs], 1), NT)
        grad_z = (cent[:local] - cent[local : local + 1, :] / total_rows).astype(bf16)
        out_ref[:, here] = grad_z
        wide_ref[:, here] = grad_z.astype(f32)


def call(kernel, outs, *args, scratch=(), limit=24, places=None):
    return pl.pallas_call(
        kernel,
        out_shape=tuple(jax.ShapeDtypeStruct(s, t) for s, t in outs),
        in_specs=[SMEM if a.dtype == jnp.int32 and a.size == 1 else (VMEM if places is None else HBM) for a in args],
        out_specs=(VMEM,) * len(outs) if places is None else places,
        scratch_shapes=list(scratch),
        compiler_params=pltpu.CompilerParams(vmem_limit_bytes=limit * 2**20),
    )(*args)


def halving():
    per, groups = lax.axis_size("dp"), lax.axis_size("group")
    group = [per << i for i in range(groups.bit_length() - 1)]
    rest = [2 << i for i in range(per.bit_length() - 2)]
    return (group + rest, group[::-1] + rest, rest + group), (3, 3, 2)


def weight_sums(turned, mine, wide, weight):
    orders, shares = halving()
    unit = wide.shape[1] // sum(shares)
    other = swap(wide, 1, 1)
    kept, first, at = [], [], 0
    for share, h in zip(shares, turned):
        shape = ((h.shape[0] // 2, share * unit), f32)
        k, s = call(functools.partial(part_kernel, at * unit, share * unit), [shape, shape], h, mine, other)
        kept.append(k)
        first.append(s)
        at += share
    first[-1], mine = lax.optimization_barrier((first[-1], mine))
    sent = [swap(s, order[0], 1) for s, order in zip(first, orders)]
    product = mm(mine, weight, NT).astype(bf16)
    kept, product = lax.optimization_barrier((kept, product))
    orders = list(orders)
    last = kept[-1]
    for step in range(1, len(orders[0])):
        if len(orders) == 3 and orders[0][step:] == orders[1][step:]:
            both = lax.optimization_barrier((kept[0], sent[0], kept[1], sent[1], last))
            last = both[4]
            kept = [jnp.concatenate([both[0], both[2]], 1), kept[2]]
            sent = [jnp.concatenate([both[1], both[3]], 1), sent[2]]
            orders = orders[1:]
        for p, order in enumerate(orders):
            k, r, last = lax.optimization_barrier((kept[p], sent[p], last))
            size = k.shape[0] // 2
            last = k[size:] + r[size:]
            kept[p] = k[:size] + r[:size]
            sent[p] = swap(last, order[step], 1)
    return jnp.concatenate([k + r for k, r in zip(kept, sent)], 1), product


def body(hidden, weight, partners):
    local, hid = hidden.shape
    emb = weight.shape[1]
    blocks = emb // BLK
    devices = lax.axis_size("group") * lax.axis_size("dp")
    total_rows = local * devices
    _, packed = starts(blocks)
    rows = padded(packed)
    half = rows // 2
    extra = -(-(blocks // 2) // 8) * 8
    pos = place()
    pay_scratch = pltpu.VMEM((rows, BLK), f32)

    slabs = 4
    embedded, keep, send = call(
        functools.partial(front_kernel, blocks, devices),
        [((local, emb), f32)] + [((half + blocks + extra, BLK), f32)] * 2,
        pos,
        hidden,
        weight,
        scratch=[
            pay_scratch,
            pltpu.VMEM((local, hid), bf16),
            pltpu.VMEM((hid, emb), bf16),
            pltpu.VMEM((local, emb), f32),
            pltpu.SemaphoreType.DMA((slabs + 2,)),
        ],
        limit=58,
        places=(HBM, VMEM, VMEM),
    )
    keep, send, early = lax.optimization_barrier((keep, send, hidden))
    me = (lax.axis_index("group") * lax.axis_size("dp") + lax.axis_index("dp")).astype(jnp.int32).reshape(1, 1)
    turned_keep, turned_send = call(
        turn_kernel,
        [((hid // 2, local), f32)] * 2,
        me,
        early,
        scratch=[pltpu.VMEM((hid, local), f32)],
        limit=58,
    )
    orders, _ = halving()
    turned = call(
        functools.partial(order_kernel, orders),
        [((hid // 2, 2 * local), bf16)] * len(orders),
        me,
        turned_keep,
        swap(turned_send, 1, 1),
        scratch=[pltpu.VMEM((hid // 2, 2 * local), f32)],
    )
    part, sums = reduce_scatter(keep, send, half, blocks)
    parts = all_gather(part)
    parts[-1], turned = lax.optimization_barrier((parts[-1], turned))
    xh, xl, wh, wl, grad, keep, send = call(
        functools.partial(factor_kernel, blocks, total_rows, devices, len(parts)),
        [((emb, emb), bf16)] * 2
        + [((local, emb), bf16)] * 2
        + [((local, emb), f32)]
        + [((half + 2 * blocks + extra, BLK), f32)] * 2,
        pos,
        sums,
        embedded,
        partners,
        *parts,
        scratch=[pltpu.VMEM((emb // PAIR, emb + local, PAIR), f32), pay_scratch]
        + [pltpu.VMEM((emb + local, PAIR), bf16)] * 3
        + [pltpu.VMEM((PAIR, PAIR), bf16)] * 3,
        limit=32,
    )
    part, sums = reduce_scatter(keep, send, half, 0)
    parts = all_gather(part)
    grad_z, wide = call(
        functools.partial(back_kernel, blocks, total_rows, devices, len(parts)),
        [((local, emb), bf16), ((local, emb), f32)],
        pos,
        sums,
        grad,
        xh,
        xl,
        wh,
        wl,
        *parts,
        scratch=[pay_scratch],
        limit=32,
    )
    grad_weight, grad_hidden = weight_sums(turned, grad_z, wide, weight)
    return (wh, grad_weight, grad_hidden)


def solution(mesh):
    return jax.shard_map(
        body,
        mesh=mesh,
        in_specs=(P(AXES, None), P(), P(AXES, None)),
        out_specs=(P(AXES, None), P(AXES, None), P(AXES, None)),
        check_vma=False,
    )
```

```python
import functools

import jax
import jax.numpy as jnp
from jax import lax
from jax.experimental import pallas as pl
from jax.experimental.pallas import tpu as pltpu
from jax.sharding import PartitionSpec as P

AXES = ("group", "dp")
epsilon = 1e-06
f32 = jnp.float32
bf16 = jnp.bfloat16
NN = (((1,), (0,)), ((), ()))
NT = (((1,), (1,)), ((), ()))
TN = (((0,), (0,)), ((), ()))
BLK = 128
PAIR = 256
PANEL = 32
AHEAD = 16
VMEM = pl.BlockSpec(memory_space=pltpu.VMEM)
SMEM = pl.BlockSpec(memory_space=pltpu.SMEM)
HBM = pl.BlockSpec(memory_space=pltpu.HBM)


def split2(x):
    high = x.astype(bf16)
    return high, (x - high.astype(f32)).astype(bf16)


def split3(x):
    high = x.astype(bf16)
    rest = x - high.astype(f32)
    mid = rest.astype(bf16)
    return high, mid, (rest - mid.astype(f32)).astype(bf16)


def left6(parts, axis):
    high, mid, low = parts
    return jnp.concatenate([high, high, mid, high, low, mid], axis=axis)


def right6(parts, axis):
    high, mid, low = parts
    return jnp.concatenate([high, mid, high, low, high, mid], axis=axis)


def left3(parts, axis):
    return jnp.concatenate([parts[0], parts[0], parts[1]], axis=axis)


def right3(parts, axis):
    return jnp.concatenate([parts[0], parts[1], parts[0]], axis=axis)


def mm(a, b, dims):
    return lax.dot_general(a, b, dims, preferred_element_type=f32)


def dot6(a, b, dims):
    (ca,), (cb,) = dims[0]
    return mm(left6(split3(a), ca), right6(split3(b), cb), dims)


def dot3(a, b, dims):
    (ca,), (cb,) = dims[0]
    return mm(left3(split2(a), ca), right3(split2(b), cb), dims)


def starts(blocks):
    out, at = [], 0
    for j in range(blocks):
        out.append(at)
        at += (blocks - j - j % 2) * BLK
    return out, at


def radices(count):
    out = []
    while count > 1:
        out.append(4 if count % 4 == 0 else 2)
        count //= out[-1]
    return out


def rounds():
    groups, per = lax.axis_size("group"), lax.axis_size("dp")
    out, at = [(1, 2)], per
    for radix in radices(groups):
        out.append((at, radix))
        at *= radix
    at = 2
    for radix in radices(per // 2):
        out.append((at, radix))
        at *= radix
    return out


def place():
    index = lax.axis_index("group") * lax.axis_size("dp") + lax.axis_index("dp")
    out = 0
    for stride, radix in rounds():
        out = out * radix + (index // stride) % radix
    return out.astype(jnp.int32).reshape(1, 1)


def swap(x, stride, by):
    count = lax.axis_size("group") * lax.axis_size("dp")
    return lax.ppermute(x, AXES, [(i, i ^ (by * stride)) for i in range(count)])


def combine_kernel(size, listed, parts, radix, *refs):
    ins, outs = refs[:parts], refs[parts:]
    total, more = ins[0][0:size, :], ins[0][size + listed :, :]
    for r in ins[1:]:
        total = total + r[0:size, :]
        more = more + r[size + listed :, :]
    if listed:
        more = jnp.concatenate([r[size : size + listed, :] for r in ins] + [more], 0)
    if radix == 1:
        outs[0][...] = total
        outs[1][...] = more
        return
    cut = size // radix
    for i, out in enumerate(outs):
        out[0:cut, :] = total[i * cut : (i + 1) * cut, :]
        out[cut:, :] = more


def reduce_scatter(keep, send, size, listed):
    steps = rounds()
    summed = keep.shape[0] - size - listed
    pieces = [keep, send]
    for at, (stride, radix) in enumerate(steps):
        ins = [pieces[0]] + [swap(p, stride, by) for by, p in enumerate(pieces) if by]
        after = steps[at + 1][1] if at + 1 < len(steps) else 1
        more = listed * radix + summed
        shapes = [(size // after + more, BLK)] * after if after > 1 else [(size, BLK), (more, BLK)]
        pieces = call(
            functools.partial(combine_kernel, size, listed, len(ins), after),
            [(s, f32) for s in shapes],
            *ins,
        )
        listed, size = listed * radix, size // after
    return pieces


def all_gather(x, beside=()):
    steps = rounds()
    parts = [x]
    for at in range(len(steps) - 1, 0, -1):
        stride, radix = steps[at]
        whole = parts[0] if len(parts) == 1 else jnp.concatenate(parts, 0)
        parts = [whole] + [swap(whole, stride, by) for by in range(1, radix)]
        if at == len(steps) - 1:
            parts, beside = lax.optimization_barrier((parts, beside))
    return parts + [swap(p, 1, 1) for p in parts], beside


def padded(rows):
    unit = 8 * lax.axis_size("group") * lax.axis_size("dp")
    return -(-rows // unit) * unit


def gather_into(pos, parts, out_ref, devices):
    chunk = out_ref.shape[0] // devices
    each = devices // len(parts)
    for i, part in enumerate(parts):
        for j in range(each):
            to = pl.multiple_of(((i * each + j) ^ pos) * chunk, 8)
            out_ref[pl.ds(to, chunk), :] = part[j * chunk : (j + 1) * chunk, :]


def scatter_from(pos, src_ref, keep_ref, send_ref, devices):
    chunk = src_ref.shape[0] // devices
    half = devices // 2
    for i in range(devices):
        at = pl.multiple_of((i ^ pos) * chunk, 8)
        out = keep_ref if i < half else send_ref
        out[(i % half) * chunk : (i % half + 1) * chunk, :] = src_ref[pl.ds(at, chunk), :]


def put_row(out_ref, at, row):
    for i in range(row.shape[1] // BLK):
        out_ref[at + i : at + i + 1, :] = row[:, i * BLK : (i + 1) * BLK]


def put_extra(refs, at, rows):
    count = sum(row.shape[1] // BLK for row in rows)
    for ref in refs:
        end = at
        for row in rows:
            put_row(ref, end, row)
            end += row.shape[1] // BLK
        if count % 8:
            ref[end : at + count + 8 - count % 8, :] = jnp.zeros((8 - count % 8, BLK), f32)


def get_row(ref, at, blocks):
    return jnp.concatenate([ref[at + i : at + i + 1, :] for i in range(blocks)], 1)


def triangle():
    shape = (BLK, BLK)
    rows, cols = lax.broadcasted_iota(jnp.int32, shape, 0), lax.broadcasted_iota(jnp.int32, shape, 1)
    return rows > cols, rows == cols


def lower_products(left, right, out_ref, blocks):
    at, total = starts(blocks)
    n = blocks * BLK
    below, middle = triangle()
    diagonals = []
    for j in range(0, blocks, 2):
        lo = j * BLK
        part = mm(left[:, lo:], right[:, lo : lo + PAIR], TN)
        other = part[BLK:PAIR, BLK:]
        diagonals.append(jnp.sum(jnp.where(middle, other, 0.0), axis=0, keepdims=True))
        out_ref[at[j] : at[j] + BLK, :] = jnp.where(below, part[:BLK, :BLK], jnp.where(middle, part[:BLK, :BLK], other.T))
        out_ref[at[j] + BLK : at[j] + n - lo, :] = part[BLK:, :BLK]
        if lo + PAIR < n:
            out_ref[at[j + 1] : at[j + 1] + n - lo - PAIR, :] = part[PAIR:, BLK:]
    if out_ref.shape[0] > total:
        out_ref[total:, :] = jnp.zeros((out_ref.shape[0] - total, BLK), f32)
    return diagonals


def unpack(pay_ref, at, diagonal):
    below, middle = triangle()
    packed = pay_ref[at : at + BLK, :]
    one = jnp.where(below, packed, 0.0)
    one = jnp.where(middle, packed, one + one.T)
    two = jnp.where(below | middle, 0.0, packed)
    two = jnp.where(middle, diagonal, two + two.T)
    return one, two


def front_kernel(blocks, devices, pos_ref, hid_hbm, w_hbm, emb_hbm, keep_ref, send_ref, hid_ref, pay_ref, w_ref, emb_ref, sems):
    slabs = sems.shape[0] - 2
    deep = w_hbm.shape[0] // slabs
    copies = [pltpu.make_async_copy(hid_hbm, hid_ref, sems.at[slabs])]
    for i in range(slabs):
        rows = pl.ds(i * deep, deep)
        copies.append(pltpu.make_async_copy(w_hbm.at[rows, :], w_ref.at[rows, :], sems.at[i]))
    for copy in copies:
        copy.start()
    copies[0].wait()
    emb = 0.0
    for i in range(slabs):
        copies[1 + i].wait()
        emb = emb + mm(hid_ref[:, i * deep : (i + 1) * deep], w_ref[i * deep : (i + 1) * deep, :], NN)
    emb_ref[...] = emb
    out = pltpu.make_async_copy(emb_ref, emb_hbm, sems.at[slabs + 1])
    out.start()
    total = jnp.sum(emb, axis=0, keepdims=True)
    parts = split3(emb - total / emb.shape[0])
    diagonals = lower_products(left6(parts, 0), right6(parts, 0), pay_ref, blocks)
    scatter_from(pos_ref[0, 0], pay_ref, keep_ref, send_ref, devices)
    put_extra((keep_ref, send_ref), pay_ref.shape[0] // 2, [total] + diagonals)
    out.wait()


def turn_kernel(me_ref, hid_ref, keep_ref, send_ref, turned_ref):
    turned_ref[...] = hid_ref[...].astype(f32).T
    count = lax.axis_size("group") * lax.axis_size("dp")
    own = turned_ref.shape[0] // count
    core = me_ref[0, 0] % 2
    for out, c in ((keep_ref, core), (send_ref, 1 - core)):
        for i in range(count // 2):
            rows = turned_ref[pl.ds(pl.multiple_of((2 * i + c) * own, 8), own), :]
            out[i * own : (i + 1) * own, :] = rows


def order_kernel(orders, me_ref, keep_ref, got_ref, *refs):
    near_refs, far_refs, part_ref = refs[: len(orders)], refs[len(orders) : -1], refs[-1]
    chip = me_ref[0, 0] // 2
    half = part_ref.shape[0]
    own = half * 2 >> len(orders[0])
    local = keep_ref.shape[1]
    for bits, near_ref, far_ref in zip(orders, near_refs, far_refs):
        for side, out in ((0, part_ref), (1, far_ref)):
            for i in range(half // own):
                far = bits[0] * side
                for t, bit in enumerate(reversed(bits[1:])):
                    far |= bit * ((i >> t) & 1)
                rows = pl.ds(pl.multiple_of((chip ^ (far // 2)) * own, 8), own)
                out[i * own : (i + 1) * own, :local] = keep_ref[rows, :]
                out[i * own : (i + 1) * own, local:] = got_ref[rows, :]
        near_ref[...] = part_ref[...].astype(bf16)


def part_kernel(near_ref, far_ref, *refs):
    rows, (keep_ref, send_ref) = refs[:4], refs[4:]
    left = jnp.concatenate([near_ref[...], far_ref[...].astype(bf16)], 1)
    part = mm(left, jnp.concatenate([r[...].astype(bf16) for r in rows], 0), NN)
    half = keep_ref.shape[0]
    keep_ref[...] = part[:half]
    send_ref[...] = part[half:]


def lane(x, c):
    return jnp.broadcast_to(x[:, c : c + 1], (x.shape[0], BLK))


def sub(x, i):
    return jnp.broadcast_to(x[i : i + 1, :], (8, x.shape[1]))


def eye():
    shape = (BLK, BLK)
    return (lax.broadcasted_iota(jnp.int32, shape, 0) == lax.broadcasted_iota(jnp.int32, shape, 1)).astype(f32)


def inverse_factor(s, out):
    row = lax.broadcasted_iota(jnp.int32, (8, BLK), 0)
    t = eye()
    count = PANEL // 8
    outs = []
    for at in range(0, BLK, PANEL):
        r = [s[8 * q : 8 * q + 8] for q in range(count)]
        v = [t[8 * q : 8 * q + 8] for q in range(count)]
        pivots = [jnp.ones((8, BLK), f32)] * count
        for first in range(0, PANEL, AHEAD):
            last = first + AHEAD
            a = {(l, q): lane(r[q], at + l) for l in range(first, last) for q in range(l // 8, count)}
            for c in range(first, last):
                p, i = c // 8, c % 8
                piv = {l: sub(a[c, l // 8], l % 8) for l in range(c, last)}
                inv = 1.0 / piv[c]
                pivots[p] = jnp.where(row == i, piv[c], pivots[p])
                rs, vs = sub(r[p], i), sub(v[p], i)
                for q in range(p, count):
                    if q == p and i == 7:
                        continue
                    m = a[c, q] * inv
                    if q == p:
                        m = jnp.where(row > i, m, 0.0)
                    for l in range(c + 1, last):
                        if q >= l // 8:
                            a[l, q] = a[l, q] - m * piv[l]
                    r[q] = r[q] - m * rs
                    v[q] = v[q] - m * vs
            yield
        scale = [lax.rsqrt(p) for p in pivots]
        u = jnp.concatenate([x * g for x, g in zip(r, scale)], 0)
        w = jnp.concatenate([x * g for x, g in zip(v, scale)], 0)
        outs.append(w)
        if at + PANEL < BLK:
            us, ws = split3(u), split3(w)
            right = jnp.concatenate([right6(us, 0), right6(ws, 0)], axis=1)
            update = mm(left6(us, 0), right, TN)
            s = s[PANEL:] - update[at + PANEL :, :BLK]
            t = t[PANEL:] - update[at + PANEL :, BLK:]
    out.append(jnp.concatenate(outs, 0))


def inverse_pair(s11, s21, s22, out):
    got = []
    yield from inverse_factor(s11, got)
    l21 = dot6(s21, got[0], NT)
    rest = s22 - dot6(l21, l21, NT)
    yield
    yield from inverse_factor(rest, got)
    x21 = -dot6(got[1], dot6(l21, got[0], NN), NN)
    top = jnp.concatenate([got[0], jnp.zeros((BLK, BLK), f32)], 1)
    out.append(jnp.concatenate([top, jnp.concatenate([x21, got[1]], 1)], 0))


def factor_kernel(blocks, total_rows, devices, parts, *refs):
    pos_ref, sums_ref, emb_ref, partner_ref = refs[:4]
    part_refs = refs[4 : 4 + parts]
    white_refs, x_refs = refs[4 + parts : 6 + parts], refs[6 + parts : 9 + parts]
    a_ref, grad_ref, keep_ref, send_ref, pay_ref, high_ref, mid_ref, low_ref = refs[9 + parts :]
    pos = pos_ref[0, 0]
    gather_into(pos, part_refs, pay_ref, devices)
    n = blocks * BLK
    local = emb_ref.shape[0]
    at, _ = starts(blocks)
    sums = jnp.concatenate([sums_ref[pl.ds(j, devices, blocks), :] for j in range(blocks)], 1)
    mean = jnp.sum(sums, axis=0, keepdims=True) / total_rows
    apart = sums / local - mean
    left, right = left6(split3(apart), 0), right6(split3(apart), 0)
    pairs = blocks // 2
    for p in range(pairs):
        lo, hi = p * PAIR, (p + 1) * PAIR
        between = local * mm(left[:, lo:], right[:, lo:hi], TN)
        begin, after = at[2 * p], at[2 * p + 1]
        d = devices * blocks + p
        one, two = unpack(pay_ref, begin, sums_ref[d : d + 1, :])
        scale = 1.0 / (total_rows - 1)
        a_ref[p, lo : lo + BLK, :BLK] = (one + between[:BLK, :BLK]) * scale
        a_ref[p, lo + BLK : n, :BLK] = (pay_ref[begin + BLK : begin + n - lo, :] + between[BLK:, :BLK]) * scale
        a_ref[p, lo + BLK : hi, BLK:] = (two + between[BLK:PAIR, BLK:]) * scale
        if hi < n:
            a_ref[p, hi:n, BLK:] = (pay_ref[after : after + n - hi, :] + between[PAIR:, BLK:]) * scale
        a_ref[p, n:, :] = emb_ref[:, lo:hi] - mean[:, lo:hi]
    last = pairs * PAIR

    def rows_of(tile):
        return pl.ds(pl.multiple_of(tile * PAIR, PAIR), PAIR) if tile is not None else slice(last, last + local)

    def keep_parts(tile, x):
        for ref, part in zip((high_ref, mid_ref, low_ref), split3(x)):
            ref[rows_of(tile), :] = part

    def parts_at(tile):
        return [ref[rows_of(tile), :] for ref in (high_ref, mid_ref, low_ref)]

    def solve(q, tile, x):
        if tile is None:
            part = mm(left3(split2(a_ref[q, rows_of(tile), :]), 1), right3(x, 1), NT)
        else:
            part = mm(left6(split3(a_ref[q, rows_of(tile), :]), 1), right6(x, 1), NT)
        a_ref[q, rows_of(tile), :] = part
        keep_parts(tile, part)

    def update(j, tile, right, valid, fresh=False):
        if tile is None:
            part = mm(left3(parts_at(tile), 1), right3(parts_at(right), 1), NT)
        else:
            part = mm(left6(parts_at(tile), 1), right6(parts_at(right), 1), NT)
        have = a_ref[j, rows_of(tile), :]
        if fresh:
            have = have * (1.0 - valid)
        a_ref[j, rows_of(tile), :] = have - part * valid

    def chain(p):
        lo = pl.multiple_of(p * PAIR, PAIR)
        top, low = pl.ds(lo, BLK), pl.ds(pl.multiple_of(lo + BLK, BLK), BLK)
        got = []
        return got, inverse_pair(a_ref[p, top, :BLK], a_ref[p, low, :BLK], a_ref[p, low, BLK:], got)

    def settle(p, x):
        a_ref[p, rows_of(p), :] = x.T
        for ref, part in zip(x_refs, split3(x)):
            ref[...] = part
        solve(p, p + 1, [ref[...] for ref in x_refs])
        next_parts = parts_at(p + 1)
        a_ref[p + 1, rows_of(p + 1), :] -= mm(left6(next_parts, 1), right6(next_parts, 1), NT)

    got, steps = chain(0)
    for _ in steps:
        pass
    settle(0, got[0])

    def step(p, _):
        q = p - 1
        x = [ref[...] for ref in x_refs]
        tasks = [lambda: keep_parts(q, a_ref[q, rows_of(q), :])]
        others = [(q + r) % pairs for r in range(2, pairs)]
        tasks += [functools.partial(solve, q, tile, x) for tile in others + [None]]
        for u in range(pairs - 1):
            j = q + 1 + u
            valid = jnp.where(j < pairs, 1.0, 0.0).astype(f32)
            j = j % pairs
            tasks.append(functools.partial(update, j, q, j, valid, True))
            tasks += [functools.partial(update, j, t, j, valid) for t in others[max(u - 1, 0) :] + [None]]
        got, steps = chain(p)
        count = 2 * BLK // AHEAD + 1
        for i, _ in enumerate(steps):
            for _ in range(-(-len(tasks) // max(count - i, 1))):
                tasks.pop(0)()
        for task in tasks:
            task()

        @pl.when(p + 1 < pairs)
        def _():
            settle(p, got[0])

        @pl.when(p + 1 == pairs)
        def _():
            a_ref[p, rows_of(p), :] = got[0].T
            for ref, part in zip(x_refs, split3(got[0])):
                ref[...] = part

        return 0

    lax.fori_loop(1, pairs, step, 0)
    solve(pairs - 1, None, [ref[...] for ref in x_refs])
    white = jnp.concatenate([a_ref[p, n:, :] for p in range(pairs)], 1)
    white_parts = split2(white)
    for ref, part in zip(white_refs, white_parts):
        ref[...] = part
    rows = white.shape[0]
    norm = jnp.sqrt(jnp.sum(white * white, axis=1, keepdims=True) + epsilon)
    unit = white / norm
    hit = (lax.broadcasted_iota(jnp.int32, (rows, rows), 0) == partner_ref[...]).astype(f32)
    both = (hit + hit.T).astype(bf16)
    parts = split3(unit)
    near = mm(jnp.concatenate([both] * 3, 1), jnp.concatenate(parts, 0), NN)
    grad_unit = 2.0 * (2.0 * unit - near)
    inner = jnp.sum(white * grad_unit, axis=1, keepdims=True)
    grad = grad_unit / norm - white * (inner / (norm * norm * norm))
    grad_ref[...] = grad
    diagonals = lower_products(left3(split2(grad), 0), right3(white_parts, 0), pay_ref, blocks)
    scatter_from(pos, pay_ref, keep_ref, send_ref, devices)
    totals = [jnp.sum(rows, axis=0, keepdims=True) for rows in (grad, white)]
    put_extra((keep_ref, send_ref), pay_ref.shape[0] // 2, totals + diagonals)


def inverse_kernel(a_ref, *refs):
    x, outs = [ref[...] for ref in refs[:3]], refs[3:]
    pairs = a_ref.shape[0]
    for p in range(pairs):
        lo, hi = p * PAIR, (p + 1) * PAIR
        for i in range(0, hi, PAIR):
            have = a_ref[p, i : i + PAIR, :]
            if p == pairs - 1 and i < lo:
                have = mm(left6(split3(have), 1), right6(x, 1), NT)
            for out, part in zip(outs, split2(have)):
                out[i : i + PAIR, lo:hi] = part


def moment_product(parts, pay_ref, diagonals, blocks):
    n = blocks * BLK
    at, _ = starts(blocks)
    outs = [0.0] * (blocks // 2)
    for j in range(0, blocks, 2):
        lo, hi = j * BLK, (j + 2) * BLK
        cross = pay_ref[at[j] + BLK : at[j] + PAIR, :]
        one, two = unpack(pay_ref, at[j], diagonals[j // 2])
        column = jnp.concatenate([jnp.concatenate([one, cross], 0), jnp.concatenate([cross.T, two], 0)], 1)
        outs[j // 2] += mm(left3([p[:, lo:hi] for p in parts], 1), right3(split2(column), 0), NN)
        if hi < n:
            rest = [pay_ref[at[j] + PAIR : at[j] + n - lo, :], pay_ref[at[j + 1] : at[j + 1] + n - hi, :]]
            rest = split2(jnp.concatenate(rest, 1))
            outs[j // 2] += mm(left3([p[:, hi:] for p in parts], 1), right3(rest, 0), NN)
            turned = mm(left3([p[:, lo:hi] for p in parts], 1), right3(rest, 1), NT)
            for i in range(hi, n, PAIR):
                outs[i // PAIR] += turned[:, i - hi : i - hi + PAIR]
    return jnp.concatenate(outs, 1)


def back_kernel(blocks, total_rows, devices, parts, shares, *refs):
    pos_ref, sums_ref, grad_ref = refs[:3]
    xt_refs, white_refs = refs[3:5], refs[5:7]
    part_refs = refs[7 : 7 + parts]
    out_ref, wide_refs, pay_ref = refs[7 + parts], refs[8 + parts : -1], refs[-1]
    gather_into(pos_ref[0, 0], part_refs, pay_ref, devices)
    n = blocks * BLK
    sums = split2(jnp.broadcast_to(get_row(sums_ref, blocks, blocks), (16, n)))
    rows = [jnp.concatenate([w[...], s], 0) for w, s in zip(white_refs, sums)]
    firsts = jnp.concatenate([grad_ref[...], jnp.broadcast_to(get_row(sums_ref, 0, blocks), (16, n))], 0)
    diagonals = [sums_ref[2 * blocks + p : 2 * blocks + p + 1, :] for p in range(blocks // 2)]
    left = split2(firsts - moment_product(rows, pay_ref, diagonals, blocks) / (total_rows - 1))
    local = grad_ref.shape[0]
    for lo in range(0, n, PAIR):
        here = slice(lo, lo + PAIR)
        cent = mm(left3([p[:, lo:] for p in left], 1), right3([x[here, lo:] for x in xt_refs], 1), NT)
        grad_z = (cent[:local] - cent[local : local + 1, :] / total_rows).astype(bf16)
        out_ref[:, here] = grad_z
        wide = grad_z.astype(f32)
        at = 0
        for ref, share in zip(wide_refs, shares):
            first, last = max(at, lo), min(at + share, lo + PAIR)
            if first < last:
                ref[:, first - at : last - at] = wide[:, first - lo : last - lo]
            at += share


def call(kernel, outs, *args, scratch=(), limit=24, places=None, flops=10**6):
    return pl.pallas_call(
        kernel,
        out_shape=tuple(jax.ShapeDtypeStruct(s, t) for s, t in outs),
        in_specs=[SMEM if a.dtype == jnp.int32 and a.size == 1 else (VMEM if places is None else HBM) for a in args],
        out_specs=(VMEM,) * len(outs) if places is None else places,
        scratch_shapes=list(scratch),
        compiler_params=pltpu.CompilerParams(vmem_limit_bytes=limit * 2**20),
        cost_estimate=pl.CostEstimate(flops=flops, bytes_accessed=10**6, transcendentals=0),
    )(*args)


def halving(emb):
    per, groups = lax.axis_size("dp"), lax.axis_size("group")
    group = [per << i for i in range(groups.bit_length() - 1)]
    rest = [2 << i for i in range(per.bit_length() - 2)]
    return (group + rest, group[::-1] + rest, rest + group), (3 * emb // 8, 3 * emb // 8, emb // 4)


def weight_sums(near, far, wide, mine, weight):
    orders, shares = halving(weight.shape[1])
    there = [swap(w, order[0], 1) for w, order in zip(wide, orders)]
    beside = [swap(w, 1, 1) for w in wide]
    product = mm(mine, weight, NT).astype(bf16)
    beside, product = lax.optimization_barrier((beside, product))
    kept, sent, last = [None] * len(orders), [None] * len(orders), product
    for group in ((2,), (0, 1)):
        ins = [there[p] for p in group], [beside[p] for p in group], last
        ins, others, last = lax.optimization_barrier(ins)
        if group == (2,):
            product = last
        across = [swap(t, 1, 1) for t in ins]
        for p, t, o, c in zip(group, ins, others, across):
            shape = ((near[p].shape[0] // 2, shares[p]), f32)
            kept[p], last = call(part_kernel, [shape, shape], near[p], far[p], wide[p], o, t, c)
            sent[p] = swap(last, orders[p][1], 1)
    orders = list(orders)
    for step in range(2, len(orders[0])):
        if len(orders) == 3 and orders[0][step:] == orders[1][step:]:
            both = lax.optimization_barrier((kept[0], sent[0], kept[1], sent[1], last))
            last = both[4]
            kept = [jnp.concatenate([both[0], both[2]], 1), kept[2]]
            sent = [jnp.concatenate([both[1], both[3]], 1), sent[2]]
            orders = orders[1:]
        for p, order in enumerate(orders):
            k, r, last = lax.optimization_barrier((kept[p], sent[p], last))
            size = k.shape[0] // 2
            last = k[size:] + r[size:]
            kept[p] = k[:size] + r[:size]
            sent[p] = swap(last, order[step], 1)
    return jnp.concatenate([k + r for k, r in zip(kept, sent)], 1), product


def body(hidden, weight, partners):
    local, hid = hidden.shape
    emb = weight.shape[1]
    blocks = emb // BLK
    devices = lax.axis_size("group") * lax.axis_size("dp")
    total_rows = local * devices
    _, packed = starts(blocks)
    rows = padded(packed)
    half = rows // 2
    extra = -(-(blocks // 2) // 8) * 8
    pos = place()
    pay_scratch = pltpu.VMEM((rows, BLK), f32)

    slabs = 4
    embedded, keep, send, early = call(
        functools.partial(front_kernel, blocks, devices),
        [((local, emb), f32)] + [((half + blocks + extra, BLK), f32)] * 2 + [((local, hid), bf16)],
        pos,
        *(pltpu.with_memory_space_constraint(a, pltpu.HBM) for a in (hidden, weight)),
        scratch=[
            pay_scratch,
            pltpu.VMEM((hid, emb), bf16),
            pltpu.VMEM((local, emb), f32),
            pltpu.SemaphoreType.DMA((slabs + 2,)),
        ],
        places=(HBM, VMEM, VMEM, VMEM),
    )
    me = (lax.axis_index("group") * lax.axis_size("dp") + lax.axis_index("dp")).astype(jnp.int32).reshape(1, 1)
    turned_keep, turned_send = call(
        turn_kernel,
        [((hid // 2, local), f32)] * 2,
        me,
        early,
        scratch=[pltpu.VMEM((hid, local), f32)],
        flops=10**9,
    )
    orders, shares = halving(emb)
    turned = call(
        functools.partial(order_kernel, orders),
        [((hid // 4, 2 * local), bf16)] * len(orders) + [((hid // 4, 2 * local), f32)] * len(orders),
        me,
        turned_keep,
        swap(turned_send, 1, 1),
        scratch=[pltpu.VMEM((hid // 4, 2 * local), f32)],
        flops=10**9,
    )
    part, sums = reduce_scatter(keep, send, half, blocks)
    parts, turned = all_gather(part, turned)
    near = turned[: len(orders)]
    far = [swap(t, order[0], 1) for t, order in zip(turned[len(orders) :], orders)]
    wh, wl, x1, x2, x3, eliminated, grad, keep, send = call(
        functools.partial(factor_kernel, blocks, total_rows, devices, len(parts)),
        [((local, emb), bf16)] * 2
        + [((PAIR, PAIR), bf16)] * 3
        + [((emb // PAIR, emb + local, PAIR), f32), ((local, emb), f32)]
        + [((half + 2 * blocks + extra, BLK), f32)] * 2,
        pos,
        sums,
        embedded,
        partners,
        *parts,
        scratch=[pay_scratch] + [pltpu.VMEM((emb + local, PAIR), bf16)] * 3,
        limit=32,
        flops=3 * 10**10,
    )
    keep, send, far = lax.optimization_barrier((keep, send, far))
    part, sums = reduce_scatter(keep, send, half, 0)
    inverse = call(inverse_kernel, [((emb, emb), bf16)] * 2, eliminated, x1, x2, x3, flops=3 * 10**9)
    parts, (xh, xl) = all_gather(part, inverse)
    grad_z, *wide = call(
        functools.partial(back_kernel, blocks, total_rows, devices, len(parts), shares),
        [((local, emb), bf16)] + [((local, share), f32) for share in shares],
        pos,
        sums,
        grad,
        xh,
        xl,
        wh,
        wl,
        *parts,
        scratch=[pay_scratch],
        limit=32,
    )
    grad_weight, grad_hidden = weight_sums(near, far, wide, grad_z, weight)
    return (wh, grad_weight, grad_hidden)


def solution(mesh):
    return jax.shard_map(
        body,
        mesh=mesh,
        in_specs=(P(AXES, None), P(), P(AXES, None)),
        out_specs=(P(AXES, None), P(AXES, None), P(AXES, None)),
        check_vma=False,
    )
```

```python
import functools

import jax
import jax.numpy as jnp
from jax import lax
from jax.experimental import pallas as pl
from jax.experimental.pallas import tpu as pltpu
from jax.sharding import PartitionSpec as P

AXES = ("group", "dp")
epsilon = 1e-06
f32 = jnp.float32
bf16 = jnp.bfloat16
NN = (((1,), (0,)), ((), ()))
NT = (((1,), (1,)), ((), ()))
TN = (((0,), (0,)), ((), ()))
BLK = 128
PAIR = 256
PANEL = 32
AHEAD = 16
VMEM = pl.BlockSpec(memory_space=pltpu.VMEM)
SMEM = pl.BlockSpec(memory_space=pltpu.SMEM)
HBM = pl.BlockSpec(memory_space=pltpu.HBM)


def split2(x):
    high = x.astype(bf16)
    return high, (x - high.astype(f32)).astype(bf16)


def split3(x):
    high = x.astype(bf16)
    rest = x - high.astype(f32)
    mid = rest.astype(bf16)
    return high, mid, (rest - mid.astype(f32)).astype(bf16)


def left6(parts, axis):
    high, mid, low = parts
    return jnp.concatenate([high, high, mid, high, low, mid], axis=axis)


def right6(parts, axis):
    high, mid, low = parts
    return jnp.concatenate([high, mid, high, low, high, mid], axis=axis)


def left3(parts, axis):
    return jnp.concatenate([parts[0], parts[0], parts[1]], axis=axis)


def right3(parts, axis):
    return jnp.concatenate([parts[0], parts[1], parts[0]], axis=axis)


def mm(a, b, dims):
    return lax.dot_general(a, b, dims, preferred_element_type=f32)


def dot6(a, b, dims):
    (ca,), (cb,) = dims[0]
    return mm(left6(split3(a), ca), right6(split3(b), cb), dims)


def dot3(a, b, dims):
    (ca,), (cb,) = dims[0]
    return mm(left3(split2(a), ca), right3(split2(b), cb), dims)


def starts(blocks):
    out, at = [], 0
    for j in range(blocks):
        out.append(at)
        at += (blocks - j - j % 2) * BLK
    return out, at


def radices(count):
    out = []
    while count > 1:
        out.append(4 if count % 4 == 0 else 2)
        count //= out[-1]
    return out


def rounds():
    groups, per = lax.axis_size("group"), lax.axis_size("dp")
    out, at = [(1, 2)], per
    for radix in radices(groups):
        out.append((at, radix))
        at *= radix
    at = 2
    for radix in radices(per // 2):
        out.append((at, radix))
        at *= radix
    return out


def place():
    index = lax.axis_index("group") * lax.axis_size("dp") + lax.axis_index("dp")
    out = 0
    for stride, radix in rounds():
        out = out * radix + (index // stride) % radix
    return out.astype(jnp.int32).reshape(1, 1)


def swap(x, stride, by):
    return exchange(x, (by * stride, by * stride))


def exchange(x, bits):
    count = lax.axis_size("group") * lax.axis_size("dp")
    return lax.ppermute(x, AXES, [(i, i ^ bits[i % 2]) for i in range(count)])


def combine_kernel(size, listed, parts, radix, *refs):
    ins, outs = refs[:parts], refs[parts:]
    total, more = ins[0][0:size, :], ins[0][size + listed :, :]
    for r in ins[1:]:
        total = total + r[0:size, :]
        more = more + r[size + listed :, :]
    if listed:
        more = jnp.concatenate([r[size : size + listed, :] for r in ins] + [more], 0)
    if radix == 1:
        outs[0][...] = total
        outs[1][...] = more
        return
    cut = size // radix
    for i, out in enumerate(outs):
        out[0:cut, :] = total[i * cut : (i + 1) * cut, :]
        out[cut:, :] = more


def reduce_scatter(keep, send, size, listed):
    steps = rounds()
    summed = keep.shape[0] - size - listed
    pieces = [keep, send]
    for at, (stride, radix) in enumerate(steps):
        ins = [pieces[0]] + [swap(p, stride, by) for by, p in enumerate(pieces) if by]
        after = steps[at + 1][1] if at + 1 < len(steps) else 1
        more = listed * radix + summed
        shapes = [(size // after + more, BLK)] * after if after > 1 else [(size, BLK), (more, BLK)]
        pieces = call(
            functools.partial(combine_kernel, size, listed, len(ins), after),
            [(s, f32) for s in shapes],
            *ins,
        )
        listed, size = listed * radix, size // after
    return pieces


def all_gather(x, beside=()):
    steps = rounds()
    parts = [x]
    for at in range(len(steps) - 1, 0, -1):
        stride, radix = steps[at]
        whole = parts[0] if len(parts) == 1 else jnp.concatenate(parts, 0)
        parts = [whole] + [swap(whole, stride, by) for by in range(1, radix)]
        if at == len(steps) - 1:
            parts, beside = lax.optimization_barrier((parts, beside))
    return parts + [swap(p, 1, 1) for p in parts], beside


def padded(rows):
    unit = 8 * lax.axis_size("group") * lax.axis_size("dp")
    return -(-rows // unit) * unit


def gather_into(pos, parts, out_ref, devices):
    chunk = out_ref.shape[0] // devices
    each = devices // len(parts)
    for i, part in enumerate(parts):
        for j in range(each):
            to = pl.multiple_of(((i * each + j) ^ pos) * chunk, 8)
            out_ref[pl.ds(to, chunk), :] = part[j * chunk : (j + 1) * chunk, :]


def scatter_from(pos, src_ref, keep_ref, send_ref, devices):
    chunk = src_ref.shape[0] // devices
    half = devices // 2
    for i in range(devices):
        at = pl.multiple_of((i ^ pos) * chunk, 8)
        out = keep_ref if i < half else send_ref
        out[(i % half) * chunk : (i % half + 1) * chunk, :] = src_ref[pl.ds(at, chunk), :]


def put_row(out_ref, at, row):
    for i in range(row.shape[1] // BLK):
        out_ref[at + i : at + i + 1, :] = row[:, i * BLK : (i + 1) * BLK]


def put_extra(refs, at, rows):
    count = sum(row.shape[1] // BLK for row in rows)
    for ref in refs:
        end = at
        for row in rows:
            put_row(ref, end, row)
            end += row.shape[1] // BLK
        if count % 8:
            ref[end : at + count + 8 - count % 8, :] = jnp.zeros((8 - count % 8, BLK), f32)


def get_row(ref, at, blocks):
    return jnp.concatenate([ref[at + i : at + i + 1, :] for i in range(blocks)], 1)


def triangle():
    shape = (BLK, BLK)
    rows, cols = lax.broadcasted_iota(jnp.int32, shape, 0), lax.broadcasted_iota(jnp.int32, shape, 1)
    return rows > cols, rows == cols


def lower_products(left, right, out_ref, blocks):
    at, total = starts(blocks)
    n = blocks * BLK
    below, middle = triangle()
    diagonals = []
    for j in range(0, blocks, 2):
        lo = j * BLK
        part = mm(left[:, lo:], right[:, lo : lo + PAIR], TN)
        other = part[BLK:PAIR, BLK:]
        diagonals.append(jnp.sum(jnp.where(middle, other, 0.0), axis=0, keepdims=True))
        out_ref[at[j] : at[j] + BLK, :] = jnp.where(below, part[:BLK, :BLK], jnp.where(middle, part[:BLK, :BLK], other.T))
        out_ref[at[j] + BLK : at[j] + n - lo, :] = part[BLK:, :BLK]
        if lo + PAIR < n:
            out_ref[at[j + 1] : at[j + 1] + n - lo - PAIR, :] = part[PAIR:, BLK:]
    if out_ref.shape[0] > total:
        out_ref[total:, :] = jnp.zeros((out_ref.shape[0] - total, BLK), f32)
    return diagonals


def unpack(pay_ref, at, diagonal):
    below, middle = triangle()
    packed = pay_ref[at : at + BLK, :]
    one = jnp.where(below, packed, 0.0)
    one = jnp.where(middle, packed, one + one.T)
    two = jnp.where(below | middle, 0.0, packed)
    two = jnp.where(middle, diagonal, two + two.T)
    return one, two


def front_kernel(blocks, devices, pos_ref, hid_hbm, w_hbm, emb_hbm, keep_ref, send_ref, hid_ref, pay_ref, w_ref, emb_ref, sems):
    slabs = sems.shape[0] - 2
    deep = w_hbm.shape[0] // slabs
    copies = [pltpu.make_async_copy(hid_hbm, hid_ref, sems.at[slabs])]
    for i in range(slabs):
        rows = pl.ds(i * deep, deep)
        copies.append(pltpu.make_async_copy(w_hbm.at[rows, :], w_ref.at[rows, :], sems.at[i]))
    for copy in copies:
        copy.start()
    copies[0].wait()
    emb = 0.0
    for i in range(slabs):
        copies[1 + i].wait()
        emb = emb + mm(hid_ref[:, i * deep : (i + 1) * deep], w_ref[i * deep : (i + 1) * deep, :], NN)
    emb_ref[...] = emb
    out = pltpu.make_async_copy(emb_ref, emb_hbm, sems.at[slabs + 1])
    out.start()
    total = jnp.sum(emb, axis=0, keepdims=True)
    parts = split3(emb - total / emb.shape[0])
    diagonals = lower_products(left6(parts, 0), right6(parts, 0), pay_ref, blocks)
    scatter_from(pos_ref[0, 0], pay_ref, keep_ref, send_ref, devices)
    put_extra((keep_ref, send_ref), pay_ref.shape[0] // 2, [total] + diagonals)
    out.wait()


def turn_kernel(me_ref, hid_ref, keep_ref, send_ref, turned_ref):
    turned_ref[...] = hid_ref[...].astype(f32).T
    count = lax.axis_size("group") * lax.axis_size("dp")
    own = turned_ref.shape[0] // count
    core = me_ref[0, 0] % 2
    for out, c in ((keep_ref, core), (send_ref, 1 - core)):
        for i in range(count // 2):
            rows = turned_ref[pl.ds(pl.multiple_of((2 * i + c) * own, 8), own), :]
            out[i * own : (i + 1) * own, :] = rows


def order_kernel(orders, me_ref, keep_ref, got_ref, *refs):
    near_refs, far_refs, part_ref = refs[: len(orders)], refs[len(orders) : -1], refs[-1]
    chip, core = me_ref[0, 0] // 2, me_ref[0, 0] % 2
    half = part_ref.shape[0]
    own = half * 2 >> len(orders[0])
    local = keep_ref.shape[1]
    for bits, near_ref, far_ref in zip(orders, near_refs, far_refs):
        for side, out in ((0, part_ref), (1, far_ref)):
            for i in range(half // own):
                far = [bits[0][0] * side] * 2
                for t, bit in enumerate(reversed(bits[1:])):
                    far = [f | b * ((i >> t) & 1) for f, b in zip(far, bit)]
                differ = far[0] // 2 if far[0] == far[1] else jnp.where(core == 0, far[0] // 2, far[1] // 2)
                rows = pl.ds(pl.multiple_of((chip ^ differ) * own, 8), own)
                out[i * own : (i + 1) * own, :local] = keep_ref[rows, :]
                out[i * own : (i + 1) * own, local:] = got_ref[rows, :]
        near_ref[...] = part_ref[...].astype(bf16)


def part_kernel(near_ref, far_ref, *refs):
    rows, (keep_ref, send_ref) = refs[:4], refs[4:]
    left = jnp.concatenate([near_ref[...], far_ref[...].astype(bf16)], 1)
    part = mm(left, jnp.concatenate([r[...].astype(bf16) for r in rows], 0), NN)
    half = keep_ref.shape[0]
    keep_ref[...] = part[:half]
    send_ref[...] = part[half:]


def lane(x, c):
    return jnp.broadcast_to(x[:, c : c + 1], (x.shape[0], BLK))


def sub(x, i):
    return jnp.broadcast_to(x[i : i + 1, :], (8, x.shape[1]))


def eye():
    shape = (BLK, BLK)
    return (lax.broadcasted_iota(jnp.int32, shape, 0) == lax.broadcasted_iota(jnp.int32, shape, 1)).astype(f32)


def inverse_factor(s, out):
    row = lax.broadcasted_iota(jnp.int32, (8, BLK), 0)
    t = eye()
    count = PANEL // 8
    outs = []
    for at in range(0, BLK, PANEL):
        r = [s[8 * q : 8 * q + 8] for q in range(count)]
        v = [t[8 * q : 8 * q + 8] for q in range(count)]
        pivots = [jnp.ones((8, BLK), f32)] * count
        for first in range(0, PANEL, AHEAD):
            last = first + AHEAD
            a = {(l, q): lane(r[q], at + l) for l in range(first, last) for q in range(l // 8, count)}
            for c in range(first, last):
                p, i = c // 8, c % 8
                piv = {l: sub(a[c, l // 8], l % 8) for l in range(c, last)}
                inv = 1.0 / piv[c]
                pivots[p] = jnp.where(row == i, piv[c], pivots[p])
                rs, vs = sub(r[p], i), sub(v[p], i)
                for q in range(p, count):
                    if q == p and i == 7:
                        continue
                    m = a[c, q] * inv
                    if q == p:
                        m = jnp.where(row > i, m, 0.0)
                    for l in range(c + 1, last):
                        if q >= l // 8:
                            a[l, q] = a[l, q] - m * piv[l]
                    r[q] = r[q] - m * rs
                    v[q] = v[q] - m * vs
            yield
        scale = [lax.rsqrt(p) for p in pivots]
        u = jnp.concatenate([x * g for x, g in zip(r, scale)], 0)
        w = jnp.concatenate([x * g for x, g in zip(v, scale)], 0)
        outs.append(w)
        if at + PANEL < BLK:
            us, ws = split3(u), split3(w)
            right = jnp.concatenate([right6(us, 0), right6(ws, 0)], axis=1)
            update = mm(left6(us, 0), right, TN)
            s = s[PANEL:] - update[at + PANEL :, :BLK]
            t = t[PANEL:] - update[at + PANEL :, BLK:]
    out.append(jnp.concatenate(outs, 0))


def inverse_pair(s11, s21, s22, out):
    got = []
    yield from inverse_factor(s11, got)
    l21 = dot6(s21, got[0], NT)
    rest = s22 - dot6(l21, l21, NT)
    yield
    yield from inverse_factor(rest, got)
    x21 = -dot6(got[1], dot6(l21, got[0], NN), NN)
    top = jnp.concatenate([got[0], jnp.zeros((BLK, BLK), f32)], 1)
    out.append(jnp.concatenate([top, jnp.concatenate([x21, got[1]], 1)], 0))


def factor_kernel(blocks, total_rows, devices, parts, *refs):
    pos_ref, sums_ref, emb_ref, partner_ref = refs[:4]
    part_refs = refs[4 : 4 + parts]
    white_refs, x_refs = refs[4 + parts : 6 + parts], refs[6 + parts : 9 + parts]
    a_ref, grad_ref, keep_ref, send_ref, pay_ref, high_ref, mid_ref, low_ref = refs[9 + parts :]
    pos = pos_ref[0, 0]
    gather_into(pos, part_refs, pay_ref, devices)
    n = blocks * BLK
    local = emb_ref.shape[0]
    at, _ = starts(blocks)
    sums = jnp.concatenate([sums_ref[pl.ds(j, devices, blocks), :] for j in range(blocks)], 1)
    mean = jnp.sum(sums, axis=0, keepdims=True) / total_rows
    apart = sums / local - mean
    left, right = left6(split3(apart), 0), right6(split3(apart), 0)
    pairs = blocks // 2
    for p in range(pairs):
        lo, hi = p * PAIR, (p + 1) * PAIR
        between = local * mm(left[:, lo:], right[:, lo:hi], TN)
        begin, after = at[2 * p], at[2 * p + 1]
        d = devices * blocks + p
        one, two = unpack(pay_ref, begin, sums_ref[d : d + 1, :])
        scale = 1.0 / (total_rows - 1)
        a_ref[p, lo : lo + BLK, :BLK] = (one + between[:BLK, :BLK]) * scale
        a_ref[p, lo + BLK : n, :BLK] = (pay_ref[begin + BLK : begin + n - lo, :] + between[BLK:, :BLK]) * scale
        a_ref[p, lo + BLK : hi, BLK:] = (two + between[BLK:PAIR, BLK:]) * scale
        if hi < n:
            a_ref[p, hi:n, BLK:] = (pay_ref[after : after + n - hi, :] + between[PAIR:, BLK:]) * scale
        a_ref[p, n:, :] = emb_ref[:, lo:hi] - mean[:, lo:hi]
    last = pairs * PAIR

    def rows_of(tile):
        return pl.ds(pl.multiple_of(tile * PAIR, PAIR), PAIR) if tile is not None else slice(last, last + local)

    def keep_parts(tile, x):
        for ref, part in zip((high_ref, mid_ref, low_ref), split3(x)):
            ref[rows_of(tile), :] = part

    def parts_at(tile):
        return [ref[rows_of(tile), :] for ref in (high_ref, mid_ref, low_ref)]

    def solve(q, tile, x):
        if tile is None:
            part = mm(left3(split2(a_ref[q, rows_of(tile), :]), 1), right3(x, 1), NT)
        else:
            part = mm(left6(split3(a_ref[q, rows_of(tile), :]), 1), right6(x, 1), NT)
        a_ref[q, rows_of(tile), :] = part
        keep_parts(tile, part)

    def update(j, tile, right, valid, fresh=False):
        if tile is None:
            part = mm(left3(parts_at(tile), 1), right3(parts_at(right), 1), NT)
        else:
            part = mm(left6(parts_at(tile), 1), right6(parts_at(right), 1), NT)
        have = a_ref[j, rows_of(tile), :]
        if fresh:
            have = have * (1.0 - valid)
        a_ref[j, rows_of(tile), :] = have - part * valid

    def chain(p):
        lo = pl.multiple_of(p * PAIR, PAIR)
        top, low = pl.ds(lo, BLK), pl.ds(pl.multiple_of(lo + BLK, BLK), BLK)
        got = []
        return got, inverse_pair(a_ref[p, top, :BLK], a_ref[p, low, :BLK], a_ref[p, low, BLK:], got)

    def settle(p, x):
        a_ref[p, rows_of(p), :] = x.T
        for ref, part in zip(x_refs, split3(x)):
            ref[...] = part
        solve(p, p + 1, [ref[...] for ref in x_refs])
        next_parts = parts_at(p + 1)
        a_ref[p + 1, rows_of(p + 1), :] -= mm(left6(next_parts, 1), right6(next_parts, 1), NT)

    got, steps = chain(0)
    for _ in steps:
        pass
    settle(0, got[0])

    def step(p, _):
        q = p - 1
        x = [ref[...] for ref in x_refs]
        tasks = [lambda: keep_parts(q, a_ref[q, rows_of(q), :])]
        others = [(q + r) % pairs for r in range(2, pairs)]
        tasks += [functools.partial(solve, q, tile, x) for tile in others + [None]]
        for u in range(pairs - 1):
            j = q + 1 + u
            valid = jnp.where(j < pairs, 1.0, 0.0).astype(f32)
            j = j % pairs
            tasks.append(functools.partial(update, j, q, j, valid, True))
            tasks += [functools.partial(update, j, t, j, valid) for t in others[max(u - 1, 0) :] + [None]]
        got, steps = chain(p)
        count = 2 * BLK // AHEAD + 1
        for i, _ in enumerate(steps):
            for _ in range(-(-len(tasks) // max(count - i, 1))):
                tasks.pop(0)()
        for task in tasks:
            task()

        @pl.when(p + 1 < pairs)
        def _():
            settle(p, got[0])

        @pl.when(p + 1 == pairs)
        def _():
            a_ref[p, rows_of(p), :] = got[0].T
            for ref, part in zip(x_refs, split3(got[0])):
                ref[...] = part

        return 0

    lax.fori_loop(1, pairs, step, 0)
    solve(pairs - 1, None, [ref[...] for ref in x_refs])
    white = jnp.concatenate([a_ref[p, n:, :] for p in range(pairs)], 1)
    white_parts = split2(white)
    for ref, part in zip(white_refs, white_parts):
        ref[...] = part
    rows = white.shape[0]
    norm = jnp.sqrt(jnp.sum(white * white, axis=1, keepdims=True) + epsilon)
    unit = white / norm
    hit = (lax.broadcasted_iota(jnp.int32, (rows, rows), 0) == partner_ref[...]).astype(f32)
    both = (hit + hit.T).astype(bf16)
    parts = split3(unit)
    near = mm(jnp.concatenate([both] * 3, 1), jnp.concatenate(parts, 0), NN)
    grad_unit = 2.0 * (2.0 * unit - near)
    inner = jnp.sum(white * grad_unit, axis=1, keepdims=True)
    grad = grad_unit / norm - white * (inner / (norm * norm * norm))
    grad_ref[...] = grad
    diagonals = lower_products(left3(split2(grad), 0), right3(white_parts, 0), pay_ref, blocks)
    scatter_from(pos, pay_ref, keep_ref, send_ref, devices)
    totals = [jnp.sum(rows, axis=0, keepdims=True) for rows in (grad, white)]
    put_extra((keep_ref, send_ref), pay_ref.shape[0] // 2, totals + diagonals)


def inverse_kernel(a_ref, *refs):
    x, outs = [ref[...] for ref in refs[:3]], refs[3:]
    pairs = a_ref.shape[0]
    for p in range(pairs):
        lo, hi = p * PAIR, (p + 1) * PAIR
        for i in range(0, hi, PAIR):
            have = a_ref[p, i : i + PAIR, :]
            if p == pairs - 1 and i < lo:
                have = mm(left6(split3(have), 1), right6(x, 1), NT)
            for out, part in zip(outs, split2(have)):
                out[i : i + PAIR, lo:hi] = part


def moment_product(parts, pay_ref, diagonals, blocks):
    n = blocks * BLK
    at, _ = starts(blocks)
    outs = [0.0] * (blocks // 2)
    for j in range(0, blocks, 2):
        lo, hi = j * BLK, (j + 2) * BLK
        cross = pay_ref[at[j] + BLK : at[j] + PAIR, :]
        one, two = unpack(pay_ref, at[j], diagonals[j // 2])
        column = jnp.concatenate([jnp.concatenate([one, cross], 0), jnp.concatenate([cross.T, two], 0)], 1)
        outs[j // 2] += mm(left3([p[:, lo:hi] for p in parts], 1), right3(split2(column), 0), NN)
        if hi < n:
            rest = [pay_ref[at[j] + PAIR : at[j] + n - lo, :], pay_ref[at[j + 1] : at[j + 1] + n - hi, :]]
            rest = split2(jnp.concatenate(rest, 1))
            outs[j // 2] += mm(left3([p[:, hi:] for p in parts], 1), right3(rest, 0), NN)
            turned = mm(left3([p[:, lo:hi] for p in parts], 1), right3(rest, 1), NT)
            for i in range(hi, n, PAIR):
                outs[i // PAIR] += turned[:, i - hi : i - hi + PAIR]
    return jnp.concatenate(outs, 1)


def back_kernel(blocks, total_rows, devices, parts, shares, *refs):
    pos_ref, sums_ref, grad_ref = refs[:3]
    xt_refs, white_refs = refs[3:5], refs[5:7]
    part_refs = refs[7 : 7 + parts]
    out_ref, wide_refs, pay_ref = refs[7 + parts], refs[8 + parts : -1], refs[-1]
    gather_into(pos_ref[0, 0], part_refs, pay_ref, devices)
    n = blocks * BLK
    sums = split2(jnp.broadcast_to(get_row(sums_ref, blocks, blocks), (16, n)))
    rows = [jnp.concatenate([w[...], s], 0) for w, s in zip(white_refs, sums)]
    firsts = jnp.concatenate([grad_ref[...], jnp.broadcast_to(get_row(sums_ref, 0, blocks), (16, n))], 0)
    diagonals = [sums_ref[2 * blocks + p : 2 * blocks + p + 1, :] for p in range(blocks // 2)]
    left = split2(firsts - moment_product(rows, pay_ref, diagonals, blocks) / (total_rows - 1))
    local = grad_ref.shape[0]
    for lo in range(0, n, PAIR):
        here = slice(lo, lo + PAIR)
        cent = mm(left3([p[:, lo:] for p in left], 1), right3([x[here, lo:] for x in xt_refs], 1), NT)
        grad_z = (cent[:local] - cent[local : local + 1, :] / total_rows).astype(bf16)
        out_ref[:, here] = grad_z
        wide = grad_z.astype(f32)
        at = 0
        for ref, share in zip(wide_refs, shares):
            first, last = max(at, lo), min(at + share, lo + PAIR)
            if first < last:
                ref[:, first - at : last - at] = wide[:, first - lo : last - lo]
            at += share


def call(kernel, outs, *args, scratch=(), limit=24, places=None, flops=10**6):
    return pl.pallas_call(
        kernel,
        out_shape=tuple(jax.ShapeDtypeStruct(s, t) for s, t in outs),
        in_specs=[SMEM if a.dtype == jnp.int32 and a.size == 1 else (VMEM if places is None else HBM) for a in args],
        out_specs=(VMEM,) * len(outs) if places is None else places,
        scratch_shapes=list(scratch),
        compiler_params=pltpu.CompilerParams(vmem_limit_bytes=limit * 2**20),
        cost_estimate=pl.CostEstimate(flops=flops, bytes_accessed=10**6, transcendentals=0),
    )(*args)


def halving(emb):
    per, groups = lax.axis_size("dp"), lax.axis_size("group")
    group = [(per << i,) * 2 for i in range(groups.bit_length() - 1)]
    rest = [2 << i for i in range(per.bit_length() - 2)]
    crossed = list(zip(rest, rest[1::-1] + rest[2:]))
    rest = [(bit, bit) for bit in rest]
    return (group + crossed, group[::-1] + crossed, rest + group), (3 * emb // 8, 3 * emb // 8, emb // 4)


def weight_sums(near, far, wide, mine, weight):
    orders, shares = halving(weight.shape[1])
    there = [exchange(w, order[0]) for w, order in zip(wide, orders)]
    beside = [swap(w, 1, 1) for w in wide]
    product = mm(mine, weight, NT).astype(bf16)
    beside, product = lax.optimization_barrier((beside, product))
    kept, sent, last = [None] * len(orders), [None] * len(orders), product
    for group in ((2,), (0, 1)):
        ins = [there[p] for p in group], [beside[p] for p in group], last
        ins, others, last = lax.optimization_barrier(ins)
        if group == (2,):
            product = last
        across = [swap(t, 1, 1) for t in ins]
        for p, t, o, c in zip(group, ins, others, across):
            shape = ((near[p].shape[0] // 2, shares[p]), f32)
            kept[p], last = call(part_kernel, [shape, shape], near[p], far[p], wide[p], o, t, c)
            sent[p] = exchange(last, orders[p][1])
    orders = list(orders)
    for step in range(2, len(orders[0])):
        for p in reversed(range(len(orders))):
            if p == 1 and len(orders) == 3 and orders[0][step:] == orders[1][step:]:
                both = lax.optimization_barrier((kept[0], sent[0], kept[1], sent[1], last))
                last = both[4]
                kept = [jnp.concatenate([both[0], both[2]], 1), kept[2]]
                sent = [jnp.concatenate([both[1], both[3]], 1), sent[2]]
                orders = orders[1:]
                p = 0
            k, r, last = lax.optimization_barrier((kept[p], sent[p], last))
            size = k.shape[0] // 2
            last = k[size:] + r[size:]
            kept[p] = k[:size] + r[:size]
            sent[p] = exchange(last, orders[p][step])
            if p == 0:
                break
    return jnp.concatenate([k + r for k, r in zip(kept, sent)], 1), product


def body(hidden, weight, partners):
    local, hid = hidden.shape
    emb = weight.shape[1]
    blocks = emb // BLK
    devices = lax.axis_size("group") * lax.axis_size("dp")
    total_rows = local * devices
    _, packed = starts(blocks)
    rows = padded(packed)
    half = rows // 2
    extra = -(-(blocks // 2) // 8) * 8
    pos = place()
    pay_scratch = pltpu.VMEM((rows, BLK), f32)

    slabs = 4
    embedded, keep, send, early = call(
        functools.partial(front_kernel, blocks, devices),
        [((local, emb), f32)] + [((half + blocks + extra, BLK), f32)] * 2 + [((local, hid), bf16)],
        pos,
        *(pltpu.with_memory_space_constraint(a, pltpu.HBM) for a in (hidden, weight)),
        scratch=[
            pay_scratch,
            pltpu.VMEM((hid, emb), bf16),
            pltpu.VMEM((local, emb), f32),
            pltpu.SemaphoreType.DMA((slabs + 2,)),
        ],
        places=(HBM, VMEM, VMEM, VMEM),
    )
    me = (lax.axis_index("group") * lax.axis_size("dp") + lax.axis_index("dp")).astype(jnp.int32).reshape(1, 1)
    turned_keep, turned_send = call(
        turn_kernel,
        [((hid // 2, local), f32)] * 2,
        me,
        early,
        scratch=[pltpu.VMEM((hid, local), f32)],
        flops=10**9,
    )
    orders, shares = halving(emb)
    turned = call(
        functools.partial(order_kernel, orders),
        [((hid // 4, 2 * local), bf16)] * len(orders) + [((hid // 4, 2 * local), f32)] * len(orders),
        me,
        turned_keep,
        swap(turned_send, 1, 1),
        scratch=[pltpu.VMEM((hid // 4, 2 * local), f32)],
        flops=10**9,
    )
    part, sums = reduce_scatter(keep, send, half, blocks)
    parts, turned = all_gather(part, turned)
    near = turned[: len(orders)]
    far = [exchange(t, order[0]) for t, order in zip(turned[len(orders) :], orders)]
    wh, wl, x1, x2, x3, eliminated, grad, keep, send = call(
        functools.partial(factor_kernel, blocks, total_rows, devices, len(parts)),
        [((local, emb), bf16)] * 2
        + [((PAIR, PAIR), bf16)] * 3
        + [((emb // PAIR, emb + local, PAIR), f32), ((local, emb), f32)]
        + [((half + 2 * blocks + extra, BLK), f32)] * 2,
        pos,
        sums,
        embedded,
        partners,
        *parts,
        scratch=[pay_scratch] + [pltpu.VMEM((emb + local, PAIR), bf16)] * 3,
        limit=32,
        flops=3 * 10**10,
    )
    keep, send, far = lax.optimization_barrier((keep, send, far))
    part, sums = reduce_scatter(keep, send, half, 0)
    inverse = call(inverse_kernel, [((emb, emb), bf16)] * 2, eliminated, x1, x2, x3, flops=3 * 10**9)
    parts, (xh, xl) = all_gather(part, inverse)
    grad_z, *wide = call(
        functools.partial(back_kernel, blocks, total_rows, devices, len(parts), shares),
        [((local, emb), bf16)] + [((local, share), f32) for share in shares],
        pos,
        sums,
        grad,
        xh,
        xl,
        wh,
        wl,
        *parts,
        scratch=[pay_scratch],
        limit=32,
    )
    grad_weight, grad_hidden = weight_sums(near, far, wide, grad_z, weight)
    return (wh, grad_weight, grad_hidden)


def solution(mesh):
    return jax.shard_map(
        body,
        mesh=mesh,
        in_specs=(P(AXES, None), P(), P(AXES, None)),
        out_specs=(P(AXES, None), P(AXES, None), P(AXES, None)),
        check_vma=False,
    )
```

```python
import functools

import jax
import jax.numpy as jnp
from jax import lax
from jax.experimental import pallas as pl
from jax.experimental.pallas import tpu as pltpu
from jax.sharding import PartitionSpec as P

AXES = ("group", "dp")
epsilon = 1e-06
f32 = jnp.float32
bf16 = jnp.bfloat16
NN = (((1,), (0,)), ((), ()))
NT = (((1,), (1,)), ((), ()))
TN = (((0,), (0,)), ((), ()))
BLK = 128
PAIR = 256
PANEL = 32
AHEAD = 16
VMEM = pl.BlockSpec(memory_space=pltpu.VMEM)
SMEM = pl.BlockSpec(memory_space=pltpu.SMEM)
HBM = pl.BlockSpec(memory_space=pltpu.HBM)


def split2(x):
    high = x.astype(bf16)
    return high, (x - high.astype(f32)).astype(bf16)


def split3(x):
    high = x.astype(bf16)
    rest = x - high.astype(f32)
    mid = rest.astype(bf16)
    return high, mid, (rest - mid.astype(f32)).astype(bf16)


def left6(parts, axis):
    high, mid, low = parts
    return jnp.concatenate([high, high, mid, high, low, mid], axis=axis)


def right6(parts, axis):
    high, mid, low = parts
    return jnp.concatenate([high, mid, high, low, high, mid], axis=axis)


def left3(parts, axis):
    return jnp.concatenate([parts[0], parts[0], parts[1]], axis=axis)


def right3(parts, axis):
    return jnp.concatenate([parts[0], parts[1], parts[0]], axis=axis)


def mm(a, b, dims):
    return lax.dot_general(a, b, dims, preferred_element_type=f32)


def dot6(a, b, dims):
    (ca,), (cb,) = dims[0]
    return mm(left6(split3(a), ca), right6(split3(b), cb), dims)


def dot3(a, b, dims):
    (ca,), (cb,) = dims[0]
    return mm(left3(split2(a), ca), right3(split2(b), cb), dims)


def starts(blocks):
    out, at = [], 0
    for j in range(blocks):
        out.append(at)
        at += (blocks - j - j % 2) * BLK
    return out, at


def radices(count):
    out = []
    while count > 1:
        out.append(4 if count % 4 == 0 else 2)
        count //= out[-1]
    return out


def rounds():
    groups, per = lax.axis_size("group"), lax.axis_size("dp")
    out, at = [((1, 1), 2)], per
    for radix in radices(groups):
        out.append(((at, at), radix))
        at *= radix
    at = 2
    for radix in radices(per // 2):
        out.append(((at, at), radix))
        at *= radix
    if crossed():
        (one, radix), (two, _) = out[1:3]
        out[1:3] = [((one[0], two[0]), radix), ((two[0], one[0]), radix)]
    return out


def crossed():
    group, rest = radices(lax.axis_size("group")), radices(lax.axis_size("dp") // 2)
    return len(group) == 1 and len(rest) > 0 and group[0] == rest[0]


def place():
    index = lax.axis_index("group") * lax.axis_size("dp") + lax.axis_index("dp")
    out = 0
    for (stride, _), radix in rounds():
        out = out * radix + (index // stride) % radix
    return out.astype(jnp.int32).reshape(1, 1)


def other_order(i):
    if not crossed():
        return i
    radix = lax.axis_size("group")
    low = lax.axis_size("dp") // 2 // radix
    core, first, second = i // (low * radix * radix), i // (low * radix) % radix, i // low % radix
    return ((core * radix + second) * radix + first) * low + i % low


def chunk_at(pos, devices, i, same):
    mine = pos // (devices // 2) == (0 if same else 1)
    far = other_order(i)
    return pos ^ (i if far == i else jnp.where(mine, i, far))


def swap(x, stride, by):
    return exchange(x, (by * stride, by * stride))


def exchange(x, bits):
    count = lax.axis_size("group") * lax.axis_size("dp")
    return lax.ppermute(x, AXES, [(i, i ^ bits[i % 2]) for i in range(count)])


def combine_kernel(size, listed, parts, radix, *refs):
    ins, outs = refs[:parts], refs[parts:]
    total, more = ins[0][0:size, :], ins[0][size + listed :, :]
    for r in ins[1:]:
        total = total + r[0:size, :]
        more = more + r[size + listed :, :]
    if listed:
        more = jnp.concatenate([r[size : size + listed, :] for r in ins] + [more], 0)
    if radix == 1:
        outs[0][...] = total
        outs[1][...] = more
        return
    cut = size // radix
    for i, out in enumerate(outs):
        out[0:cut, :] = total[i * cut : (i + 1) * cut, :]
        out[cut:, :] = more


def reduce_scatter(keep, send, size, listed):
    steps = rounds()
    summed = keep.shape[0] - size - listed
    pieces = [keep, send]
    for at, (stride, radix) in enumerate(steps):
        ins = [pieces[0]] + [exchange(p, (by * stride[0], by * stride[1])) for by, p in enumerate(pieces) if by]
        after = steps[at + 1][1] if at + 1 < len(steps) else 1
        more = listed * radix + summed
        shapes = [(size // after + more, BLK)] * after if after > 1 else [(size, BLK), (more, BLK)]
        pieces = call(
            functools.partial(combine_kernel, size, listed, len(ins), after),
            [(s, f32) for s in shapes],
            *ins,
        )
        listed, size = listed * radix, size // after
    return pieces


def all_gather(x, beside=()):
    steps = rounds()
    parts = [x]
    for at in range(len(steps) - 1, 0, -1):
        stride, radix = steps[at]
        whole = parts[0] if len(parts) == 1 else jnp.concatenate(parts, 0)
        parts = [whole] + [exchange(whole, (by * stride[0], by * stride[1])) for by in range(1, radix)]
        if at == len(steps) - 1:
            parts, beside = lax.optimization_barrier((parts, beside))
    return parts + [swap(p, 1, 1) for p in parts], beside


def padded(rows):
    unit = 8 * lax.axis_size("group") * lax.axis_size("dp")
    return -(-rows // unit) * unit


def gather_into(pos, parts, out_ref, devices):
    chunk = out_ref.shape[0] // devices
    each = devices // len(parts)
    for i, part in enumerate(parts):
        for j in range(each):
            to = pl.multiple_of(chunk_at(pos, devices, i * each + j, i < len(parts) // 2) * chunk, 8)
            out_ref[pl.ds(to, chunk), :] = part[j * chunk : (j + 1) * chunk, :]


def scatter_from(pos, src_ref, keep_ref, send_ref, devices):
    chunk = src_ref.shape[0] // devices
    half = devices // 2
    for i in range(devices):
        at = pl.multiple_of(chunk_at(pos, devices, i, i < half) * chunk, 8)
        out = keep_ref if i < half else send_ref
        out[(i % half) * chunk : (i % half + 1) * chunk, :] = src_ref[pl.ds(at, chunk), :]


def put_row(out_ref, at, row):
    for i in range(row.shape[1] // BLK):
        out_ref[at + i : at + i + 1, :] = row[:, i * BLK : (i + 1) * BLK]


def put_extra(refs, at, rows):
    count = sum(row.shape[1] // BLK for row in rows)
    for ref in refs:
        end = at
        for row in rows:
            put_row(ref, end, row)
            end += row.shape[1] // BLK
        if count % 8:
            ref[end : at + count + 8 - count % 8, :] = jnp.zeros((8 - count % 8, BLK), f32)


def get_row(ref, at, blocks):
    return jnp.concatenate([ref[at + i : at + i + 1, :] for i in range(blocks)], 1)


def triangle():
    shape = (BLK, BLK)
    rows, cols = lax.broadcasted_iota(jnp.int32, shape, 0), lax.broadcasted_iota(jnp.int32, shape, 1)
    return rows > cols, rows == cols


def lower_products(left, right, out_ref, blocks):
    at, total = starts(blocks)
    n = blocks * BLK
    below, middle = triangle()
    diagonals = []
    for j in range(0, blocks, 2):
        lo = j * BLK
        part = mm(left[:, lo:], right[:, lo : lo + PAIR], TN)
        other = part[BLK:PAIR, BLK:]
        diagonals.append(jnp.sum(jnp.where(middle, other, 0.0), axis=0, keepdims=True))
        out_ref[at[j] : at[j] + BLK, :] = jnp.where(below, part[:BLK, :BLK], jnp.where(middle, part[:BLK, :BLK], other.T))
        out_ref[at[j] + BLK : at[j] + n - lo, :] = part[BLK:, :BLK]
        if lo + PAIR < n:
            out_ref[at[j + 1] : at[j + 1] + n - lo - PAIR, :] = part[PAIR:, BLK:]
    if out_ref.shape[0] > total:
        out_ref[total:, :] = jnp.zeros((out_ref.shape[0] - total, BLK), f32)
    return diagonals


def unpack(pay_ref, at, diagonal):
    below, middle = triangle()
    packed = pay_ref[at : at + BLK, :]
    one = jnp.where(below, packed, 0.0)
    one = jnp.where(middle, packed, one + one.T)
    two = jnp.where(below | middle, 0.0, packed)
    two = jnp.where(middle, diagonal, two + two.T)
    return one, two


def front_kernel(blocks, devices, pos_ref, hid_hbm, w_hbm, emb_hbm, keep_ref, send_ref, hid_ref, pay_ref, w_ref, emb_ref, sems):
    slabs = sems.shape[0] - 2
    deep = w_hbm.shape[0] // slabs
    copies = [pltpu.make_async_copy(hid_hbm, hid_ref, sems.at[slabs])]
    for i in range(slabs):
        rows = pl.ds(i * deep, deep)
        copies.append(pltpu.make_async_copy(w_hbm.at[rows, :], w_ref.at[rows, :], sems.at[i]))
    for copy in copies:
        copy.start()
    copies[0].wait()
    emb = 0.0
    for i in range(slabs):
        copies[1 + i].wait()
        emb = emb + mm(hid_ref[:, i * deep : (i + 1) * deep], w_ref[i * deep : (i + 1) * deep, :], NN)
    emb_ref[...] = emb
    out = pltpu.make_async_copy(emb_ref, emb_hbm, sems.at[slabs + 1])
    out.start()
    total = jnp.sum(emb, axis=0, keepdims=True)
    parts = split3(emb - total / emb.shape[0])
    diagonals = lower_products(left6(parts, 0), right6(parts, 0), pay_ref, blocks)
    scatter_from(pos_ref[0, 0], pay_ref, keep_ref, send_ref, devices)
    put_extra((keep_ref, send_ref), pay_ref.shape[0] // 2, [total] + diagonals)
    out.wait()


def turn_kernel(me_ref, hid_ref, keep_ref, send_ref, turned_ref):
    turned_ref[...] = hid_ref[...].astype(f32).T
    count = lax.axis_size("group") * lax.axis_size("dp")
    own = turned_ref.shape[0] // count
    core = me_ref[0, 0] % 2
    for out, c in ((keep_ref, core), (send_ref, 1 - core)):
        for i in range(count // 2):
            rows = turned_ref[pl.ds(pl.multiple_of((2 * i + c) * own, 8), own), :]
            out[i * own : (i + 1) * own, :] = rows


def order_kernel(orders, me_ref, keep_ref, got_ref, *refs):
    near_refs, far_refs, part_ref = refs[: len(orders)], refs[len(orders) : -1], refs[-1]
    chip, core = me_ref[0, 0] // 2, me_ref[0, 0] % 2
    half = part_ref.shape[0]
    own = half * 2 >> len(orders[0])
    local = keep_ref.shape[1]
    for bits, near_ref, far_ref in zip(orders, near_refs, far_refs):
        for side, out in ((0, part_ref), (1, far_ref)):
            for i in range(half // own):
                far = [bits[0][0] * side] * 2
                for t, bit in enumerate(reversed(bits[1:])):
                    far = [f | b * ((i >> t) & 1) for f, b in zip(far, bit)]
                differ = far[0] // 2 if far[0] == far[1] else jnp.where(core == 0, far[0] // 2, far[1] // 2)
                rows = pl.ds(pl.multiple_of((chip ^ differ) * own, 8), own)
                out[i * own : (i + 1) * own, :local] = keep_ref[rows, :]
                out[i * own : (i + 1) * own, local:] = got_ref[rows, :]
        near_ref[...] = part_ref[...].astype(bf16)


def part_kernel(near_ref, far_ref, *refs):
    rows, (keep_ref, send_ref) = refs[:4], refs[4:]
    left = jnp.concatenate([near_ref[...], far_ref[...].astype(bf16)], 1)
    part = mm(left, jnp.concatenate([r[...].astype(bf16) for r in rows], 0), NN)
    half = keep_ref.shape[0]
    keep_ref[...] = part[:half]
    send_ref[...] = part[half:]


def lane(x, c):
    return jnp.broadcast_to(x[:, c : c + 1], (x.shape[0], BLK))


def sub(x, i):
    return jnp.broadcast_to(x[i : i + 1, :], (8, x.shape[1]))


def eye():
    shape = (BLK, BLK)
    return (lax.broadcasted_iota(jnp.int32, shape, 0) == lax.broadcasted_iota(jnp.int32, shape, 1)).astype(f32)


def inverse_factor(s, out):
    row = lax.broadcasted_iota(jnp.int32, (8, BLK), 0)
    t = eye()
    count = PANEL // 8
    outs = []
    for at in range(0, BLK, PANEL):
        r = [s[8 * q : 8 * q + 8] for q in range(count)]
        v = [t[8 * q : 8 * q + 8] for q in range(count)]
        pivots = [jnp.ones((8, BLK), f32)] * count
        for first in range(0, PANEL, AHEAD):
            last = first + AHEAD
            a = {(l, q): lane(r[q], at + l) for l in range(first, last) for q in range(l // 8, count)}
            for c in range(first, last):
                p, i = c // 8, c % 8
                piv = {l: sub(a[c, l // 8], l % 8) for l in range(c, last)}
                inv = 1.0 / piv[c]
                pivots[p] = jnp.where(row == i, piv[c], pivots[p])
                rs, vs = sub(r[p], i), sub(v[p], i)
                for q in range(p, count):
                    if q == p and i == 7:
                        continue
                    m = a[c, q] * inv
                    if q == p:
                        m = jnp.where(row > i, m, 0.0)
                    for l in range(c + 1, last):
                        if q >= l // 8:
                            a[l, q] = a[l, q] - m * piv[l]
                    r[q] = r[q] - m * rs
                    v[q] = v[q] - m * vs
            yield
        scale = [lax.rsqrt(p) for p in pivots]
        u = jnp.concatenate([x * g for x, g in zip(r, scale)], 0)
        w = jnp.concatenate([x * g for x, g in zip(v, scale)], 0)
        outs.append(w)
        if at + PANEL < BLK:
            us, ws = split3(u), split3(w)
            right = jnp.concatenate([right6(us, 0), right6(ws, 0)], axis=1)
            update = mm(left6(us, 0), right, TN)
            s = s[PANEL:] - update[at + PANEL :, :BLK]
            t = t[PANEL:] - update[at + PANEL :, BLK:]
    out.append(jnp.concatenate(outs, 0))


def inverse_pair(s11, s21, s22, out):
    got = []
    yield from inverse_factor(s11, got)
    l21 = dot6(s21, got[0], NT)
    rest = s22 - dot6(l21, l21, NT)
    yield
    yield from inverse_factor(rest, got)
    x21 = -dot6(got[1], dot6(l21, got[0], NN), NN)
    top = jnp.concatenate([got[0], jnp.zeros((BLK, BLK), f32)], 1)
    out.append(jnp.concatenate([top, jnp.concatenate([x21, got[1]], 1)], 0))


def factor_kernel(blocks, total_rows, devices, parts, *refs):
    pos_ref, sums_ref, emb_ref, partner_ref = refs[:4]
    part_refs = refs[4 : 4 + parts]
    white_refs, x_refs = refs[4 + parts : 6 + parts], refs[6 + parts : 9 + parts]
    a_ref, grad_ref, keep_ref, send_ref, pay_ref, high_ref, mid_ref, low_ref = refs[9 + parts :]
    pos = pos_ref[0, 0]
    gather_into(pos, part_refs, pay_ref, devices)
    n = blocks * BLK
    local = emb_ref.shape[0]
    at, _ = starts(blocks)
    sums = jnp.concatenate([sums_ref[pl.ds(j, devices, blocks), :] for j in range(blocks)], 1)
    mean = jnp.sum(sums, axis=0, keepdims=True) / total_rows
    apart = sums / local - mean
    left, right = left6(split3(apart), 0), right6(split3(apart), 0)
    pairs = blocks // 2
    for p in range(pairs):
        lo, hi = p * PAIR, (p + 1) * PAIR
        between = local * mm(left[:, lo:], right[:, lo:hi], TN)
        begin, after = at[2 * p], at[2 * p + 1]
        d = devices * blocks + p
        one, two = unpack(pay_ref, begin, sums_ref[d : d + 1, :])
        scale = 1.0 / (total_rows - 1)
        a_ref[p, lo : lo + BLK, :BLK] = (one + between[:BLK, :BLK]) * scale
        a_ref[p, lo + BLK : n, :BLK] = (pay_ref[begin + BLK : begin + n - lo, :] + between[BLK:, :BLK]) * scale
        a_ref[p, lo + BLK : hi, BLK:] = (two + between[BLK:PAIR, BLK:]) * scale
        if hi < n:
            a_ref[p, hi:n, BLK:] = (pay_ref[after : after + n - hi, :] + between[PAIR:, BLK:]) * scale
        a_ref[p, n:, :] = emb_ref[:, lo:hi] - mean[:, lo:hi]
    last = pairs * PAIR

    def rows_of(tile):
        return pl.ds(pl.multiple_of(tile * PAIR, PAIR), PAIR) if tile is not None else slice(last, last + local)

    def keep_parts(tile, x):
        for ref, part in zip((high_ref, mid_ref, low_ref), split3(x)):
            ref[rows_of(tile), :] = part

    def parts_at(tile):
        return [ref[rows_of(tile), :] for ref in (high_ref, mid_ref, low_ref)]

    def solve(q, tile, x):
        if tile is None:
            part = mm(left3(split2(a_ref[q, rows_of(tile), :]), 1), right3(x, 1), NT)
        else:
            part = mm(left6(split3(a_ref[q, rows_of(tile), :]), 1), right6(x, 1), NT)
        a_ref[q, rows_of(tile), :] = part
        keep_parts(tile, part)

    def update(j, tile, right, valid, fresh=False):
        if tile is None:
            part = mm(left3(parts_at(tile), 1), right3(parts_at(right), 1), NT)
        else:
            part = mm(left6(parts_at(tile), 1), right6(parts_at(right), 1), NT)
        have = a_ref[j, rows_of(tile), :]
        if fresh:
            have = have * (1.0 - valid)
        a_ref[j, rows_of(tile), :] = have - part * valid

    def chain(p):
        lo = pl.multiple_of(p * PAIR, PAIR)
        top, low = pl.ds(lo, BLK), pl.ds(pl.multiple_of(lo + BLK, BLK), BLK)
        got = []
        return got, inverse_pair(a_ref[p, top, :BLK], a_ref[p, low, :BLK], a_ref[p, low, BLK:], got)

    def settle(p, x):
        a_ref[p, rows_of(p), :] = x.T
        for ref, part in zip(x_refs, split3(x)):
            ref[...] = part
        solve(p, p + 1, [ref[...] for ref in x_refs])
        next_parts = parts_at(p + 1)
        a_ref[p + 1, rows_of(p + 1), :] -= mm(left6(next_parts, 1), right6(next_parts, 1), NT)

    got, steps = chain(0)
    for _ in steps:
        pass
    settle(0, got[0])

    def step(p, _):
        q = p - 1
        x = [ref[...] for ref in x_refs]
        tasks = [lambda: keep_parts(q, a_ref[q, rows_of(q), :])]
        others = [(q + r) % pairs for r in range(2, pairs)]
        tasks += [functools.partial(solve, q, tile, x) for tile in others + [None]]
        for u in range(pairs - 1):
            j = q + 1 + u
            valid = jnp.where(j < pairs, 1.0, 0.0).astype(f32)
            j = j % pairs
            tasks.append(functools.partial(update, j, q, j, valid, True))
            tasks += [functools.partial(update, j, t, j, valid) for t in others[max(u - 1, 0) :] + [None]]
        got, steps = chain(p)
        count = 2 * BLK // AHEAD + 1
        for i, _ in enumerate(steps):
            for _ in range(-(-len(tasks) // max(count - i, 1))):
                tasks.pop(0)()
        for task in tasks:
            task()

        @pl.when(p + 1 < pairs)
        def _():
            settle(p, got[0])

        @pl.when(p + 1 == pairs)
        def _():
            a_ref[p, rows_of(p), :] = got[0].T
            for ref, part in zip(x_refs, split3(got[0])):
                ref[...] = part

        return 0

    lax.fori_loop(1, pairs, step, 0)
    solve(pairs - 1, None, [ref[...] for ref in x_refs])
    white = jnp.concatenate([a_ref[p, n:, :] for p in range(pairs)], 1)
    white_parts = split2(white)
    for ref, part in zip(white_refs, white_parts):
        ref[...] = part
    rows = white.shape[0]
    norm = jnp.sqrt(jnp.sum(white * white, axis=1, keepdims=True) + epsilon)
    unit = white / norm
    hit = (lax.broadcasted_iota(jnp.int32, (rows, rows), 0) == partner_ref[...]).astype(f32)
    both = (hit + hit.T).astype(bf16)
    parts = split3(unit)
    near = mm(jnp.concatenate([both] * 3, 1), jnp.concatenate(parts, 0), NN)
    grad_unit = 2.0 * (2.0 * unit - near)
    inner = jnp.sum(white * grad_unit, axis=1, keepdims=True)
    grad = grad_unit / norm - white * (inner / (norm * norm * norm))
    grad_ref[...] = grad
    diagonals = lower_products(left3(split2(grad), 0), right3(white_parts, 0), pay_ref, blocks)
    scatter_from(pos, pay_ref, keep_ref, send_ref, devices)
    totals = [jnp.sum(rows, axis=0, keepdims=True) for rows in (grad, white)]
    put_extra((keep_ref, send_ref), pay_ref.shape[0] // 2, totals + diagonals)


def inverse_kernel(a_ref, *refs):
    x, outs = [ref[...] for ref in refs[:3]], refs[3:]
    pairs = a_ref.shape[0]
    for p in range(pairs):
        lo, hi = p * PAIR, (p + 1) * PAIR
        for i in range(0, hi, PAIR):
            have = a_ref[p, i : i + PAIR, :]
            if p == pairs - 1 and i < lo:
                have = mm(left6(split3(have), 1), right6(x, 1), NT)
            for out, part in zip(outs, split2(have)):
                out[i : i + PAIR, lo:hi] = part


def moment_product(parts, pay_ref, diagonals, blocks):
    n = blocks * BLK
    at, _ = starts(blocks)
    outs = [0.0] * (blocks // 2)
    for j in range(0, blocks, 2):
        lo, hi = j * BLK, (j + 2) * BLK
        cross = pay_ref[at[j] + BLK : at[j] + PAIR, :]
        one, two = unpack(pay_ref, at[j], diagonals[j // 2])
        column = jnp.concatenate([jnp.concatenate([one, cross], 0), jnp.concatenate([cross.T, two], 0)], 1)
        outs[j // 2] += mm(left3([p[:, lo:hi] for p in parts], 1), right3(split2(column), 0), NN)
        if hi < n:
            rest = [pay_ref[at[j] + PAIR : at[j] + n - lo, :], pay_ref[at[j + 1] : at[j + 1] + n - hi, :]]
            rest = split2(jnp.concatenate(rest, 1))
            outs[j // 2] += mm(left3([p[:, hi:] for p in parts], 1), right3(rest, 0), NN)
            turned = mm(left3([p[:, lo:hi] for p in parts], 1), right3(rest, 1), NT)
            for i in range(hi, n, PAIR):
                outs[i // PAIR] += turned[:, i - hi : i - hi + PAIR]
    return jnp.concatenate(outs, 1)


def back_kernel(blocks, total_rows, devices, parts, shares, *refs):
    pos_ref, sums_ref, grad_ref = refs[:3]
    xt_refs, white_refs = refs[3:5], refs[5:7]
    part_refs = refs[7 : 7 + parts]
    out_ref, wide_refs, pay_ref = refs[7 + parts], refs[8 + parts : -1], refs[-1]
    gather_into(pos_ref[0, 0], part_refs, pay_ref, devices)
    n = blocks * BLK
    sums = split2(jnp.broadcast_to(get_row(sums_ref, blocks, blocks), (16, n)))
    rows = [jnp.concatenate([w[...], s], 0) for w, s in zip(white_refs, sums)]
    firsts = jnp.concatenate([grad_ref[...], jnp.broadcast_to(get_row(sums_ref, 0, blocks), (16, n))], 0)
    diagonals = [sums_ref[2 * blocks + p : 2 * blocks + p + 1, :] for p in range(blocks // 2)]
    left = split2(firsts - moment_product(rows, pay_ref, diagonals, blocks) / (total_rows - 1))
    local = grad_ref.shape[0]
    for lo in range(0, n, PAIR):
        here = slice(lo, lo + PAIR)
        cent = mm(left3([p[:, lo:] for p in left], 1), right3([x[here, lo:] for x in xt_refs], 1), NT)
        grad_z = (cent[:local] - cent[local : local + 1, :] / total_rows).astype(bf16)
        out_ref[:, here] = grad_z
        wide = grad_z.astype(f32)
        at = 0
        for ref, share in zip(wide_refs, shares):
            first, last = max(at, lo), min(at + share, lo + PAIR)
            if first < last:
                ref[:, first - at : last - at] = wide[:, first - lo : last - lo]
            at += share


def call(kernel, outs, *args, scratch=(), limit=24, places=None, flops=10**6):
    return pl.pallas_call(
        kernel,
        out_shape=tuple(jax.ShapeDtypeStruct(s, t) for s, t in outs),
        in_specs=[SMEM if a.dtype == jnp.int32 and a.size == 1 else (VMEM if places is None else HBM) for a in args],
        out_specs=(VMEM,) * len(outs) if places is None else places,
        scratch_shapes=list(scratch),
        compiler_params=pltpu.CompilerParams(vmem_limit_bytes=limit * 2**20),
        cost_estimate=pl.CostEstimate(flops=flops, bytes_accessed=10**6, transcendentals=0),
    )(*args)


def halving(emb):
    per, groups = lax.axis_size("dp"), lax.axis_size("group")
    group = [(per << i,) * 2 for i in range(groups.bit_length() - 1)]
    rest = [2 << i for i in range(per.bit_length() - 2)]
    crossed = list(zip(rest, rest[1::-1] + rest[2:]))
    rest = [(bit, bit) for bit in rest]
    return (group + crossed, group[::-1] + crossed, rest + group), (3 * emb // 8, 3 * emb // 8, emb // 4)


def weight_sums(near, far, wide, mine, weight):
    orders, shares = halving(weight.shape[1])
    there = [exchange(w, order[0]) for w, order in zip(wide, orders)]
    beside = [swap(w, 1, 1) for w in wide]
    product = mm(mine, weight, NT).astype(bf16)
    beside, product = lax.optimization_barrier((beside, product))
    kept, sent, last = [None] * len(orders), [None] * len(orders), product
    for group in ((2,), (0, 1)):
        ins = [there[p] for p in group], [beside[p] for p in group], last
        ins, others, last = lax.optimization_barrier(ins)
        if group == (2,):
            product = last
        across = [swap(t, 1, 1) for t in ins]
        for p, t, o, c in zip(group, ins, others, across):
            shape = ((near[p].shape[0] // 2, shares[p]), f32)
            kept[p], last = call(part_kernel, [shape, shape], near[p], far[p], wide[p], o, t, c)
            sent[p] = exchange(last, orders[p][1])
    orders = list(orders)
    for step in range(2, len(orders[0])):
        for p in reversed(range(len(orders))):
            if p == 1 and len(orders) == 3 and orders[0][step:] == orders[1][step:]:
                both = lax.optimization_barrier((kept[0], sent[0], kept[1], sent[1], last))
                last = both[4]
                kept = [jnp.concatenate([both[0], both[2]], 1), kept[2]]
                sent = [jnp.concatenate([both[1], both[3]], 1), sent[2]]
                orders = orders[1:]
                p = 0
            k, r, last = lax.optimization_barrier((kept[p], sent[p], last))
            size = k.shape[0] // 2
            last = k[size:] + r[size:]
            kept[p] = k[:size] + r[:size]
            sent[p] = exchange(last, orders[p][step])
            if p == 0:
                break
    return jnp.concatenate([k + r for k, r in zip(kept, sent)], 1), product


def body(hidden, weight, partners):
    local, hid = hidden.shape
    emb = weight.shape[1]
    blocks = emb // BLK
    devices = lax.axis_size("group") * lax.axis_size("dp")
    total_rows = local * devices
    _, packed = starts(blocks)
    rows = padded(packed)
    half = rows // 2
    extra = -(-(blocks // 2) // 8) * 8
    pos = place()
    pay_scratch = pltpu.VMEM((rows, BLK), f32)

    slabs = 4
    embedded, keep, send, early = call(
        functools.partial(front_kernel, blocks, devices),
        [((local, emb), f32)] + [((half + blocks + extra, BLK), f32)] * 2 + [((local, hid), bf16)],
        pos,
        *(pltpu.with_memory_space_constraint(a, pltpu.HBM) for a in (hidden, weight)),
        scratch=[
            pay_scratch,
            pltpu.VMEM((hid, emb), bf16),
            pltpu.VMEM((local, emb), f32),
            pltpu.SemaphoreType.DMA((slabs + 2,)),
        ],
        places=(HBM, VMEM, VMEM, VMEM),
    )
    me = (lax.axis_index("group") * lax.axis_size("dp") + lax.axis_index("dp")).astype(jnp.int32).reshape(1, 1)
    turned_keep, turned_send = call(
        turn_kernel,
        [((hid // 2, local), f32)] * 2,
        me,
        early,
        scratch=[pltpu.VMEM((hid, local), f32)],
        flops=10**9,
    )
    orders, shares = halving(emb)
    turned = call(
        functools.partial(order_kernel, orders),
        [((hid // 4, 2 * local), bf16)] * len(orders) + [((hid // 4, 2 * local), f32)] * len(orders),
        me,
        turned_keep,
        swap(turned_send, 1, 1),
        scratch=[pltpu.VMEM((hid // 4, 2 * local), f32)],
        flops=10**9,
    )
    part, sums = reduce_scatter(keep, send, half, blocks)
    parts, turned = all_gather(part, turned)
    near = turned[: len(orders)]
    far = [exchange(t, order[0]) for t, order in zip(turned[len(orders) :], orders)]
    wh, wl, x1, x2, x3, eliminated, grad, keep, send = call(
        functools.partial(factor_kernel, blocks, total_rows, devices, len(parts)),
        [((local, emb), bf16)] * 2
        + [((PAIR, PAIR), bf16)] * 3
        + [((emb // PAIR, emb + local, PAIR), f32), ((local, emb), f32)]
        + [((half + 2 * blocks + extra, BLK), f32)] * 2,
        pos,
        sums,
        embedded,
        partners,
        *parts,
        scratch=[pay_scratch] + [pltpu.VMEM((emb + local, PAIR), bf16)] * 3,
        limit=32,
        flops=3 * 10**10,
    )
    keep, send, far = lax.optimization_barrier((keep, send, far))
    part, sums = reduce_scatter(keep, send, half, 0)
    inverse = call(inverse_kernel, [((emb, emb), bf16)] * 2, eliminated, x1, x2, x3, flops=3 * 10**9)
    parts, (xh, xl) = all_gather(part, inverse)
    grad_z, *wide = call(
        functools.partial(back_kernel, blocks, total_rows, devices, len(parts), shares),
        [((local, emb), bf16)] + [((local, share), f32) for share in shares],
        pos,
        sums,
        grad,
        xh,
        xl,
        wh,
        wl,
        *parts,
        scratch=[pay_scratch],
        limit=32,
    )
    grad_weight, grad_hidden = weight_sums(near, far, wide, grad_z, weight)
    return (wh, grad_weight, grad_hidden)


def solution(mesh):
    return jax.shard_map(
        body,
        mesh=mesh,
        in_specs=(P(AXES, None), P(), P(AXES, None)),
        out_specs=(P(AXES, None), P(AXES, None), P(AXES, None)),
        check_vma=False,
    )
```

```python
import functools

import jax
import jax.numpy as jnp
from jax import lax
from jax.experimental import pallas as pl
from jax.experimental.pallas import tpu as pltpu
from jax.sharding import PartitionSpec as P

AXES = ("group", "dp")
epsilon = 1e-06
f32 = jnp.float32
bf16 = jnp.bfloat16
NN = (((1,), (0,)), ((), ()))
NT = (((1,), (1,)), ((), ()))
TN = (((0,), (0,)), ((), ()))
BLK = 128
PAIR = 256
PANEL = 32
AHEAD = 16
VMEM = pl.BlockSpec(memory_space=pltpu.VMEM)
SMEM = pl.BlockSpec(memory_space=pltpu.SMEM)
HBM = pl.BlockSpec(memory_space=pltpu.HBM)


def split2(x):
    high = x.astype(bf16)
    return high, (x - high.astype(f32)).astype(bf16)


def split3(x):
    high = x.astype(bf16)
    rest = x - high.astype(f32)
    mid = rest.astype(bf16)
    return high, mid, (rest - mid.astype(f32)).astype(bf16)


def left6(parts, axis):
    high, mid, low = parts
    return jnp.concatenate([high, high, mid, high, low, mid], axis=axis)


def right6(parts, axis):
    high, mid, low = parts
    return jnp.concatenate([high, mid, high, low, high, mid], axis=axis)


def left3(parts, axis):
    return jnp.concatenate([parts[0], parts[0], parts[1]], axis=axis)


def right3(parts, axis):
    return jnp.concatenate([parts[0], parts[1], parts[0]], axis=axis)


def mm(a, b, dims):
    return lax.dot_general(a, b, dims, preferred_element_type=f32)


def dot6(a, b, dims):
    (ca,), (cb,) = dims[0]
    return mm(left6(split3(a), ca), right6(split3(b), cb), dims)


def dot3(a, b, dims):
    (ca,), (cb,) = dims[0]
    return mm(left3(split2(a), ca), right3(split2(b), cb), dims)


def starts(blocks):
    out, at = [], 0
    for j in range(blocks):
        out.append(at)
        at += (blocks - j - j % 2) * BLK
    return out, at


def radices(count):
    out = []
    while count > 1:
        out.append(4 if count % 4 == 0 else 2)
        count //= out[-1]
    return out


def rounds():
    groups, per = lax.axis_size("group"), lax.axis_size("dp")
    out, at = [((1, 1), 2)], per
    for radix in radices(groups):
        out.append(((at, at), radix))
        at *= radix
    at = 2
    for radix in radices(per // 2):
        out.append(((at, at), radix))
        at *= radix
    if crossed():
        (one, radix), (two, _) = out[1:3]
        out[1:3] = [((one[0], two[0]), radix), ((two[0], one[0]), radix)]
    return out


def crossed():
    group, rest = radices(lax.axis_size("group")), radices(lax.axis_size("dp") // 2)
    return len(group) == 1 and len(rest) > 0 and group[0] == rest[0]


def place():
    index = lax.axis_index("group") * lax.axis_size("dp") + lax.axis_index("dp")
    out = 0
    for (stride, _), radix in rounds():
        out = out * radix + (index // stride) % radix
    return out.astype(jnp.int32).reshape(1, 1)


def other_order(i):
    if not crossed():
        return i
    radix = lax.axis_size("group")
    low = lax.axis_size("dp") // 2 // radix
    core, first, second = i // (low * radix * radix), i // (low * radix) % radix, i // low % radix
    return ((core * radix + second) * radix + first) * low + i % low


def chunk_at(pos, devices, i, same):
    mine = pos // (devices // 2) == (0 if same else 1)
    far = other_order(i)
    return pos ^ (i if far == i else jnp.where(mine, i, far))


def swap(x, stride, by):
    return exchange(x, (by * stride, by * stride))


def exchange(x, bits):
    count = lax.axis_size("group") * lax.axis_size("dp")
    return lax.ppermute(x, AXES, [(i, i ^ bits[i % 2]) for i in range(count)])


def combine_kernel(size, listed, parts, radix, *refs):
    ins, outs = refs[:parts], refs[parts:]
    total, more = ins[0][0:size, :], ins[0][size + listed :, :]
    for r in ins[1:]:
        total = total + r[0:size, :]
        more = more + r[size + listed :, :]
    if listed:
        more = jnp.concatenate([r[size : size + listed, :] for r in ins] + [more], 0)
    if radix == 1:
        outs[0][...] = total
        outs[1][...] = more
        return
    cut = size // radix
    for i, out in enumerate(outs):
        out[0:cut, :] = total[i * cut : (i + 1) * cut, :]
        out[cut:, :] = more


def reduce_scatter(keep, send, size, listed):
    steps = rounds()
    summed = keep.shape[0] - size - listed
    pieces = [keep, send]
    for at, (stride, radix) in enumerate(steps):
        ins = [exchange(pieces[by], (by * stride[0], by * stride[1])) for by in range(radix - 1, 0, -1)]
        ins = [pieces[0]] + ins
        after = steps[at + 1][1] if at + 1 < len(steps) else 1
        more = listed * radix + summed
        shapes = [(size // after + more, BLK)] * after if after > 1 else [(size, BLK), (more, BLK)]
        pieces = call(
            functools.partial(combine_kernel, size, listed, len(ins), after),
            [(s, f32) for s in shapes],
            *ins,
        )
        listed, size = listed * radix, size // after
    return pieces


def all_gather(x, beside=()):
    steps = rounds()
    parts = [x]
    for at in range(len(steps) - 1, 0, -1):
        stride, radix = steps[at]
        whole = parts[0] if len(parts) == 1 else jnp.concatenate(parts, 0)
        parts = [whole] + [exchange(whole, (by * stride[0], by * stride[1])) for by in range(1, radix)]
        if at == len(steps) - 1:
            parts, beside = lax.optimization_barrier((parts, beside))
    return parts + [swap(p, 1, 1) for p in parts], beside


def padded(rows):
    unit = 8 * lax.axis_size("group") * lax.axis_size("dp")
    return -(-rows // unit) * unit


def gather_into(pos, parts, out_ref, devices):
    chunk = out_ref.shape[0] // devices
    each = devices // len(parts)
    for i, part in enumerate(parts):
        for j in range(each):
            to = pl.multiple_of(chunk_at(pos, devices, i * each + j, i < len(parts) // 2) * chunk, 8)
            out_ref[pl.ds(to, chunk), :] = part[j * chunk : (j + 1) * chunk, :]


def scatter_from(pos, src_ref, keep_ref, send_ref, devices):
    chunk = src_ref.shape[0] // devices
    half = devices // 2
    for i in range(devices):
        at = pl.multiple_of(chunk_at(pos, devices, i, i < half) * chunk, 8)
        out = keep_ref if i < half else send_ref
        out[(i % half) * chunk : (i % half + 1) * chunk, :] = src_ref[pl.ds(at, chunk), :]


def put_row(out_ref, at, row):
    for i in range(row.shape[1] // BLK):
        out_ref[at + i : at + i + 1, :] = row[:, i * BLK : (i + 1) * BLK]


def put_extra(refs, at, rows):
    count = sum(row.shape[1] // BLK for row in rows)
    for ref in refs:
        end = at
        for row in rows:
            put_row(ref, end, row)
            end += row.shape[1] // BLK
        if count % 8:
            ref[end : at + count + 8 - count % 8, :] = jnp.zeros((8 - count % 8, BLK), f32)


def get_row(ref, at, blocks):
    return jnp.concatenate([ref[at + i : at + i + 1, :] for i in range(blocks)], 1)


def triangle():
    shape = (BLK, BLK)
    rows, cols = lax.broadcasted_iota(jnp.int32, shape, 0), lax.broadcasted_iota(jnp.int32, shape, 1)
    return rows > cols, rows == cols


def lower_products(left, right, out_ref, blocks):
    at, total = starts(blocks)
    n = blocks * BLK
    below, middle = triangle()
    diagonals = []
    for j in range(0, blocks, 2):
        lo = j * BLK
        part = mm(left[:, lo:], right[:, lo : lo + PAIR], TN)
        other = part[BLK:PAIR, BLK:]
        diagonals.append(jnp.sum(jnp.where(middle, other, 0.0), axis=0, keepdims=True))
        out_ref[at[j] : at[j] + BLK, :] = jnp.where(below, part[:BLK, :BLK], jnp.where(middle, part[:BLK, :BLK], other.T))
        out_ref[at[j] + BLK : at[j] + n - lo, :] = part[BLK:, :BLK]
        if lo + PAIR < n:
            out_ref[at[j + 1] : at[j + 1] + n - lo - PAIR, :] = part[PAIR:, BLK:]
    if out_ref.shape[0] > total:
        out_ref[total:, :] = jnp.zeros((out_ref.shape[0] - total, BLK), f32)
    return diagonals


def unpack(pay_ref, at, diagonal):
    below, middle = triangle()
    packed = pay_ref[at : at + BLK, :]
    one = jnp.where(below, packed, 0.0)
    one = jnp.where(middle, packed, one + one.T)
    two = jnp.where(below | middle, 0.0, packed)
    two = jnp.where(middle, diagonal, two + two.T)
    return one, two


def front_kernel(blocks, devices, pos_ref, hid_hbm, w_hbm, emb_hbm, keep_ref, send_ref, hid_ref, pay_ref, w_ref, emb_ref, sems):
    slabs = sems.shape[0] - 2
    deep = w_hbm.shape[0] // slabs
    copies = [pltpu.make_async_copy(hid_hbm, hid_ref, sems.at[slabs])]
    for i in range(slabs):
        rows = pl.ds(i * deep, deep)
        copies.append(pltpu.make_async_copy(w_hbm.at[rows, :], w_ref.at[rows, :], sems.at[i]))
    for copy in copies:
        copy.start()
    copies[0].wait()
    emb = 0.0
    for i in range(slabs):
        copies[1 + i].wait()
        emb = emb + mm(hid_ref[:, i * deep : (i + 1) * deep], w_ref[i * deep : (i + 1) * deep, :], NN)
    emb_ref[...] = emb
    out = pltpu.make_async_copy(emb_ref, emb_hbm, sems.at[slabs + 1])
    out.start()
    total = jnp.sum(emb, axis=0, keepdims=True)
    parts = split3(emb - total / emb.shape[0])
    diagonals = lower_products(left6(parts, 0), right6(parts, 0), pay_ref, blocks)
    scatter_from(pos_ref[0, 0], pay_ref, keep_ref, send_ref, devices)
    put_extra((keep_ref, send_ref), pay_ref.shape[0] // 2, [total] + diagonals)
    out.wait()


def turn_kernel(me_ref, hid_ref, keep_ref, send_ref, turned_ref):
    turned_ref[...] = hid_ref[...].astype(f32).T
    count = lax.axis_size("group") * lax.axis_size("dp")
    own = turned_ref.shape[0] // count
    core = me_ref[0, 0] % 2
    for out, c in ((keep_ref, core), (send_ref, 1 - core)):
        for i in range(count // 2):
            rows = turned_ref[pl.ds(pl.multiple_of((2 * i + c) * own, 8), own), :]
            out[i * own : (i + 1) * own, :] = rows


def order_kernel(orders, me_ref, keep_ref, got_ref, *refs):
    near_refs, far_refs, part_ref = refs[: len(orders)], refs[len(orders) : -1], refs[-1]
    chip, core = me_ref[0, 0] // 2, me_ref[0, 0] % 2
    half = part_ref.shape[0]
    own = half * 2 >> len(orders[0])
    local = keep_ref.shape[1]
    for bits, near_ref, far_ref in zip(orders, near_refs, far_refs):
        for side, out in ((0, part_ref), (1, far_ref)):
            for i in range(half // own):
                far = [bits[0][0] * side] * 2
                for t, bit in enumerate(reversed(bits[1:])):
                    far = [f | b * ((i >> t) & 1) for f, b in zip(far, bit)]
                differ = far[0] // 2 if far[0] == far[1] else jnp.where(core == 0, far[0] // 2, far[1] // 2)
                rows = pl.ds(pl.multiple_of((chip ^ differ) * own, 8), own)
                out[i * own : (i + 1) * own, :local] = keep_ref[rows, :]
                out[i * own : (i + 1) * own, local:] = got_ref[rows, :]
        near_ref[...] = part_ref[...].astype(bf16)


def part_kernel(near_ref, far_ref, *refs):
    rows, (keep_ref, send_ref) = refs[:4], refs[4:]
    left = jnp.concatenate([near_ref[...], far_ref[...].astype(bf16)], 1)
    part = mm(left, jnp.concatenate([r[...].astype(bf16) for r in rows], 0), NN)
    half = keep_ref.shape[0]
    keep_ref[...] = part[:half]
    send_ref[...] = part[half:]


def lane(x, c):
    return jnp.broadcast_to(x[:, c : c + 1], (x.shape[0], BLK))


def sub(x, i):
    return jnp.broadcast_to(x[i : i + 1, :], (8, x.shape[1]))


def eye():
    shape = (BLK, BLK)
    return (lax.broadcasted_iota(jnp.int32, shape, 0) == lax.broadcasted_iota(jnp.int32, shape, 1)).astype(f32)


def inverse_factor(s, out):
    row = lax.broadcasted_iota(jnp.int32, (8, BLK), 0)
    t = eye()
    count = PANEL // 8
    outs = []
    for at in range(0, BLK, PANEL):
        r = [s[8 * q : 8 * q + 8] for q in range(count)]
        v = [t[8 * q : 8 * q + 8] for q in range(count)]
        pivots = [jnp.ones((8, BLK), f32)] * count
        for first in range(0, PANEL, AHEAD):
            last = first + AHEAD
            a = {(l, q): lane(r[q], at + l) for l in range(first, last) for q in range(l // 8, count)}
            for c in range(first, last):
                p, i = c // 8, c % 8
                piv = {l: sub(a[c, l // 8], l % 8) for l in range(c, last)}
                inv = 1.0 / piv[c]
                pivots[p] = jnp.where(row == i, piv[c], pivots[p])
                rs, vs = sub(r[p], i), sub(v[p], i)
                for q in range(p, count):
                    if q == p and i == 7:
                        continue
                    m = a[c, q] * inv
                    if q == p:
                        m = jnp.where(row > i, m, 0.0)
                    for l in range(c + 1, last):
                        if q >= l // 8:
                            a[l, q] = a[l, q] - m * piv[l]
                    r[q] = r[q] - m * rs
                    v[q] = v[q] - m * vs
            yield
        scale = [lax.rsqrt(p) for p in pivots]
        u = jnp.concatenate([x * g for x, g in zip(r, scale)], 0)
        w = jnp.concatenate([x * g for x, g in zip(v, scale)], 0)
        outs.append(w)
        if at + PANEL < BLK:
            us, ws = split3(u), split3(w)
            right = jnp.concatenate([right6(us, 0), right6(ws, 0)], axis=1)
            update = mm(left6(us, 0), right, TN)
            s = s[PANEL:] - update[at + PANEL :, :BLK]
            t = t[PANEL:] - update[at + PANEL :, BLK:]
    out.append(jnp.concatenate(outs, 0))


def inverse_pair(s11, s21, s22, out):
    got = []
    yield from inverse_factor(s11, got)
    l21 = dot6(s21, got[0], NT)
    rest = s22 - dot6(l21, l21, NT)
    yield
    yield from inverse_factor(rest, got)
    x21 = -dot6(got[1], dot6(l21, got[0], NN), NN)
    top = jnp.concatenate([got[0], jnp.zeros((BLK, BLK), f32)], 1)
    out.append(jnp.concatenate([top, jnp.concatenate([x21, got[1]], 1)], 0))


def factor_kernel(blocks, total_rows, devices, parts, *refs):
    pos_ref, sums_ref, emb_ref, partner_ref = refs[:4]
    part_refs = refs[4 : 4 + parts]
    white_refs, x_refs = refs[4 + parts : 6 + parts], refs[6 + parts : 9 + parts]
    a_ref, grad_ref, keep_ref, send_ref, pay_ref, high_ref, mid_ref, low_ref = refs[9 + parts :]
    pos = pos_ref[0, 0]
    gather_into(pos, part_refs, pay_ref, devices)
    n = blocks * BLK
    local = emb_ref.shape[0]
    at, _ = starts(blocks)
    sums = jnp.concatenate([sums_ref[pl.ds(j, devices, blocks), :] for j in range(blocks)], 1)
    mean = jnp.sum(sums, axis=0, keepdims=True) / total_rows
    apart = sums / local - mean
    left, right = left6(split3(apart), 0), right6(split3(apart), 0)
    pairs = blocks // 2
    for p in range(pairs):
        lo, hi = p * PAIR, (p + 1) * PAIR
        between = local * mm(left[:, lo:], right[:, lo:hi], TN)
        begin, after = at[2 * p], at[2 * p + 1]
        d = devices * blocks + p
        one, two = unpack(pay_ref, begin, sums_ref[d : d + 1, :])
        scale = 1.0 / (total_rows - 1)
        a_ref[p, lo : lo + BLK, :BLK] = (one + between[:BLK, :BLK]) * scale
        a_ref[p, lo + BLK : n, :BLK] = (pay_ref[begin + BLK : begin + n - lo, :] + between[BLK:, :BLK]) * scale
        a_ref[p, lo + BLK : hi, BLK:] = (two + between[BLK:PAIR, BLK:]) * scale
        if hi < n:
            a_ref[p, hi:n, BLK:] = (pay_ref[after : after + n - hi, :] + between[PAIR:, BLK:]) * scale
        a_ref[p, n:, :] = emb_ref[:, lo:hi] - mean[:, lo:hi]
    last = pairs * PAIR

    def rows_of(tile):
        return pl.ds(pl.multiple_of(tile * PAIR, PAIR), PAIR) if tile is not None else slice(last, last + local)

    def keep_parts(tile, x):
        for ref, part in zip((high_ref, mid_ref, low_ref), split3(x)):
            ref[rows_of(tile), :] = part

    def parts_at(tile):
        return [ref[rows_of(tile), :] for ref in (high_ref, mid_ref, low_ref)]

    def solve(q, tile, x):
        if tile is None:
            part = mm(left3(split2(a_ref[q, rows_of(tile), :]), 1), right3(x, 1), NT)
        else:
            part = mm(left6(split3(a_ref[q, rows_of(tile), :]), 1), right6(x, 1), NT)
        a_ref[q, rows_of(tile), :] = part
        keep_parts(tile, part)

    def update(j, tile, right, valid, fresh=False):
        if tile is None:
            part = mm(left3(parts_at(tile), 1), right3(parts_at(right), 1), NT)
        else:
            part = mm(left6(parts_at(tile), 1), right6(parts_at(right), 1), NT)
        have = a_ref[j, rows_of(tile), :]
        if fresh:
            have = have * (1.0 - valid)
        a_ref[j, rows_of(tile), :] = have - part * valid

    def chain(p):
        lo = pl.multiple_of(p * PAIR, PAIR)
        top, low = pl.ds(lo, BLK), pl.ds(pl.multiple_of(lo + BLK, BLK), BLK)
        got = []
        return got, inverse_pair(a_ref[p, top, :BLK], a_ref[p, low, :BLK], a_ref[p, low, BLK:], got)

    def settle(p, x):
        a_ref[p, rows_of(p), :] = x.T
        for ref, part in zip(x_refs, split3(x)):
            ref[...] = part
        solve(p, p + 1, [ref[...] for ref in x_refs])
        next_parts = parts_at(p + 1)
        a_ref[p + 1, rows_of(p + 1), :] -= mm(left6(next_parts, 1), right6(next_parts, 1), NT)

    got, steps = chain(0)
    for _ in steps:
        pass
    settle(0, got[0])

    def step(p, _):
        q = p - 1
        x = [ref[...] for ref in x_refs]
        tasks = [lambda: keep_parts(q, a_ref[q, rows_of(q), :])]
        others = [(q + r) % pairs for r in range(2, pairs)]
        tasks += [functools.partial(solve, q, tile, x) for tile in others + [None]]
        for u in range(pairs - 1):
            j = q + 1 + u
            valid = jnp.where(j < pairs, 1.0, 0.0).astype(f32)
            j = j % pairs
            tasks.append(functools.partial(update, j, q, j, valid, True))
            tasks += [functools.partial(update, j, t, j, valid) for t in others[max(u - 1, 0) :] + [None]]
        got, steps = chain(p)
        count = 2 * BLK // AHEAD + 1
        for i, _ in enumerate(steps):
            for _ in range(-(-len(tasks) // max(count - i, 1))):
                tasks.pop(0)()
        for task in tasks:
            task()

        @pl.when(p + 1 < pairs)
        def _():
            settle(p, got[0])

        @pl.when(p + 1 == pairs)
        def _():
            a_ref[p, rows_of(p), :] = got[0].T
            for ref, part in zip(x_refs, split3(got[0])):
                ref[...] = part

        return 0

    lax.fori_loop(1, pairs, step, 0)
    solve(pairs - 1, None, [ref[...] for ref in x_refs])
    white = jnp.concatenate([a_ref[p, n:, :] for p in range(pairs)], 1)
    white_parts = split2(white)
    for ref, part in zip(white_refs, white_parts):
        ref[...] = part
    rows = white.shape[0]
    norm = jnp.sqrt(jnp.sum(white * white, axis=1, keepdims=True) + epsilon)
    unit = white / norm
    hit = (lax.broadcasted_iota(jnp.int32, (rows, rows), 0) == partner_ref[...]).astype(f32)
    both = (hit + hit.T).astype(bf16)
    parts = split3(unit)
    near = mm(jnp.concatenate([both] * 3, 1), jnp.concatenate(parts, 0), NN)
    grad_unit = 2.0 * (2.0 * unit - near)
    inner = jnp.sum(white * grad_unit, axis=1, keepdims=True)
    grad = grad_unit / norm - white * (inner / (norm * norm * norm))
    grad_ref[...] = grad
    diagonals = lower_products(left3(split2(grad), 0), right3(white_parts, 0), pay_ref, blocks)
    scatter_from(pos, pay_ref, keep_ref, send_ref, devices)
    totals = [jnp.sum(rows, axis=0, keepdims=True) for rows in (grad, white)]
    put_extra((keep_ref, send_ref), pay_ref.shape[0] // 2, totals + diagonals)


def inverse_kernel(a_ref, *refs):
    x, outs = [ref[...] for ref in refs[:3]], refs[3:]
    pairs = a_ref.shape[0]
    for p in range(pairs):
        lo, hi = p * PAIR, (p + 1) * PAIR
        for i in range(0, hi, PAIR):
            have = a_ref[p, i : i + PAIR, :]
            if p == pairs - 1 and i < lo:
                have = mm(left6(split3(have), 1), right6(x, 1), NT)
            for out, part in zip(outs, split2(have)):
                out[i : i + PAIR, lo:hi] = part


def moment_product(parts, pay_ref, diagonals, blocks):
    n = blocks * BLK
    at, _ = starts(blocks)
    outs = [0.0] * (blocks // 2)
    for j in range(0, blocks, 2):
        lo, hi = j * BLK, (j + 2) * BLK
        cross = pay_ref[at[j] + BLK : at[j] + PAIR, :]
        one, two = unpack(pay_ref, at[j], diagonals[j // 2])
        column = jnp.concatenate([jnp.concatenate([one, cross], 0), jnp.concatenate([cross.T, two], 0)], 1)
        outs[j // 2] += mm(left3([p[:, lo:hi] for p in parts], 1), right3(split2(column), 0), NN)
        if hi < n:
            rest = [pay_ref[at[j] + PAIR : at[j] + n - lo, :], pay_ref[at[j + 1] : at[j + 1] + n - hi, :]]
            rest = split2(jnp.concatenate(rest, 1))
            outs[j // 2] += mm(left3([p[:, hi:] for p in parts], 1), right3(rest, 0), NN)
            turned = mm(left3([p[:, lo:hi] for p in parts], 1), right3(rest, 1), NT)
            for i in range(hi, n, PAIR):
                outs[i // PAIR] += turned[:, i - hi : i - hi + PAIR]
    return jnp.concatenate(outs, 1)


def back_kernel(blocks, total_rows, devices, parts, shares, *refs):
    pos_ref, sums_ref, grad_ref = refs[:3]
    xt_refs, white_refs = refs[3:5], refs[5:7]
    part_refs = refs[7 : 7 + parts]
    out_ref, wide_refs, pay_ref = refs[7 + parts], refs[8 + parts : -1], refs[-1]
    gather_into(pos_ref[0, 0], part_refs, pay_ref, devices)
    n = blocks * BLK
    sums = split2(jnp.broadcast_to(get_row(sums_ref, blocks, blocks), (16, n)))
    rows = [jnp.concatenate([w[...], s], 0) for w, s in zip(white_refs, sums)]
    firsts = jnp.concatenate([grad_ref[...], jnp.broadcast_to(get_row(sums_ref, 0, blocks), (16, n))], 0)
    diagonals = [sums_ref[2 * blocks + p : 2 * blocks + p + 1, :] for p in range(blocks // 2)]
    left = split2(firsts - moment_product(rows, pay_ref, diagonals, blocks) / (total_rows - 1))
    local = grad_ref.shape[0]
    for lo in range(0, n, PAIR):
        here = slice(lo, lo + PAIR)
        cent = mm(left3([p[:, lo:] for p in left], 1), right3([x[here, lo:] for x in xt_refs], 1), NT)
        grad_z = (cent[:local] - cent[local : local + 1, :] / total_rows).astype(bf16)
        out_ref[:, here] = grad_z
        wide = grad_z.astype(f32)
        at = 0
        for ref, share in zip(wide_refs, shares):
            first, last = max(at, lo), min(at + share, lo + PAIR)
            if first < last:
                ref[:, first - at : last - at] = wide[:, first - lo : last - lo]
            at += share


def call(kernel, outs, *args, scratch=(), limit=24, places=None, flops=10**6):
    return pl.pallas_call(
        kernel,
        out_shape=tuple(jax.ShapeDtypeStruct(s, t) for s, t in outs),
        in_specs=[SMEM if a.dtype == jnp.int32 and a.size == 1 else (VMEM if places is None else HBM) for a in args],
        out_specs=(VMEM,) * len(outs) if places is None else places,
        scratch_shapes=list(scratch),
        compiler_params=pltpu.CompilerParams(vmem_limit_bytes=limit * 2**20),
        cost_estimate=pl.CostEstimate(flops=flops, bytes_accessed=10**6, transcendentals=0),
    )(*args)


def halving(emb):
    per, groups = lax.axis_size("dp"), lax.axis_size("group")
    group = [(per << i,) * 2 for i in range(groups.bit_length() - 1)]
    rest = [2 << i for i in range(per.bit_length() - 2)]
    crossed = list(zip(rest, rest[1::-1] + rest[2:]))
    rest = [(bit, bit) for bit in rest]
    return (group + crossed, group[::-1] + crossed, rest + group), (3 * emb // 8, 3 * emb // 8, emb // 4)


def weight_sums(near, far, wide, mine, weight):
    orders, shares = halving(weight.shape[1])
    there = [exchange(w, order[0]) for w, order in zip(wide, orders)]
    beside = [swap(w, 1, 1) for w in wide]
    product = mm(mine, weight, NT).astype(bf16)
    beside, product = lax.optimization_barrier((beside, product))
    kept, sent, last = [None] * len(orders), [None] * len(orders), product
    for group in ((2,), (0, 1)):
        ins = [there[p] for p in group], [beside[p] for p in group], last
        ins, others, last = lax.optimization_barrier(ins)
        if group == (2,):
            product = last
        across = [swap(t, 1, 1) for t in ins]
        for p, t, o, c in zip(group, ins, others, across):
            shape = ((near[p].shape[0] // 2, shares[p]), f32)
            kept[p], last = call(part_kernel, [shape, shape], near[p], far[p], wide[p], o, t, c)
            sent[p] = exchange(last, orders[p][1])
    orders = list(orders)
    for step in range(2, len(orders[0])):
        for p in reversed(range(len(orders))):
            if p == 1 and len(orders) == 3 and orders[0][step:] == orders[1][step:]:
                both = lax.optimization_barrier((kept[0], sent[0], kept[1], sent[1], last))
                last = both[4]
                kept = [jnp.concatenate([both[0], both[2]], 1), kept[2]]
                sent = [jnp.concatenate([both[1], both[3]], 1), sent[2]]
                orders = orders[1:]
                p = 0
            k, r, last = lax.optimization_barrier((kept[p], sent[p], last))
            size = k.shape[0] // 2
            last = k[size:] + r[size:]
            kept[p] = k[:size] + r[:size]
            sent[p] = exchange(last, orders[p][step])
            if p == 0:
                break
    return jnp.concatenate([k + r for k, r in zip(kept, sent)], 1), product


def body(hidden, weight, partners):
    local, hid = hidden.shape
    emb = weight.shape[1]
    blocks = emb // BLK
    devices = lax.axis_size("group") * lax.axis_size("dp")
    total_rows = local * devices
    _, packed = starts(blocks)
    rows = padded(packed)
    half = rows // 2
    extra = -(-(blocks // 2) // 8) * 8
    pos = place()
    pay_scratch = pltpu.VMEM((rows, BLK), f32)

    slabs = 4
    embedded, keep, send, early = call(
        functools.partial(front_kernel, blocks, devices),
        [((local, emb), f32)] + [((half + blocks + extra, BLK), f32)] * 2 + [((local, hid), bf16)],
        pos,
        *(pltpu.with_memory_space_constraint(a, pltpu.HBM) for a in (hidden, weight)),
        scratch=[
            pay_scratch,
            pltpu.VMEM((hid, emb), bf16),
            pltpu.VMEM((local, emb), f32),
            pltpu.SemaphoreType.DMA((slabs + 2,)),
        ],
        places=(HBM, VMEM, VMEM, VMEM),
    )
    me = (lax.axis_index("group") * lax.axis_size("dp") + lax.axis_index("dp")).astype(jnp.int32).reshape(1, 1)
    turned_keep, turned_send = call(
        turn_kernel,
        [((hid // 2, local), f32)] * 2,
        me,
        early,
        scratch=[pltpu.VMEM((hid, local), f32)],
        flops=10**9,
    )
    orders, shares = halving(emb)
    turned = call(
        functools.partial(order_kernel, orders),
        [((hid // 4, 2 * local), bf16)] * len(orders) + [((hid // 4, 2 * local), f32)] * len(orders),
        me,
        turned_keep,
        swap(turned_send, 1, 1),
        scratch=[pltpu.VMEM((hid // 4, 2 * local), f32)],
        flops=10**9,
    )
    part, sums = reduce_scatter(keep, send, half, blocks)
    parts, turned = all_gather(part, turned)
    near = turned[: len(orders)]
    far = [exchange(t, order[0]) for t, order in zip(turned[len(orders) :], orders)]
    wh, wl, x1, x2, x3, eliminated, grad, keep, send = call(
        functools.partial(factor_kernel, blocks, total_rows, devices, len(parts)),
        [((local, emb), bf16)] * 2
        + [((PAIR, PAIR), bf16)] * 3
        + [((emb // PAIR, emb + local, PAIR), f32), ((local, emb), f32)]
        + [((half + 2 * blocks + extra, BLK), f32)] * 2,
        pos,
        sums,
        embedded,
        partners,
        *parts,
        scratch=[pay_scratch] + [pltpu.VMEM((emb + local, PAIR), bf16)] * 3,
        limit=32,
        flops=3 * 10**10,
    )
    keep, send, far = lax.optimization_barrier((keep, send, far))
    part, sums = reduce_scatter(keep, send, half, 0)
    inverse = call(inverse_kernel, [((emb, emb), bf16)] * 2, eliminated, x1, x2, x3, flops=3 * 10**9)
    parts, (xh, xl) = all_gather(part, inverse)
    grad_z, *wide = call(
        functools.partial(back_kernel, blocks, total_rows, devices, len(parts), shares),
        [((local, emb), bf16)] + [((local, share), f32) for share in shares],
        pos,
        sums,
        grad,
        xh,
        xl,
        wh,
        wl,
        *parts,
        scratch=[pay_scratch],
        limit=32,
    )
    grad_weight, grad_hidden = weight_sums(near, far, wide, grad_z, weight)
    return (wh, grad_weight, grad_hidden)


def solution(mesh):
    return jax.shard_map(
        body,
        mesh=mesh,
        in_specs=(P(AXES, None), P(), P(AXES, None)),
        out_specs=(P(AXES, None), P(AXES, None), P(AXES, None)),
        check_vma=False,
    )
```
